32 devices in a mesh: seq: 8 (over z, y), head: 4 (over x, core).
Axes of the slice: x: 2, y: 2, z: 4, core: 2. Of those that a mesh axis runs over, the one named last changes fastest.
Arguments:
- tokens: bfloat16 [8, 4096, 1024], P(None, 'seq'), may hold values from -6 to 6
- doc_ids: int32 [8, 4096], replicated, may hold values from 0 to 8, as said below
- norm_gain: float32 [1024], replicated, may hold values from 0.5 to 1.5
- head_input_weight: bfloat16 [1024, 2, 2048], P(None, None, 'head'), may hold values from -0.1875 to 0.1875
- state_input_weight: bfloat16 [1024, 256], replicated, may hold values from -0.1875 to 0.1875
- timestep_input_weight: bfloat16 [1024, 32], P(None, 'head'), may hold values from -0.1875 to 0.1875
- conv_x: float32 [5, 2048], P(None, 'head'), may hold values from -3 to 3
- conv_state: float32 [5, 256], replicated, may hold values from -3 to 3
- head_params: float32 [3, 32], P(None, 'head'), as said below
- gated_gain: float32 [2048], P('head'), may hold values from 0.5 to 1.5
- output_weight: bfloat16 [2048, 1024], P('head'), may hold values from -0.125 to 0.125
- cotangent: bfloat16 [8, 4096, 1024], P(None, 'seq'), may hold values from -6 to 6
Outputs:
- output: bfloat16 [8, 4096, 1024], P(None, 'seq')
- input_grad: bfloat16 [8, 4096, 1024], P(None, 'seq')
- norm_gain_grad: float32 [1024], replicated
- in_heads_grad: float32 [1024, 2, 2048], P('seq', None, 'head')
- in_state_grad: float32 [1024, 256], P('seq')
- in_dt_grad: float32 [1024, 32], P(None, 'head')
- conv_x_grad: float32 [5, 2048], P(None, 'head')
- conv_state_grad: float32 [5, 256], replicated
- head_params_grad: float32 [3, 32], P(None, 'head')
- gated_gain_grad: float32 [2048], P('head')
- out_proj_grad: float32 [2048, 1024], P('head', 'seq')
The draws below stay inside these ranges and needn't reach their ends.
Inputs may be any that keep to these rules, and one draw needn't show every extreme that they name: `doc_ids`: never falls along a sequence and starts at 0 in every sequence; one sequence, chosen by the draw, is a single document. `head_params`: row 0 is the time-step bias, row 1 the logarithm of the decay rate, row 2 the skip coefficient.
All inputs are finite; a program needn't handle non-finite values.
Results may differ from the reference program's by a relative error of at most 0.012.
The reference program's roundings to bfloat16 on the way count: a program that leaves them out, or rounds other values in their place, can miss the bound.
Values may be sent and summed in bfloat16 or wider, within the bound.
No kernel may reach another device: no remote copies, remote signals or barrier semaphores. Data moves between devices by JAX's collectives and lax.ppermute only.
A program may use at most 640 MiB of HBM per device.

```python
import math
import jax
import jax.numpy as jnp
from jax import lax

D = 1024
HEADS = 32
HEAD_DIM = 64
STATE = 128
K = 4
BLOCK = 256
SEQS = 8
DI = 2048
LEN = 4096
BREAKS = 8


def draw_doc_ids(key, part):
    key = jax.random.fold_in(key, 11)
    first, second, third = jax.random.split(key, 3)
    spots = jax.random.randint(first, (SEQS, BREAKS), 0, LEN)
    skewed = jax.random.randint(second, (SEQS, BREAKS), 0, LEN)
    places = 1 + spots * skewed // LEN
    whole = jax.random.randint(third, (), 0, SEQS)
    positions = jnp.arange(LEN, dtype=jnp.int32)
    marks = jnp.sum((places[:, :, None] <= positions[None, None, :]).astype(jnp.int32), axis=1)
    marks = jnp.where(jnp.arange(SEQS)[:, None] == whole, 0, marks)
    return marks.astype(jnp.int32)


def draw_head_params(key, part):
    key = jax.random.fold_in(key, 23)
    first, second, third = jax.random.split(key, 3)
    bias = jax.random.uniform(first, (HEADS,), jnp.float32, -7.0, -2.5)
    rates = jax.random.uniform(second, (HEADS,), jnp.float32, math.log(0.01), math.log(10.0))
    skip = jax.random.uniform(third, (HEADS,), jnp.float32, 0.5, 1.5)
    return jnp.stack([bias, rates, skip]).astype(jnp.float32)


def block_scale(stream_key, shape, cuts, low, high):
    gain = 1.0
    for dim, blocks in cuts:
        heights = jax.random.uniform(jax.random.fold_in(jax.random.fold_in(stream_key, 6), dim), (blocks,), jnp.float32, low / len(cuts), high / len(cuts))
        gain = gain * jnp.repeat(jnp.exp(heights), shape[dim] // blocks).reshape((-1,) + (1,) * (len(shape) - 1 - dim))
    return gain


def gaussian(key, shape, scale, bound, cuts=(), held_as=jnp.bfloat16):
    entries = scale * jax.random.normal(key, shape, jnp.float32)
    if cuts:
        entries = entries * block_scale(key, shape, cuts, -0.22, 0.18)
    return jnp.clip(entries, -bound, bound).astype(held_as)


def setup_inputs(seed: int = 0) -> dict:
    arg_keys = jax.random.split(jax.random.key(seed), 13)
    tokens = gaussian(arg_keys[0], (SEQS, LEN, D), 1.0, 6.0, ((1, 8),))
    doc_ids = draw_doc_ids(jax.random.fold_in(arg_keys[12], 71), 0)
    norm_gain = jnp.clip(1.0 + 0.1 * jax.random.normal(arg_keys[2], (D,), jnp.float32), 0.5, 1.5)
    head_input_weight = gaussian(arg_keys[3], (D, 2, DI), D ** -0.5, 0.1875, ((2, 4),))
    state_input_weight = gaussian(arg_keys[4], (D, 2 * STATE), D ** -0.5, 0.1875)
    timestep_input_weight = gaussian(arg_keys[5], (D, HEADS), D ** -0.5, 0.1875, ((1, 4),))
    conv_x = gaussian(arg_keys[6], (K + 1, DI), K ** -0.5, 3.0, ((1, 4),), jnp.float32)
    conv_state = gaussian(arg_keys[7], (K + 1, 2 * STATE), K ** -0.5, 3.0, (), jnp.float32)
    head_params = draw_head_params(jax.random.fold_in(arg_keys[12], 71), 0)
    gated_gain = jnp.clip(1.0 + 0.1 * jax.random.normal(arg_keys[9], (DI,), jnp.float32), 0.5, 1.5)
    output_weight = gaussian(arg_keys[10], (DI, D), DI ** -0.5, 0.125, ((0, 4),))
    cotangent = gaussian(arg_keys[11], (SEQS, LEN, D), 1.0, 6.0, ((1, 8),))
    return {"tokens": tokens, "doc_ids": doc_ids, "norm_gain": norm_gain, "head_input_weight": head_input_weight, "state_input_weight": state_input_weight, "timestep_input_weight": timestep_input_weight, "conv_x": conv_x, "conv_state": conv_state, "head_params": head_params, "gated_gain": gated_gain, "output_weight": output_weight, "cotangent": cotangent}


epsilon = 1e-05
highest_precision = lax.Precision.HIGHEST

@jax.custom_vjp
def low(v):
    return lax.optimization_barrier(v.astype(jnp.bfloat16)).astype(jnp.float32)

@jax.custom_vjp
def lower_backward(v):
    return v

def low_keep(v):
    return (low(v), None)

def low_pass(kept, grad):
    return (grad,)

def back_keep(v):
    return (v, None)

def back_low(kept, grad):
    return (low(grad),)
low.defvjp(low_keep, low_pass)
lower_backward.defvjp(back_keep, back_low)

def paired_rounding(value):
    return low(lower_backward(value))

def causal_conv(padded, padded_ids, weights):
    width = weights.shape[0] - 1
    length = padded.shape[1] - width + 1
    current = padded_ids[:, width - 1:]
    total = jnp.zeros((padded.shape[0], length, padded.shape[2]), jnp.float32) + weights[width]
    for offset in range(width):
        same_doc = (padded_ids[:, offset:offset + length] == current).astype(jnp.float32)
        total = total + weights[offset] * padded[:, offset:offset + length] * same_doc[:, :, None]
    return jax.nn.silu(total)

def block_pass(carry, block):
    state, prev_ids = carry
    x_heads, b_proj, c_proj, step_sizes, log_decay, block_ids = block
    length = x_heads.shape[1]
    cumulated = jnp.cumsum(log_decay, axis=1)
    later = lax.broadcasted_iota(jnp.int32, (length, length), 0) >= lax.broadcasted_iota(jnp.int32, (length, length), 1)
    same_doc = (block_ids[:, :, None] == block_ids[:, None, :]) & later[None]
    by_head = jnp.transpose(cumulated, (0, 2, 1))
    spread = jnp.minimum(by_head[:, :, :, None] - by_head[:, :, None, :], 0.0)
    decays = jnp.where(same_doc[:, None], jnp.exp(spread), 0.0)
    scores = jnp.einsum('sin,sjn->sij', c_proj, b_proj, precision=highest_precision)
    mixing = scores[:, None] * decays * jnp.transpose(step_sizes, (0, 2, 1))[:, :, None, :]
    inside = jnp.einsum('shij,sjhp->sihp', mixing, x_heads, precision=highest_precision)
    carried = (block_ids == prev_ids[:, None]).astype(jnp.float32)[:, :, None] * jnp.exp(cumulated)
    outside = jnp.einsum('sin,shnp->sihp', c_proj, state, precision=highest_precision) * carried[..., None]
    last_doc = (block_ids == block_ids[:, -1:]).astype(jnp.float32)
    tail = jnp.exp(cumulated[:, -1:, :] - cumulated) * last_doc[:, :, None]
    survive = jnp.exp(cumulated[:, -1, :]) * (block_ids[:, -1] == prev_ids).astype(jnp.float32)[:, None]
    fresh = jnp.einsum('sjn,sjhp->shnp', b_proj, x_heads * (tail * step_sizes)[..., None], precision=highest_precision)
    new_state = state * survive[:, :, None, None] + fresh
    return ((new_state, block_ids[:, -1]), inside + outside)

def ssd_scan(x_heads, b_proj, c_proj, step_sizes, log_decay, seq_ids, prev_ids, state):
    count, total = seq_ids.shape
    blocks_n = total // BLOCK

    def split(value):
        return jnp.moveaxis(value.reshape((count, blocks_n, BLOCK) + value.shape[2:]), 1, 0)
    pieces = tuple((split(value) for value in (x_heads, b_proj, c_proj, step_sizes, log_decay, seq_ids)))
    (state, prev_ids), outs = lax.scan(jax.checkpoint(block_pass), (state, prev_ids), pieces)
    return (jnp.moveaxis(outs, 0, 1).reshape(x_heads.shape), state)

def forward(tokens, doc_ids, norm_gain, head_input_weight, state_input_weight, timestep_input_weight, conv_x, conv_state, head_params, gated_gain, output_weight):
    count = tokens.shape[0]
    inner = HEADS * HEAD_DIM
    scale = lax.rsqrt(lax.optimization_barrier(jnp.mean(tokens * tokens, axis=-1, keepdims=True)) + epsilon)
    normalized_rows = low(tokens * scale * norm_gain)
    projected_rows = paired_rounding(jnp.einsum('ipr,rzm->ipzm', normalized_rows, head_input_weight, precision=highest_precision))
    incoming_state = paired_rounding(jnp.einsum('tfa,aw->tfw', normalized_rows, state_input_weight, precision=highest_precision))
    unprocessed_steps = lower_backward(jnp.einsum('coz,zx->cox', normalized_rows, timestep_input_weight, precision=highest_precision))
    padded_ids = jnp.concatenate([jnp.full((count, K - 1), -1, jnp.int32), doc_ids.astype(jnp.int32)], axis=1)
    rows = jnp.concatenate([projected_rows[:, :, 1], incoming_state], axis=2)
    padded = jnp.concatenate([jnp.zeros((count, K - 1, rows.shape[2]), jnp.float32), rows], axis=1)
    weights = jnp.concatenate([conv_x, conv_state], axis=1)
    acted = low(causal_conv(padded, padded_ids, weights))
    x_heads = acted[:, :, :inner].reshape(count, LEN, HEADS, HEAD_DIM)
    b_proj = acted[:, :, inner:inner + STATE]
    c_proj = acted[:, :, inner + STATE:]
    step_sizes = jax.nn.softplus(unprocessed_steps + head_params[0])
    log_decay = -step_sizes * jnp.exp(head_params[1])
    start_state = jnp.zeros((count, HEADS, STATE, HEAD_DIM), jnp.float32)
    start_ids = jnp.full((count,), -1, jnp.int32)
    mixed_ssd, final_state = ssd_scan(x_heads, b_proj, c_proj, step_sizes, log_decay, doc_ids.astype(jnp.int32), start_ids, start_state)
    summed = (mixed_ssd + head_params[2][:, None] * x_heads).reshape(count, LEN, inner)
    gated = summed * jax.nn.silu(projected_rows[:, :, 0])
    rescale = lax.rsqrt(lax.optimization_barrier(jnp.mean(gated * gated, axis=-1, keepdims=True)) + epsilon)
    normalized_output = low(gated * rescale * gated_gain)
    branch_path = jnp.einsum('tqe,ez->tqz', normalized_output, output_weight, precision=highest_precision)
    return tokens + branch_path

def reference(tokens, doc_ids, norm_gain, head_input_weight, state_input_weight, timestep_input_weight, conv_x, conv_state, head_params, gated_gain, output_weight, cotangent):
    weights = tuple((value.astype(jnp.float32) for value in (norm_gain, head_input_weight, state_input_weight, timestep_input_weight, conv_x, conv_state, head_params, gated_gain, output_weight)))

    def one_sequence(totals, item):
        seq_tokens, seq_ids, seq_cot = item

        def apply(inputs, *params):
            return forward(inputs[None], seq_ids[None], *params)[0]
        value, pull = jax.vjp(apply, seq_tokens.astype(jnp.float32), *weights)
        grads = pull(seq_cot.astype(jnp.float32))
        totals = tuple((total + grad for total, grad in zip(totals, grads[1:])))
        return (totals, (value.astype(jnp.bfloat16), grads[0].astype(jnp.bfloat16)))
    zeros = tuple((jnp.zeros_like(value) for value in weights))
    totals, (outputs, input_grads) = lax.scan(one_sequence, zeros, (tokens, doc_ids, cotangent))
    return (outputs, input_grads) + totals
```

```python
import functools

import jax
import jax.numpy as jnp
from jax import lax
from jax.experimental import pallas as pl
from jax.experimental.pallas import tpu as pltpu
from jax.sharding import PartitionSpec as P

F32 = jnp.float32
BF16 = jnp.bfloat16
EPS = 1e-5
CHUNK = 128
PAD = 16
LANES = 128
HEAD_DIM = 64
VMEM = 60 * 1024 * 1024


def dot(a, b):
    return lax.dot_general(a, b, (((1,), (0,)), ((), ())), preferred_element_type=F32)


def dot_nt(a, b):
    return lax.dot_general(a, b, (((1,), (1,)), ((), ())), preferred_element_type=F32)


def dot_tn(a, b):
    return lax.dot_general(a, b, (((0,), (0,)), ((), ())), preferred_element_type=F32)


def split(value):
    high = value.astype(BF16)
    return high, (value - high.astype(F32)).astype(BF16)


def head_map(width):
    lane = lax.broadcasted_iota(jnp.int32, (LANES, width), 1)
    row = lax.broadcasted_iota(jnp.int32, (LANES, width), 0)
    return (lax.shift_right_logical(lane, 6) == row).astype(F32).astype(BF16)


def expand(value, heads):
    high, low = split(value)
    return dot(high, heads) + dot(low, heads)


def by_head(value, heads):
    high, low = split(value)
    return dot_nt(high, heads) + dot_nt(low, heads)


def widen(value, width):
    return jnp.concatenate([value] * (width // LANES), axis=1)


def fold8(value):
    return value[0:8] + value[8:16]


def sigmoid(value):
    return 1.0 / (1.0 + jnp.exp(-value))


def triangle(lower):
    row = lax.broadcasted_iota(jnp.int32, (CHUNK, CHUNK), 0)
    column = lax.broadcasted_iota(jnp.int32, (CHUNK, CHUNK), 1)
    return (row >= column if lower else row <= column)


def exact_dot(ones, value):
    return jnp.dot(ones, value, precision=lax.Precision.HIGHEST, preferred_element_type=F32)


def rows_at(start, count):
    return pl.ds(pl.multiple_of(start, 16), count)


def conv_slab(rows, ids, taps, start):
    values = rows(start - PAD, 32).astype(F32)
    marks = ids(start - PAD, 32)
    current = marks[16:32]
    total = taps[4:5]
    entering = []
    for k in range(4):
        moved = values[13 + k : 29 + k]
        if k < 3:
            same = (marks[13 + k : 29 + k] == current).astype(F32)
            moved = moved * widen(same, values.shape[1])
        entering.append(moved)
        total = total + taps[k : k + 1] * moved
    return total, entering


def conv_forward(rows, ids, taps, store, length):
    def step(i, carry):
        total, _ = conv_slab(rows, ids, taps, PAD + i * 16)
        store(i * 16, (total * sigmoid(total)).astype(BF16))
        return carry

    lax.fori_loop(0, length // 16, step, 0)


def conv_backward(rows, ids, taps, d_acted, d_pre, d_rows, length):
    width = d_pre.shape[1]
    zero = jnp.zeros((16, width), F32)
    d_pre[0:16, :] = zero
    d_pre[length + PAD : length + PAD + 16, :] = zero

    def first(i, sums):
        start = PAD + i * 16
        total, entering = conv_slab(rows, ids, taps, start)
        sigma = sigmoid(total)
        grad = d_acted(i * 16) * (sigma * (1.0 + total * (1.0 - sigma)))
        d_pre[rows_at(start, 16), :] = grad
        return tuple(s + fold8(grad * e) for s, e in zip(sums, entering + [1.0]))

    sums = lax.fori_loop(0, length // 16, first, tuple(jnp.zeros((8, width), F32) for _ in range(5)))

    def second(i, carry):
        start = i * 16
        values = d_pre[rows_at(start, 32), :]
        marks = ids(start, 32)
        current = marks[0:16]
        total = taps[3:4] * values[0:16]
        for k in range(3):
            same = (marks[3 - k : 19 - k] == current).astype(F32)
            total = total + taps[k : k + 1] * (values[3 - k : 19 - k] * widen(same, width))
        d_rows(start, total.astype(BF16))
        return carry

    lax.fori_loop(0, (length + PAD) // 16, second, 0)
    return sums


def project_kernel(blocks, normed, state_w, *refs):
    weights, refs = refs[:blocks], refs[blocks:]
    steps, refs = refs[:blocks], refs[blocks:]
    gate, rows, raw, state_rows = refs
    width = gate.shape[3]
    values = normed[0]
    state_rows[0] = dot(values, state_w[...]).astype(BF16)
    for r in range(blocks):
        gate[r, 0] = dot(values[PAD:], weights[r][:, :width]).astype(BF16)
        rows[r, 0] = dot(values, weights[r][:, width:]).astype(BF16)
        raw[r, 0] = dot_nt(values[PAD:], steps[r][...])


def project(normed, state_w, weights, steps):
    n, padded, model = normed.shape
    blocks = len(weights)
    width = weights[0].shape[1] // 2
    length = padded - PAD
    whole = lambda a: pl.BlockSpec(a.shape, lambda s: (0,) * a.ndim)
    return pl.pallas_call(
        functools.partial(project_kernel, blocks),
        grid=(n,),
        in_specs=[pl.BlockSpec((1, padded, model), lambda s: (s, 0, 0)), whole(state_w)]
        + [whole(v) for v in weights]
        + [whole(v) for v in steps],
        out_specs=[
            pl.BlockSpec((blocks, 1, length, width), lambda s: (0, s, 0, 0)),
            pl.BlockSpec((blocks, 1, padded, width), lambda s: (0, s, 0, 0)),
            pl.BlockSpec((blocks, 1, length, LANES), lambda s: (0, s, 0, 0)),
            pl.BlockSpec((1, padded, state_w.shape[1]), lambda s: (s, 0, 0)),
        ],
        out_shape=[
            jax.ShapeDtypeStruct((blocks, n, length, width), BF16),
            jax.ShapeDtypeStruct((blocks, n, padded, width), BF16),
            jax.ShapeDtypeStruct((blocks, n, length, LANES), F32),
            jax.ShapeDtypeStruct((n, padded, state_w.shape[1]), BF16),
        ],
        compiler_params=pltpu.CompilerParams(vmem_limit_bytes=VMEM),
        name="project",
    )(normed, state_w, *weights, *steps)


def conv_state_kernel(rows, ids, taps, acted):
    length = acted.shape[1]

    def store(start, value):
        acted[0, rows_at(start, 16), :] = value

    conv_forward(
        lambda i, c: rows[0, rows_at(i, c), :], lambda i, c: ids[0, rows_at(i, c), :], taps[...], store, length
    )


def conv_state_call(rows, ids, taps):
    n, padded, width = rows.shape
    length = padded - PAD
    return pl.pallas_call(
        conv_state_kernel,
        grid=(n,),
        in_specs=[
            pl.BlockSpec((1, padded, width), lambda s: (s, 0, 0)),
            pl.BlockSpec((1,) + ids.shape[1:], lambda s: (s, 0, 0)),
            pl.BlockSpec(taps.shape, lambda s: (0, 0)),
        ],
        out_specs=pl.BlockSpec((1, length, width), lambda s: (s, 0, 0)),
        out_shape=jax.ShapeDtypeStruct((n, length, width), BF16),
        compiler_params=pltpu.CompilerParams(vmem_limit_bytes=VMEM),
        name="conv_state",
    )(rows, ids, taps)


def state_kernel(rows, bc, ids, steps, log_decay, taps, acted, cum, message):
    length, width = acted.shape[2:]
    heads = head_map(width)

    def store(start, value):
        acted[0, 0, rows_at(start, 16), :] = value

    conv_forward(
        lambda i, c: rows[0, 0, rows_at(i, c), :],
        lambda i, c: ids[0, rows_at(i, c), :],
        taps[0],
        store,
        length,
    )
    ones = triangle(True).astype(F32)
    total = jnp.zeros((1, LANES), F32)
    for c in range(length // CHUNK):
        part = exact_dot(ones, log_decay[0, 0, c * CHUNK : (c + 1) * CHUNK, :]) + total
        cum[0, 0, c * CHUNK : (c + 1) * CHUNK, :] = part
        total = part[CHUNK - 1 : CHUNK]
    last = ids[0, PAD + length - 1 : PAD + length, :]
    before = ids[0, PAD - 1 : PAD, :]
    state = jnp.zeros((LANES, width), F32)
    for c in range(length // CHUNK):
        here = slice(c * CHUNK, (c + 1) * CHUNK)
        same = (ids[0, PAD + c * CHUNK : PAD + (c + 1) * CHUNK, :] == last).astype(F32)
        tail = jnp.exp(total - cum[0, 0, here, :]) * same * steps[0, 0, here, :]
        scaled = (expand(tail, heads) * acted[0, 0, here, :].astype(F32)).astype(BF16)
        state = state + dot_tn(bc[0, here, :LANES], scaled)
    message[0, 0, :LANES, :] = state.astype(BF16)
    survive = jnp.exp(total) * (last == before).astype(F32)
    message[0, 0, LANES:, :] = expand(jnp.broadcast_to(survive, (16, LANES)), heads).astype(BF16)


def state_call(rows, bc, ids, steps, log_decay, taps):
    blocks, n, padded, width = rows.shape
    length = padded - PAD
    four = lambda a, b: pl.BlockSpec((1, 1, a, b), lambda g, s: (g, s, 0, 0))
    return pl.pallas_call(
        state_kernel,
        grid=(blocks, n),
        in_specs=[
            four(padded, width),
            pl.BlockSpec((1,) + bc.shape[1:], lambda g, s: (s, 0, 0)),
            pl.BlockSpec((1,) + ids.shape[1:], lambda g, s: (s, 0, 0)),
            four(length, LANES),
            four(length, LANES),
            pl.BlockSpec((1,) + taps.shape[1:], lambda g, s: (g, 0, 0)),
        ],
        out_specs=[four(length, width), four(length, LANES), four(LANES + 16, width)],
        out_shape=[
            jax.ShapeDtypeStruct((blocks, n, length, width), BF16),
            jax.ShapeDtypeStruct((blocks, n, length, LANES), F32),
            jax.ShapeDtypeStruct((blocks, n, LANES + 16, width), BF16),
        ],
        compiler_params=pltpu.CompilerParams(vmem_limit_bytes=VMEM),
        name="range_state",
    )(rows, bc, ids, steps, log_decay, taps)


def chunk_marks(ids, c):
    first = PAD + c * CHUNK
    return ids[0, first : first + CHUNK, :], ids[0, first + CHUNK - 1 : first + CHUNK, :], ids[0, first - 1 : first, :]


def chunk_decays(ids, cum, c):
    here, last, before = chunk_marks(ids, c)
    value = cum[0, 0, c * CHUNK : (c + 1) * CHUNK, :]
    base = cum[0, 0, c * CHUNK - 1 : c * CHUNK, :] if c else jnp.zeros((1, LANES), F32)
    end = value[CHUNK - 1 : CHUNK]
    entering = jnp.exp(value - base) * (here == before).astype(F32)
    tail = jnp.exp(end - value) * (here == last).astype(F32)
    survive = jnp.exp(end - base) * (last == before).astype(F32)
    return entering, tail, survive


def lane_halves(pair):
    lane = lax.broadcasted_iota(jnp.int32, pair.shape, 1)
    zero = jnp.zeros_like(pair)
    return jnp.concatenate([jnp.where(lane < HEAD_DIM, pair, zero), jnp.where(lane < HEAD_DIM, zero, pair)], axis=0)


def row_of(value, width):
    return jnp.broadcast_to(value, (16, LANES))


def inside_kernel(acted, bc, ids, id_rows, steps, cum, mixed, states, carried):
    length, width = acted.shape[2:]
    heads = head_map(width)
    later = triangle(True)
    for c in range(length // CHUNK):
        here = slice(c * CHUNK, (c + 1) * CHUNK)
        b_part, c_part = bc[0, here, :LANES], bc[0, here, LANES:]
        marks, _, _ = chunk_marks(ids, c)
        same = later & (marks == id_rows[0, 0:1, here])
        scores = jnp.where(same, dot_nt(c_part, b_part), 0.0)
        value = cum[0, 0, here, :]
        value_t = jnp.transpose(value)
        entering, tail, survive = chunk_decays(ids, cum, c)
        scaled = (expand(steps[0, 0, here, :], heads) * acted[0, 0, here, :].astype(F32)).astype(BF16)
        if c:
            held = carried[...]
            held_low = held.astype(BF16)
            states[0, 0, c - 1] = held_low
            outside = dot(c_part, held_low) * expand(entering, heads)
        for pair in range(width // LANES):
            lanes = slice(pair * LANES, (pair + 1) * LANES)
            mixing = []
            for h in (2 * pair, 2 * pair + 1):
                spread = jnp.minimum(value[:, h : h + 1] - value_t[h : h + 1, :], 0.0)
                mixing.append((scores * jnp.exp(spread)).astype(BF16))
            result = dot(jnp.concatenate(mixing, axis=1), lane_halves(scaled[:, lanes]))
            mixed[0, 0, here, lanes] = result + outside[:, lanes] if c else result
        if c + 1 < length // CHUNK:
            fresh = dot_tn(b_part, (expand(tail, heads) * scaled.astype(F32)).astype(BF16))
            if c:
                fresh = fresh + held * expand(jnp.broadcast_to(survive, (16, LANES)), heads)[0:1]
            carried[...] = fresh


def inside_call(acted, bc, ids, id_rows, steps, cum):
    blocks, n, length, width = acted.shape
    chunks = length // CHUNK
    four = lambda a, b: pl.BlockSpec((1, 1, a, b), lambda g, s: (g, s, 0, 0))
    per_seq = lambda a: pl.BlockSpec((1,) + a.shape[1:], lambda g, s: (s, 0, 0))
    return pl.pallas_call(
        inside_kernel,
        grid=(blocks, n),
        in_specs=[four(length, width), per_seq(bc), per_seq(ids), per_seq(id_rows), four(length, LANES), four(length, LANES)],
        out_specs=[
            four(length, width),
            pl.BlockSpec((1, 1, chunks - 1, LANES, width), lambda g, s: (g, s, 0, 0, 0)),
        ],
        out_shape=[
            jax.ShapeDtypeStruct((blocks, n, length, width), F32),
            jax.ShapeDtypeStruct((blocks, n, chunks - 1, LANES, width), BF16),
        ],
        scratch_shapes=[pltpu.VMEM((LANES, width), F32)],
        compiler_params=pltpu.CompilerParams(vmem_limit_bytes=VMEM),
        name="inside",
    )(acted, bc, ids, id_rows, steps, cum)


def relay_kernel(backward, message, carried):
    ranges, rows, width = carried.shape
    state = jnp.zeros((rows, width), F32)
    order = range(ranges - 1, -1, -1) if backward else range(ranges)
    for q in order:
        carried[q] = state.astype(BF16)
        decay = message[q, rows : rows + 1, :].astype(F32)
        state = state * decay + message[q, :rows, :].astype(F32)


def relay(message, backward):
    blocks, n, rows, width = message.shape
    ranges = lax.axis_size("seq")
    cuts = max(1, ranges // (blocks * n))
    own = LANES // cuts
    parts = message.reshape(blocks * n, rows, width)
    if cuts > 1:
        ends = parts[:, LANES:]
        parts = jnp.stack(
            [jnp.concatenate([parts[:, i * own : (i + 1) * own], ends], axis=1) for i in range(cuts)], axis=1
        ).reshape(blocks * n * cuts, own + 16, width)
    arrived = lax.all_to_all(parts, "seq", 0, 0, tiled=True)
    carried = pl.pallas_call(
        functools.partial(relay_kernel, backward),
        out_shape=jax.ShapeDtypeStruct((ranges, own, width), BF16),
        name="relay",
    )(arrived)
    back = lax.all_to_all(carried, "seq", 0, 0, tiled=True)
    return back.reshape(blocks, n, LANES, width)


def middle_kernel(
    blocks, total_width, mixed, gate, acted, cum, entered, bc, ids, ids_before, tokens, cotangent, params, message, *refs
):
    weights, refs = refs[:blocks], refs[blocks:]
    output, normed_out, d_gate, d_summed, pulled, gain_grad, skip_grad = refs[:7]
    summed_s, gated_s, grad_s, first_s, second_s, low_s, row_s, pull_s = refs[7:]
    tile, width = mixed.shape[2:]
    s, t = pl.program_id(0), pl.program_id(1)
    heads = head_map(width)
    before = ids_before[0, PAD - 1 : PAD, :]
    marks = ids[0]
    c_part = bc[0, :, LANES:]
    slabs = tile // 16
    same = (marks == before).astype(F32)
    row_s[...] = jnp.zeros_like(row_s)

    def lanes_sum(value):
        total = value[:, :LANES]
        for i in range(1, width // LANES):
            total = total + value[:, i * LANES : (i + 1) * LANES]
        return total

    @pl.when((s == 0) & (t == 0))
    def _():
        gain_grad[...] = jnp.zeros_like(gain_grad)
        skip_grad[...] = jnp.zeros_like(skip_grad)

    @pl.when(t == 0)
    def _():
        pull_s[...] = jnp.zeros_like(pull_s)

    for r in range(blocks):
        first_s[...] = dot(c_part, entered[r, 0])
        second_s[r] = expand(jnp.exp(cum[r, 0]) * same, heads)
        skip = params[r, 6:7, :]

        def step(i, carry, r=r, skip=skip):
            here = rows_at(i * 16, 16)
            value = mixed[r, 0, here, :] + first_s[here, :] * second_s[r, here, :]
            summed = value + skip * acted[r, 0, here, :].astype(F32)
            g = gate[r, 0, here, :].astype(F32)
            gated = summed * (g * sigmoid(g))
            summed_s[r, here, :] = summed
            gated_s[r, here, :] = gated
            row_s[here, :] = row_s[here, :] + lanes_sum(gated * gated)
            return carry

        lax.fori_loop(0, slabs, step, 0)
    squares = jnp.sum(row_s[...], axis=1, keepdims=True)
    rescale = jnp.broadcast_to(lax.rsqrt(squares / total_width + EPS), (tile, LANES))
    row_s[...] = rescale
    for r in range(blocks):
        gain = params[r, 5:6, :]

        def step(i, carry, r=r, gain=gain):
            here = rows_at(i * 16, 16)
            normed_out[r, 0, here, :] = (gated_s[r, here, :] * widen(row_s[here, :], width) * gain).astype(BF16)
            return carry

        lax.fori_loop(0, slabs, step, 0)
    branch = tokens[0].astype(F32)
    for r in range(blocks):
        branch = branch + dot(normed_out[r, 0], weights[r][...])
    output[0] = branch.astype(BF16)
    first_s[:, :LANES] = jnp.zeros((tile, LANES), F32)
    for r in range(blocks):
        grad_s[r] = dot_nt(cotangent[0], weights[r][...])
        gain = params[r, 5:6, :]

        def step(i, total, r=r, gain=gain):
            here = rows_at(i * 16, 16)
            both = grad_s[r, here, :] * gated_s[r, here, :]
            first_s[here, :LANES] = first_s[here, :LANES] + lanes_sum(both * gain)
            return total + fold8(both * widen(row_s[here, :], width))

        gain_grad[r] = gain_grad[r] + lax.fori_loop(0, slabs, step, jnp.zeros((8, width), F32))
    cross = jnp.sum(first_s[:, :LANES], axis=1, keepdims=True) / total_width
    first_s[:, :LANES] = rescale * rescale * rescale * cross
    for r in range(blocks):
        gain = params[r, 5:6, :]

        def step(i, total, r=r, gain=gain):
            here = rows_at(i * 16, 16)
            g = gate[r, 0, here, :].astype(F32)
            sigma = sigmoid(g)
            d_gated = widen(row_s[here, :], width) * (grad_s[r, here, :] * gain) - gated_s[r, here, :] * widen(
                first_s[here, :LANES], width
            )
            d_sum = d_gated * (g * sigma)
            d_gate[r, 0, here, :] = (d_gated * summed_s[r, here, :] * (sigma * (1.0 + g * (1.0 - sigma)))).astype(BF16)
            low = d_sum.astype(BF16)
            d_summed[r, 0, here, :] = low
            low_s[here, :] = (d_sum * second_s[r, here, :]).astype(BF16)
            return total + fold8(d_sum * acted[r, 0, here, :].astype(F32))

        skip_grad[r] = skip_grad[r] + lax.fori_loop(0, slabs, step, jnp.zeros((8, width), F32))
        pull_s[r] = pull_s[r] + dot_tn(c_part, low_s[...])

    @pl.when(t == pl.num_programs(1) - 1)
    def _():
        for r in range(blocks):
            pulled[r, 0, :LANES, :] = pull_s[r].astype(BF16)
            pulled[r, 0, LANES:, :] = message[r, 0, LANES:, :]


def middle_call(mixed, gate, acted, cum, entered, bc, ids, tokens, cotangent, params, message, weights, total_width):
    blocks, n, length, width = mixed.shape
    model = tokens.shape[2]
    tile = min(256, length)
    wide = lambda w: pl.BlockSpec((blocks, 1, tile, w), lambda s, t: (0, s, t, 0))
    rows = lambda w: pl.BlockSpec((1, tile, w), lambda s, t: (s, t, 0))
    per_seq = lambda a: pl.BlockSpec((a.shape[0], 1) + a.shape[2:], lambda s, t: (0, s, 0, 0))
    whole = lambda a: pl.BlockSpec(a.shape, lambda s, t: (0,) * a.ndim, pipeline_mode=pl.Buffered(1))
    kept = lambda *shape: pl.BlockSpec(shape, lambda s, t: (0,) * len(shape))
    ids_here = ids[:, PAD : PAD + length]
    return pl.pallas_call(
        functools.partial(middle_kernel, blocks, total_width),
        grid=(n, length // tile),
        in_specs=[
            wide(width), wide(width), wide(width), wide(LANES), per_seq(entered), rows(2 * LANES), rows(LANES),
            pl.BlockSpec((1, PAD, LANES), lambda s, t: (s, 0, 0)), rows(model), rows(model), whole(params), per_seq(message),
        ] + [whole(v) for v in weights],
        out_specs=[
            rows(model), wide(width), wide(width), wide(width), per_seq(message),
            kept(blocks, 8, width), kept(blocks, 8, width),
        ],
        out_shape=[
            jax.ShapeDtypeStruct((n, length, model), BF16),
            jax.ShapeDtypeStruct((blocks, n, length, width), BF16),
            jax.ShapeDtypeStruct((blocks, n, length, width), BF16),
            jax.ShapeDtypeStruct((blocks, n, length, width), BF16),
            jax.ShapeDtypeStruct(message.shape, BF16),
            jax.ShapeDtypeStruct((blocks, 8, width), F32),
            jax.ShapeDtypeStruct((blocks, 8, width), F32),
        ],
        scratch_shapes=[
            pltpu.VMEM((blocks, tile, width), F32),
            pltpu.VMEM((blocks, tile, width), F32),
            pltpu.VMEM((blocks, tile, width), F32),
            pltpu.VMEM((tile, width), F32),
            pltpu.VMEM((blocks, tile, width), F32),
            pltpu.VMEM((tile, width), BF16),
            pltpu.VMEM((tile, LANES), F32),
            pltpu.VMEM((blocks, LANES, width), F32),
        ],
        compiler_params=pltpu.CompilerParams(vmem_limit_bytes=VMEM),
        name="middle",
    )(mixed, gate, acted, cum, entered, bc, ids_here, ids[:, :PAD], tokens, cotangent, params, message, *weights)


def inside_back_kernel(
    acted, d_summed, mixed, bc, ids, id_rows, steps, cum, states, entered, d_scaled, d_b, d_c, d_cum, carried
):
    length, width = acted.shape[2:]
    chunks = length // CHUNK
    heads = head_map(width)
    g = pl.program_id(1)
    sooner = triangle(False)
    first_before = ids[0, PAD - 1 : PAD, :]

    @pl.when(g == 0)
    def _():
        d_b[...] = jnp.zeros_like(d_b)
        d_c[...] = jnp.zeros_like(d_c)

    for c in range(chunks - 1, -1, -1):
        here = slice(c * CHUNK, (c + 1) * CHUNK)
        b_part, c_part = bc[0, here, :LANES], bc[0, here, LANES:]
        marks, _, _ = chunk_marks(ids, c)
        same = sooner & (marks == id_rows[0, 0:1, here])
        scores_t = jnp.where(same, dot_nt(b_part, c_part), 0.0)
        value = cum[0, 0, here, :]
        value_t = jnp.transpose(value)
        entering, tail, survive = chunk_decays(ids, cum, c)
        scaled = (expand(steps[0, 0, here, :], heads) * acted[0, 0, here, :].astype(F32)).astype(BF16)
        grad = d_summed[0, 0, here, :]
        grad_wide = grad.astype(F32)
        from_start = jnp.exp(value) * (marks == first_before).astype(F32)
        start_wide = expand(from_start, heads)
        d_c_part = dot_nt((grad_wide * start_wide).astype(BF16), entered[0, 0])
        dots = grad_wide * (mixed[0, 0, here, :] + start_wide * dot(c_part, entered[0, 0]))
        if c < chunks - 1:
            held = carried[...]
            held_low = held.astype(BF16)
            tail_wide = expand(tail, heads)
            later = dot(b_part, held_low) * tail_wide
            d_b_part = dot_nt((tail_wide * scaled.astype(F32)).astype(BF16), held_low)
        if c:
            entering_grad = (expand(entering, heads) * grad_wide).astype(BF16)
            d_c_part = d_c_part + dot_nt(entering_grad, states[0, 0, c - 1])
        d_scores_t = jnp.zeros((CHUNK, CHUNK), F32)
        results = []
        for pair in range(width // LANES):
            lanes = slice(pair * LANES, (pair + 1) * LANES)
            products = dot_nt(lane_halves(scaled[:, lanes]), grad[:, lanes])
            mixing = []
            for half, h in enumerate((2 * pair, 2 * pair + 1)):
                spread = jnp.minimum(value_t[h : h + 1, :] - value[:, h : h + 1], 0.0)
                decay = jnp.exp(spread)
                mixing.append((scores_t * decay).astype(BF16))
                d_scores_t = d_scores_t + products[half * CHUNK : (half + 1) * CHUNK] * decay
            results.append(dot(jnp.concatenate(mixing, axis=1), lane_halves(grad[:, lanes])))
        result = jnp.concatenate(results, axis=1)
        if c < chunks - 1:
            result = result + later
        d_scaled[0, 0, here, :] = result.astype(BF16)
        d_cum[0, 0, here, :] = by_head(dots - scaled.astype(F32) * result, heads)
        d_scores_t = jnp.where(same, d_scores_t, 0.0).astype(BF16)
        d_b_here = dot(d_scores_t, c_part)
        if c < chunks - 1:
            d_b_here = d_b_here + d_b_part
        d_b[0, here, :] = d_b[0, here, :] + d_b_here
        d_c[0, here, :] = d_c[0, here, :] + d_c_part + dot_tn(d_scores_t, b_part)
        if c:
            pulled = dot_tn(c_part, entering_grad)
            if c < chunks - 1:
                pulled = pulled + held * expand(jnp.broadcast_to(survive, (16, LANES)), heads)[0:1]
            carried[...] = pulled


def inside_back_call(acted, d_summed, mixed, bc, ids, id_rows, steps, cum, states, entered):
    blocks, n, length, width = acted.shape
    four = lambda a, b: pl.BlockSpec((1, 1, a, b), lambda s, g: (g, s, 0, 0))
    per_seq = lambda a: pl.BlockSpec((1,) + a.shape[1:], lambda s, g: (s, 0, 0))
    summed = pl.BlockSpec((1, length, LANES), lambda s, g: (s, 0, 0))
    return pl.pallas_call(
        inside_back_kernel,
        grid=(n, blocks),
        in_specs=[
            four(length, width), four(length, width), four(length, width), per_seq(bc), per_seq(ids), per_seq(id_rows),
            four(length, LANES), four(length, LANES),
            pl.BlockSpec((1, 1) + states.shape[2:], lambda s, g: (g, s, 0, 0, 0)), four(LANES, width),
        ],
        out_specs=[four(length, width), summed, summed, four(length, LANES)],
        out_shape=[
            jax.ShapeDtypeStruct((blocks, n, length, width), BF16),
            jax.ShapeDtypeStruct((n, length, LANES), F32),
            jax.ShapeDtypeStruct((n, length, LANES), F32),
            jax.ShapeDtypeStruct((blocks, n, length, LANES), F32),
        ],
        scratch_shapes=[pltpu.VMEM((LANES, width), F32)],
        compiler_params=pltpu.CompilerParams(vmem_limit_bytes=VMEM),
        name="inside_back",
    )(acted, d_summed, mixed, bc, ids, id_rows, steps, cum, states, entered)


def close_kernel(
    rows, acted, d_summed, d_scaled, bc, ids, steps, raw, log_decay, cum, d_cum, leaving, entered, params, small,
    d_rows, d_raw, d_b, taps_grad, small_grad, d_pre, d_acted, d_log,
):
    length, width = acted.shape[2:]
    chunks = length // CHUNK
    heads = head_map(width)
    s, g = pl.program_id(0), pl.program_id(1)
    last = ids[0, PAD + length - 1 : PAD + length, :]
    before = ids[0, PAD - 1 : PAD, :]
    end = cum[0, 0, length - 1 : length, :]
    skip = params[0, 6:7, :]
    held = leaving[0, 0]

    @pl.when(g == 0)
    def _():
        d_b[...] = jnp.zeros_like(d_b)

    boundary = jnp.zeros((1, LANES), F32)
    for c in range(chunks):
        here = slice(c * CHUNK, (c + 1) * CHUNK)
        marks, _, _ = chunk_marks(ids, c)
        tail = jnp.exp(end - cum[0, 0, here, :]) * (marks == last).astype(F32)
        tail_wide = expand(tail, heads)
        steps_wide = expand(steps[0, 0, here, :], heads)
        x = acted[0, 0, here, :].astype(F32)
        scaled = (steps_wide * x).astype(BF16).astype(F32)
        later = dot(bc[0, here, :LANES], held) * tail_wide
        total = d_scaled[0, 0, here, :].astype(F32) + later
        d_acted[here, :] = steps_wide * total + skip * d_summed[0, 0, here, :].astype(F32)
        d_b[0, here, :] = d_b[0, here, :] + dot_nt((tail_wide * scaled).astype(BF16), held)
        from_later = by_head(scaled * later, heads)
        boundary = boundary + jnp.sum(from_later, axis=0, keepdims=True)
        d_log[here, :] = d_cum[0, 0, here, :] - from_later
        d_raw[0, 0, here, :] = by_head(x * total, heads)
    product = held.astype(F32) * entered[0, 0].astype(F32)
    product = jnp.sum(product, axis=0, keepdims=True)
    survive = jnp.exp(end) * (last == before).astype(F32)
    boundary = boundary + survive * by_head(jnp.broadcast_to(product, (16, width)), heads)[0:1]
    rate = jnp.exp(small[0, 1:2, :])
    ones = triangle(False).astype(F32)
    carry = boundary
    decay_sum = jnp.zeros((1, LANES), F32)
    bias_sum = jnp.zeros((1, LANES), F32)
    for c in range(chunks - 1, -1, -1):
        here = slice(c * CHUNK, (c + 1) * CHUNK)
        grads = exact_dot(ones, d_log[here, :]) + carry
        carry = grads[0:1]
        decay_sum = decay_sum + jnp.sum(grads * log_decay[0, 0, here, :], axis=0, keepdims=True)
        value = (d_raw[0, 0, here, :] - grads * rate) * sigmoid(raw[0, 0, here, :] + small[0, 0:1, :])
        bias_sum = bias_sum + jnp.sum(value, axis=0, keepdims=True)
        d_raw[0, 0, here, :] = value
    small_grad[0, 0] = jnp.concatenate([bias_sum, decay_sum, jnp.zeros((6, LANES), F32)], axis=0)

    def store(start, value):
        d_rows[0, 0, rows_at(start, 16), :] = value

    sums = conv_backward(
        lambda i, n: rows[0, 0, rows_at(i, n), :],
        lambda i, n: ids[0, rows_at(i, n), :],
        params[0],
        lambda i: d_acted[rows_at(i, 16), :],
        d_pre,
        store,
        length,
    )
    taps_grad[0, 0] = jnp.concatenate(
        [jnp.sum(v, axis=0, keepdims=True) for v in sums] + [jnp.zeros((3, width), F32)], axis=0
    )


def close_call(
    rows, acted, d_summed, d_scaled, bc, ids, steps, raw, log_decay, cum, d_cum, leaving, entered, params, small
):
    blocks, n, length, width = acted.shape
    four = lambda a, b: pl.BlockSpec((1, 1, a, b), lambda s, g: (g, s, 0, 0))
    per_seq = lambda a: pl.BlockSpec((1,) + a.shape[1:], lambda s, g: (s, 0, 0))
    per_block = lambda a: pl.BlockSpec((1,) + a.shape[1:], lambda s, g: (g, 0, 0))
    lanes = four(length, LANES)
    wide = four(length, width)
    return pl.pallas_call(
        close_kernel,
        grid=(n, blocks),
        in_specs=[
            four(length + PAD, width), wide, wide, wide, per_seq(bc), per_seq(ids), lanes, lanes, lanes, lanes, lanes,
            four(LANES, width), four(LANES, width), per_block(params), per_block(small),
        ],
        out_specs=[
            four(length + PAD, width), lanes, pl.BlockSpec((1, length, LANES), lambda s, g: (s, 0, 0)),
            four(8, width), four(8, LANES),
        ],
        out_shape=[
            jax.ShapeDtypeStruct((blocks, n, length + PAD, width), BF16),
            jax.ShapeDtypeStruct((blocks, n, length, LANES), F32),
            jax.ShapeDtypeStruct((n, length, LANES), F32),
            jax.ShapeDtypeStruct((blocks, n, 8, width), F32),
            jax.ShapeDtypeStruct((blocks, n, 8, LANES), F32),
        ],
        scratch_shapes=[
            pltpu.VMEM((length + 2 * PAD, width), F32),
            pltpu.VMEM((length, width), F32),
            pltpu.VMEM((length, LANES), F32),
        ],
        compiler_params=pltpu.CompilerParams(vmem_limit_bytes=VMEM),
        name="close",
    )(rows, acted, d_summed, d_scaled, bc, ids, steps, raw, log_decay, cum, d_cum, leaving, entered, params, small)


def conv_state_back_kernel(rows, ids, taps, d_b, d_b_more, d_c, d_rows, taps_grad, d_pre, d_acted):
    length = d_b.shape[1]
    d_acted[:, :LANES] = d_b[0] + d_b_more[0]
    d_acted[:, LANES:] = d_c[0]

    def store(start, value):
        d_rows[0, rows_at(start, 16), :] = value

    sums = conv_backward(
        lambda i, n: rows[0, rows_at(i, n), :],
        lambda i, n: ids[0, rows_at(i, n), :],
        taps[...],
        lambda i: d_acted[rows_at(i, 16), :],
        d_pre,
        store,
        length,
    )
    taps_grad[0] = jnp.concatenate(
        [jnp.sum(v, axis=0, keepdims=True) for v in sums] + [jnp.zeros((3, 2 * LANES), F32)], axis=0
    )


def conv_state_back_call(rows, ids, taps, d_b, d_b_more, d_c):
    n, padded, width = rows.shape
    length = padded - PAD
    per_seq = lambda a, b: pl.BlockSpec((1, a, b), lambda s: (s, 0, 0))
    return pl.pallas_call(
        conv_state_back_kernel,
        grid=(n,),
        in_specs=[
            per_seq(padded, width), per_seq(*ids.shape[1:]), pl.BlockSpec(taps.shape, lambda s: (0, 0)),
            per_seq(length, LANES), per_seq(length, LANES), per_seq(length, LANES),
        ],
        out_specs=[per_seq(padded, width), per_seq(8, width)],
        out_shape=[
            jax.ShapeDtypeStruct((n, padded, width), BF16),
            jax.ShapeDtypeStruct((n, 8, width), F32),
        ],
        scratch_shapes=[pltpu.VMEM((length + 2 * PAD, width), F32), pltpu.VMEM((length, width), F32)],
        compiler_params=pltpu.CompilerParams(vmem_limit_bytes=VMEM),
        name="conv_state_back",
    )(rows, ids, taps, d_b, d_b_more, d_c)


def input_kernel(blocks, d_gate, d_rows, d_raw, d_state, tokens, cotangent, gain, state_w, *refs):
    weights, refs = refs[:blocks], refs[blocks:]
    steps, refs = refs[:blocks], refs[blocks:]
    input_grad, edge, halo, gain_grad, main_s, halo_s = refs
    length, width = d_gate.shape[2:]
    model = tokens.shape[2]
    total = dot_nt(d_state[0], state_w[...])
    main_s[...] = total[PAD:]
    halo_s[...] = total[:PAD]
    for r in range(blocks):
        part = dot_nt(d_rows[r, 0], weights[r][:, width:])
        halo_s[...] = halo_s[...] + part[:PAD]
        main_s[...] = main_s[...] + (
            part[PAD:] + dot_nt(d_gate[r, 0], weights[r][:, :width]) + dot(d_raw[r, 0].astype(BF16), steps[r][...])
        )

    def norm_back(value, token):
        scale = lax.rsqrt(jnp.mean(token * token, axis=1, keepdims=True) + EPS)
        unit = value * gain[...]
        inner = jnp.mean(unit * token, axis=1, keepdims=True)
        return scale * unit - token * (scale * scale * scale * inner), fold8(value * token * scale)

    grad, sums = norm_back(halo_s[...], tokens[0, :PAD, :].astype(F32))
    halo[0] = grad.astype(BF16)

    def step(i, carry):
        here = rows_at(i * 16, 16)
        grad, more = norm_back(main_s[here, :], tokens[0, rows_at(PAD + i * 16, 16), :].astype(F32))
        value = grad + cotangent[0, here, :].astype(F32)
        edge[0] = value
        input_grad[0, here, :] = value.astype(BF16)
        return carry + more

    gain_grad[0] = lax.fori_loop(0, length // 16, step, sums)


def input_call(d_gate, d_rows, d_raw, d_state, tokens, cotangent, gain, state_w, weights, steps):
    blocks, n, length, width = d_gate.shape
    padded, model = tokens.shape[1:]
    wide = lambda a, b: pl.BlockSpec((blocks, 1, a, b), lambda s: (0, s, 0, 0))
    per_seq = lambda a, b: pl.BlockSpec((1, a, b), lambda s: (s, 0, 0))
    whole = lambda a: pl.BlockSpec(a.shape, lambda s: (0,) * a.ndim, pipeline_mode=pl.Buffered(1))
    return pl.pallas_call(
        functools.partial(input_kernel, blocks),
        grid=(n,),
        in_specs=[
            wide(length, width), wide(padded, width), wide(length, LANES), per_seq(padded, state_w.shape[1]),
            per_seq(padded, model), per_seq(length, model), whole(gain), whole(state_w),
        ] + [whole(v) for v in weights] + [whole(v) for v in steps],
        out_specs=[per_seq(length, model), per_seq(PAD, model), per_seq(PAD, model), per_seq(8, model)],
        out_shape=[
            jax.ShapeDtypeStruct((n, length, model), BF16),
            jax.ShapeDtypeStruct((n, PAD, model), F32),
            jax.ShapeDtypeStruct((n, PAD, model), BF16),
            jax.ShapeDtypeStruct((n, 8, model), F32),
        ],
        scratch_shapes=[pltpu.VMEM((length, model), F32), pltpu.VMEM((PAD, model), F32)],
        compiler_params=pltpu.CompilerParams(vmem_limit_bytes=VMEM),
        name="input_gradient",
    )(d_gate, d_rows, d_raw, d_state, tokens, cotangent, gain, state_w, *weights, *steps)


def swapped(value, axis, step):
    return lax.ppermute(value, axis, [(i, i ^ step) for i in range(lax.axis_size(axis))])


def gathered(value):
    parts = [value]
    for r in range(1, lax.axis_size("head")):
        parts.append(swapped(parts[r - 1], "head", 1) if r % 2 else swapped(value, "head", r))
    return parts


def scattered(parts):
    parts = list(parts)
    bit = 1
    while bit < lax.axis_size("head"):
        for r in range(0, lax.axis_size("head"), 2 * bit):
            arrived = swapped(parts[r + bit], "head", bit)
            parts[r] = (parts[r].astype(F32) + arrived.astype(F32)).astype(parts[r].dtype)
        bit *= 2
    return parts[0]


def summed_over(value, axis):
    bit = 1
    while bit < lax.axis_size(axis):
        value = value + swapped(value, axis, bit)
        bit *= 2
    return value


def ranges_sum(value):
    ranges = lax.axis_size("seq")
    arrived = lax.all_to_all(value, "seq", 0, 0, tiled=True)
    return jnp.sum(arrived.reshape((ranges, value.shape[0] // ranges) + value.shape[1:]).astype(F32), axis=0)


def assembled(value):
    n = value.shape[0]
    me = lax.axis_index("head")
    whole = jnp.zeros((n * lax.axis_size("head"),) + value.shape[1:], value.dtype)
    for r, part in enumerate(gathered(value)):
        whole = lax.dynamic_update_slice(whole, part, ((me ^ r) * n, 0, 0))
    return whole


def padded_lanes(value, size):
    return jnp.pad(value, ((0, 0), (0, size - value.shape[1])))


def shards(
    tokens,
    doc_ids,
    norm_gain,
    head_input_weight,
    state_input_weight,
    timestep_input_weight,
    conv_x,
    conv_state,
    head_params,
    gated_gain,
    output_weight,
    cotangent,
):
    seqs, length, model = tokens.shape
    blocks = lax.axis_size("head")
    ranges = lax.axis_size("seq")
    n = seqs // blocks
    width = gated_gain.shape[0]
    heads = head_params.shape[1]
    me = lax.axis_index("head")
    tokens = lax.dynamic_slice_in_dim(tokens, me * n, n, 0)
    cotangent = lax.dynamic_slice_in_dim(cotangent, me * n, n, 0)
    before = lax.ppermute(tokens[:, length - PAD :], "seq", [(i, i + 1) for i in range(ranges - 1)])
    padded = jnp.concatenate([before, tokens], axis=1)

    start = lax.axis_index("seq") * length
    lead = jnp.concatenate(
        [jnp.full((seqs, PAD), -1, jnp.int32), doc_ids, jnp.full((seqs, PAD), -2, jnp.int32)], axis=1
    )
    ids = lax.dynamic_slice(lead, (me * n, start), (n, length + 2 * PAD)).astype(F32)
    id_rows = jnp.broadcast_to(ids[:, None, PAD : PAD + length], (n, 8, length))
    ids = jnp.broadcast_to(ids[:, :, None], (n, length + 2 * PAD, LANES))

    pack = jnp.concatenate(
        [
            conv_x,
            gated_gain[None],
            padded_lanes(head_params, width),
            jnp.transpose(timestep_input_weight).astype(F32).reshape(heads * model // width, width),
        ],
        axis=0,
    )
    packs = gathered(pack)
    in_weights = gathered(head_input_weight.reshape(model, 2 * width))
    out_weights = gathered(output_weight)
    small = jnp.stack([jnp.pad(v[6:9, :heads], ((0, 5), (0, LANES - heads))) for v in packs])
    step_weights = [jnp.pad(v[9:].reshape(heads, model).astype(BF16), ((0, LANES - heads), (0, 0))) for v in packs]
    skips = [jnp.repeat(v[8, :heads], HEAD_DIM)[None] for v in packs]
    params = jnp.stack(
        [jnp.concatenate([v[:6], skip, jnp.zeros((1, width), F32)], axis=0) for v, skip in zip(packs, skips)]
    )
    state_taps = jnp.pad(conv_state, ((0, 3), (0, 0)))

    tok_float = padded.astype(F32)
    scale = lax.rsqrt(jnp.mean(tok_float * tok_float, axis=-1, keepdims=True) + EPS)
    normed = (tok_float * scale * norm_gain).astype(BF16)
    gate, rows, raw, state_rows = project(normed, state_input_weight, in_weights, step_weights)
    lane = lax.broadcasted_iota(jnp.int32, (1, 1, 1, LANES), 3) < heads
    step_in = raw + small[:, None, 0:1]
    steps = jnp.where(lane, jax.nn.softplus(step_in), 0.0)
    log_decay = -steps * jnp.exp(small[:, None, 1:2])
    bc = conv_state_call(state_rows, ids, state_taps)
    acted, cum, message = state_call(rows, bc, ids, steps, log_decay, params)
    mixed, states = inside_call(acted, bc, ids, id_rows, steps, cum)
    entered = relay(message, False)
    output, normed_out, d_gate, d_summed, pulled, gain_parts, skip_parts = middle_call(
        mixed, gate, acted, cum, entered, bc, ids, tokens, cotangent, params, message, out_weights, width * blocks
    )
    whole_output = assembled(output)
    leaving = relay(pulled, True)
    d_scaled, d_b, d_c, d_cum = inside_back_call(
        acted, d_summed, mixed, bc, ids, id_rows, steps, cum, states, entered
    )
    d_rows, d_raw, d_b_more, taps_grad, small_grad = close_call(
        rows, acted, d_summed, d_scaled, bc, ids, steps, raw, log_decay, cum, d_cum, leaving, entered, params, small
    )
    d_state, state_taps_grad = conv_state_back_call(state_rows, ids, state_taps, d_b, d_b_more, d_c)
    input_grad, edge, halo, norm_parts = input_call(
        d_gate, d_rows, d_raw, d_state, padded, cotangent, norm_gain[None], state_input_weight, in_weights, step_weights
    )
    halo = lax.ppermute(halo, "seq", [(i + 1, i) for i in range(ranges - 1)])
    edge = (edge + halo.astype(F32)).astype(BF16)
    input_grad = lax.dynamic_update_slice(input_grad, edge, (0, length - PAD, 0))
    whole_input = assembled(input_grad)

    def over_tokens(a, b):
        return jnp.einsum("std,stc->dc", a, b, preferred_element_type=F32)

    plain = normed[:, PAD:]
    out_total = scattered([over_tokens(cotangent, normed_out[r]).astype(BF16) for r in range(blocks)])
    gate_total = scattered([over_tokens(plain, d_gate[r]).astype(BF16) for r in range(blocks)])
    rows_total = scattered([over_tokens(normed, d_rows[r]).astype(BF16) for r in range(blocks)])
    out_grad = jnp.transpose(ranges_sum(out_total))
    heads_grad = jnp.stack([ranges_sum(gate_total), ranges_sum(rows_total)], axis=1)
    state_grad = summed_over(ranges_sum(over_tokens(normed, d_state).astype(BF16)), "head")

    d_raw = d_raw.astype(BF16)
    step_grads = [
        jnp.einsum("sth,std->hd", d_raw[r, :, :, :heads], plain, preferred_element_type=F32) for r in range(blocks)
    ]
    smalls = []
    for r in range(blocks):
        taps = jnp.sum(taps_grad[r], axis=0)[:5]
        gain = jnp.sum(gain_parts[r], axis=0)[None]
        skip = jnp.sum(jnp.sum(skip_parts[r], axis=0).reshape(heads, HEAD_DIM), axis=1)
        rest = jnp.sum(small_grad[r], axis=0)[:2, :heads]
        head_rows = padded_lanes(jnp.concatenate([rest, skip[None]], axis=0), width)
        smalls.append(jnp.concatenate([taps, gain, head_rows, step_grads[r].reshape(-1, width)], axis=0))
    own = summed_over(scattered(smalls), "seq")
    shared = jnp.concatenate(
        [jnp.sum(norm_parts, axis=(0, 1)).reshape(-1, 2 * LANES), jnp.sum(state_taps_grad, axis=0)[:5]], axis=0
    )
    shared = summed_over(summed_over(shared, "head"), "seq")
    count = model // (2 * LANES)
    return (
        whole_output,
        whole_input,
        shared[:count].reshape(model),
        heads_grad,
        state_grad,
        jnp.transpose(own[9:].reshape(heads, model)),
        own[:5],
        shared[count:],
        own[6:9, :heads],
        own[5],
        out_grad,
    )


def solution(mesh):
    return jax.shard_map(
        shards,
        mesh=mesh,
        in_specs=(
            P(None, "seq", None),
            P(),
            P(),
            P(None, None, "head"),
            P(),
            P(None, "head"),
            P(None, "head"),
            P(),
            P(None, "head"),
            P("head"),
            P("head", None),
            P(None, "seq", None),
        ),
        out_specs=(
            P(None, "seq", None),
            P(None, "seq", None),
            P(),
            P("seq", None, "head"),
            P("seq", None),
            P(None, "head"),
            P(None, "head"),
            P(),
            P(None, "head"),
            P("head"),
            P("head", "seq"),
        ),
        check_vma=False,
    )
```

```python
import functools

import jax
import jax.numpy as jnp
from jax import lax
from jax.experimental import pallas as pl
from jax.experimental.pallas import tpu as pltpu
from jax.sharding import PartitionSpec as P

F32 = jnp.float32
BF16 = jnp.bfloat16
EPS = 1e-5
CHUNK = 128
PAD = 16
LANES = 128
HEAD_DIM = 64
VMEM = 60 * 1024 * 1024


def dot(a, b):
    return lax.dot_general(a, b, (((1,), (0,)), ((), ())), preferred_element_type=F32)


def dot_nt(a, b):
    return lax.dot_general(a, b, (((1,), (1,)), ((), ())), preferred_element_type=F32)


def dot_tn(a, b):
    return lax.dot_general(a, b, (((0,), (0,)), ((), ())), preferred_element_type=F32)


def split(value):
    high = value.astype(BF16)
    return high, (value - high.astype(F32)).astype(BF16)


def head_map(width, offset):
    lane = lax.broadcasted_iota(jnp.int32, (LANES, width), 1)
    row = lax.broadcasted_iota(jnp.int32, (LANES, width), 0)
    return (lax.shift_right_logical(lane, 6) + offset == row).astype(F32).astype(BF16)


def expand(value, width, offset):
    lane = lax.shift_right_logical(lax.broadcasted_iota(jnp.int32, value.shape, 1), 6) + offset
    return jnp.concatenate(
        [jnp.take_along_axis(value, lane + 2 * p, axis=1) for p in range(width // LANES)], axis=1
    )


def expand_row(value, width, offset):
    return expand(jnp.broadcast_to(value, (8, LANES)), width, offset)


def column(value, index):
    return jnp.take_along_axis(value, jnp.zeros(value.shape, jnp.int32) + index, axis=1)


def by_head(value, heads):
    high, low = split(value)
    return dot_nt(high, heads) + dot_nt(low, heads)


def by_head_low(value, heads):
    return dot_nt(value.astype(BF16), heads)


def widen(value, width):
    return jnp.concatenate([value] * (width // LANES), axis=1)


def fold8(value):
    return value[0:8] + value[8:16]


def sigmoid(value):
    return 0.5 * jnp.tanh(0.5 * value) + 0.5


def triangle(lower):
    row = lax.broadcasted_iota(jnp.int32, (CHUNK, CHUNK), 0)
    column = lax.broadcasted_iota(jnp.int32, (CHUNK, CHUNK), 1)
    return (row >= column if lower else row <= column)


def exact_dot(ones, value):
    return jnp.dot(ones, value, precision=lax.Precision.HIGHEST, preferred_element_type=F32)


def rows_at(start, count):
    return pl.ds(pl.multiple_of(start, 16), count)


def entering_maps(columns, rows, first, count):
    window = count + PAD
    token = lax.broadcasted_iota(jnp.int32, (count, window), 0)
    entry = lax.broadcasted_iota(jnp.int32, (count, window), 1)
    same = wide_marks(columns[0, first : first + count, :], window) == rows[0, 0:1, first - PAD : first + count]
    distance = entry - token
    return jnp.concatenate(
        [jnp.where(same & (distance == PAD - 3 + k), 1.0, 0.0).astype(BF16) for k in range(3)], axis=0
    )


def leaving_maps(columns, rows, first, count):
    window = count + PAD
    row = lax.broadcasted_iota(jnp.int32, (count, window), 0)
    token = lax.broadcasted_iota(jnp.int32, (count, window), 1)
    same = wide_marks(columns[0, first : first + count, :], window) == rows[0, 0:1, first : first + window]
    distance = token - row
    return jnp.concatenate(
        [jnp.where(same & (distance == 3 - k), 1.0, 0.0).astype(BF16) for k in range(3)], axis=0
    )


def wide_marks(columns, window):
    whole = jnp.concatenate([columns] * -(-window // LANES), axis=1)
    return whole[:, :window]


def conv_sum(rows, maps, taps, first, lanes):
    moved = dot(maps, rows[first - PAD : first + CHUNK, lanes])
    entering = [moved[k * CHUNK : (k + 1) * CHUNK] for k in range(3)]
    entering.append(rows[first : first + CHUNK, lanes].astype(F32))
    total = taps[4:5, lanes]
    for k in range(4):
        total = total + taps[k : k + 1, lanes] * entering[k]
    return total, entering


def lane_groups(width):
    step = min(width, 2 * LANES)
    return [slice(i, i + step) for i in range(0, width, step)]


def conv_forward(rows, ids, id_rows, taps, store, length):
    for c in range(length // CHUNK):
        first = PAD + c * CHUNK
        maps = entering_maps(ids, id_rows, first, CHUNK)
        for lanes in lane_groups(rows.shape[1]):
            total, _ = conv_sum(rows, maps, taps, first, lanes)
            store(slice(c * CHUNK, (c + 1) * CHUNK), lanes, (total * sigmoid(total)).astype(BF16))


def conv_backward(rows, ids, id_rows, taps, d_acted, d_pre, d_rows, length):
    width = d_pre.shape[1]
    zero = jnp.zeros((16, width), BF16)
    d_pre[0:16, :] = zero
    d_pre[length + PAD : length + PAD + 16, :] = zero
    groups = lane_groups(width)
    sums = [[jnp.zeros((8, g.stop - g.start), F32) for _ in range(5)] for g in groups]
    for c in range(length // CHUNK - 1, -1, -1):
        first = PAD + c * CHUNK
        here = slice(first, first + CHUNK)
        maps = entering_maps(ids, id_rows, first, CHUNK)
        back = leaving_maps(ids, id_rows, first, CHUNK)
        for i, lanes in enumerate(groups):
            total, entering = conv_sum(rows, maps, taps, first, lanes)
            sigma = sigmoid(total)
            grad = d_acted(c, lanes) * (sigma * (1.0 + total * (1.0 - sigma)))
            d_pre[here, lanes] = grad.astype(BF16)
            for k in range(5):
                product = grad * entering[k] if k < 4 else grad
                sums[i][k] = sums[i][k] + jnp.sum(product.reshape(CHUNK // 8, 8, -1), axis=0)
            moved = dot(back, d_pre[first : first + CHUNK + PAD, lanes])
            result = taps[3:4, lanes] * grad
            for k in range(3):
                result = result + taps[k : k + 1, lanes] * moved[k * CHUNK : (k + 1) * CHUNK]
            d_rows(here, lanes, result.astype(BF16))
    back = leaving_maps(ids, id_rows, 0, PAD)
    for lanes in groups:
        moved = dot(back, d_pre[0 : 2 * PAD, lanes])
        result = taps[0:1, lanes] * moved[0:PAD]
        for k in range(1, 3):
            result = result + taps[k : k + 1, lanes] * moved[k * PAD : (k + 1) * PAD]
        d_rows(slice(0, PAD), lanes, result.astype(BF16))
    return [
        jnp.concatenate([jnp.sum(part[k], axis=0, keepdims=True) for part in sums], axis=1) for k in range(5)
    ]


def softplus(value):
    return jnp.maximum(value, 0.0) + jnp.log1p(jnp.exp(-jnp.abs(value)))


def project_rows(values, weights, rows):
    for r, weight in enumerate(weights):
        rows[r, 0] = dot(values, weight[...]).astype(BF16)


def project_first_kernel(blocks, heads, normed, state_w, step_w, small, ids, id_rows, taps, *refs):
    weights, refs = refs[:blocks], refs[blocks:]
    rows, raw, steps, log_decay, cum, state_rows, bc = refs
    length = bc.shape[1]
    values = normed[0]
    state_rows[0] = dot(values, state_w[...]).astype(BF16)
    part = dot_nt(values[PAD:], step_w[...])
    raw[0] = part
    lane = lax.broadcasted_iota(jnp.int32, (length, LANES), 1)
    size = jnp.where(lane < heads, softplus(part + small[0:1, :]), 0.0)
    steps[0] = size
    log_decay[0] = -size * jnp.exp(small[1:2, :])
    ones = triangle(True).astype(F32)
    total = jnp.zeros((1, LANES), F32)
    for c in range(length // CHUNK):
        here = slice(c * CHUNK, (c + 1) * CHUNK)
        value = exact_dot(ones, log_decay[0, here, :]) + total
        cum[0, here, :] = value
        total = value[CHUNK - 1 : CHUNK]

    def store(here, lanes, value):
        bc[0, here, lanes] = value

    conv_forward(state_rows.at[0], ids, id_rows, taps[...], store, length)
    project_rows(values, weights, rows)


def project_more_kernel(blocks, normed, held, *refs):
    project_rows(normed[0], refs[:blocks], refs[blocks])


def project_first(normed, state_w, step_w, small, ids, id_rows, taps, weights, blocks, heads):
    n, padded, model = normed.shape
    width = weights[0].shape[1]
    length = padded - PAD
    whole = lambda a: pl.BlockSpec(a.shape, lambda s: (0,) * a.ndim, pipeline_mode=pl.Buffered(1))
    per_seq = lambda a, b: pl.BlockSpec((1, a, b), lambda s: (s, 0, 0))
    lanes = jax.ShapeDtypeStruct((n, length, LANES), F32)
    return pl.pallas_call(
        functools.partial(project_first_kernel, len(weights), heads),
        grid=(n,),
        in_specs=[
            per_seq(padded, model), whole(state_w), whole(step_w), whole(small), per_seq(*ids.shape[1:]),
            per_seq(*id_rows.shape[1:]), whole(taps),
        ] + [whole(v) for v in weights],
        out_specs=[pl.BlockSpec((len(weights), 1, padded, width), lambda s: (0, s, 0, 0))]
        + [per_seq(length, LANES)] * 4
        + [per_seq(padded, 2 * LANES), per_seq(length, 2 * LANES)],
        out_shape=[
            jax.ShapeDtypeStruct((blocks, n, padded, width), BF16), lanes, lanes, lanes, lanes,
            jax.ShapeDtypeStruct((n, padded, 2 * LANES), BF16),
            jax.ShapeDtypeStruct((n, length, 2 * LANES), BF16),
        ],
        compiler_params=pltpu.CompilerParams(vmem_limit_bytes=VMEM),
        name="project_first",
    )(normed, state_w, step_w, small, ids, id_rows, taps, *weights)


def project_more(normed, rows, weights, first):
    n, padded, model = normed.shape
    width = weights[0].shape[1]
    count = len(weights)
    return pl.pallas_call(
        functools.partial(project_more_kernel, count),
        grid=(n,),
        in_specs=[pl.BlockSpec((1, padded, model), lambda s: (s, 0, 0)), pl.BlockSpec(memory_space=pl.ANY)]
        + [pl.BlockSpec(v.shape, lambda s: (0, 0), pipeline_mode=pl.Buffered(1)) for v in weights],
        out_specs=pl.BlockSpec((count, 1, padded, width), lambda s: (first // count, s, 0, 0)),
        out_shape=jax.ShapeDtypeStruct(rows.shape, BF16),
        input_output_aliases={1: 0},
        compiler_params=pltpu.CompilerParams(vmem_limit_bytes=VMEM),
        name="project_more",
    )(normed, rows, *weights)


def project_gate_kernel(blocks, normed, *refs):
    for r in range(blocks):
        refs[blocks][r, 0] = dot(normed[0, PAD:, :], refs[r][...]).astype(BF16)


def project_gate(normed, weights):
    n, padded, model = normed.shape
    width = weights[0].shape[1]
    count = len(weights)
    return pl.pallas_call(
        functools.partial(project_gate_kernel, count),
        grid=(n,),
        in_specs=[pl.BlockSpec((1, padded, model), lambda s: (s, 0, 0))]
        + [pl.BlockSpec(v.shape, lambda s: (0, 0), pipeline_mode=pl.Buffered(1)) for v in weights],
        out_specs=pl.BlockSpec((count, 1, padded - PAD, width), lambda s: (0, s, 0, 0)),
        out_shape=jax.ShapeDtypeStruct((count, n, padded - PAD, width), BF16),
        compiler_params=pltpu.CompilerParams(vmem_limit_bytes=VMEM),
        name="project_gate",
    )(normed, *weights)


def write_message(message, state, survive):
    cuts, rows, width = message.shape
    own = rows - 16
    survive = jnp.concatenate([survive, survive], axis=0).astype(BF16)
    for i in range(cuts):
        message[i, :own, :] = state[i * own : (i + 1) * own].astype(BF16)
        message[i, own:, :] = survive


def state_kernel(first, per_block, rows, bc, ids, id_rows, steps, cum, taps, *refs):
    acted, message = refs[-2:]
    length, width = acted.shape[2:]
    offset = (pl.program_id(0) + first) * per_block

    def store(here, lanes, value):
        acted[0, 0, here, lanes] = value

    conv_forward(rows.at[0, 0], ids, id_rows, taps[0], store, length)
    total = cum[0, length - 1 : length, :]
    last = ids[0, PAD + length - 1 : PAD + length, :]
    before = ids[0, PAD - 1 : PAD, :]
    state = jnp.zeros((LANES, width), F32)
    for c in range(length // CHUNK):
        here = slice(c * CHUNK, (c + 1) * CHUNK)
        same = (ids[0, PAD + c * CHUNK : PAD + (c + 1) * CHUNK, :] == last).astype(F32)
        tail = jnp.exp(total - cum[0, here, :]) * same * steps[0, here, :]
        scaled = (expand(tail, width, offset) * acted[0, 0, here, :].astype(F32)).astype(BF16)
        state = state + dot_tn(bc[0, here, :LANES], scaled)
    survive = jnp.exp(total) * (last == before).astype(F32)
    write_message(message.at[0, 0], state, expand_row(survive, width, offset))


def state_call(rows, bc, ids, id_rows, steps, cum, taps, held, first, count, per_block, cuts):
    blocks, n, padded, width = rows.shape
    length = padded - PAD
    four = lambda a, b: pl.BlockSpec((1, 1, a, b), lambda g, s: (g + first, s, 0, 0))
    per_seq = lambda a: pl.BlockSpec((1,) + a.shape[1:], lambda g, s: (s, 0, 0))
    piece = LANES // cuts + 16
    return pl.pallas_call(
        functools.partial(state_kernel, first, per_block),
        grid=(count, n),
        in_specs=[
            four(padded, width), per_seq(bc), per_seq(ids), per_seq(id_rows), per_seq(steps), per_seq(cum),
            pl.BlockSpec((1,) + taps.shape[1:], lambda g, s: (g + first, 0, 0)),
        ] + [pl.BlockSpec(memory_space=pl.ANY) for _ in held],
        out_specs=[
            four(length, width),
            pl.BlockSpec((1, 1, cuts, piece, width), lambda g, s: (g + first, s, 0, 0, 0)),
        ],
        out_shape=[
            jax.ShapeDtypeStruct((blocks, n, length, width), BF16),
            jax.ShapeDtypeStruct((blocks, n, cuts, piece, width), BF16),
        ],
        input_output_aliases={7: 0, 8: 1} if held else {},
        compiler_params=pltpu.CompilerParams(vmem_limit_bytes=VMEM),
        name="range_state",
    )(rows, bc, ids, id_rows, steps, cum, taps, *held)


def chunk_marks(ids, c):
    first = PAD + c * CHUNK
    return ids[0, first : first + CHUNK, :], ids[0, first + CHUNK - 1 : first + CHUNK, :], ids[0, first - 1 : first, :]


def chunk_decays(ids, cum, c):
    here, last, before = chunk_marks(ids, c)
    value = cum[0, c * CHUNK : (c + 1) * CHUNK, :]
    base = cum[0, c * CHUNK - 1 : c * CHUNK, :] if c else jnp.zeros((1, LANES), F32)
    end = value[CHUNK - 1 : CHUNK]
    entering = jnp.exp(value - base) * (here == before).astype(F32)
    tail = jnp.exp(end - value) * (here == last).astype(F32)
    survive = jnp.exp(end - base) * (last == before).astype(F32)
    return entering, tail, survive


def lane_halves(pair):
    lane = lax.broadcasted_iota(jnp.int32, pair.shape, 1)
    zero = jnp.zeros_like(pair)
    return jnp.concatenate([jnp.where(lane < HEAD_DIM, pair, zero), jnp.where(lane < HEAD_DIM, zero, pair)], axis=0)


def inside_kernel(per_block, acted, bc, ids, id_rows, steps, cum, mixed, states, carried, turned):
    length, width = acted.shape[2:]
    offset = pl.program_id(1) * per_block
    later = triangle(True)
    for c in range(length // CHUNK):
        here = slice(c * CHUNK, (c + 1) * CHUNK)
        b_part, c_part = bc[0, here, :LANES], bc[0, here, LANES:]
        marks, _, _ = chunk_marks(ids, c)
        same = later & (marks == id_rows[0, 0:1, PAD + c * CHUNK : PAD + (c + 1) * CHUNK])
        scores = jnp.where(same, dot_nt(c_part, b_part), 0.0)
        value = cum[0, here, :]
        turned[...] = jnp.transpose(value)
        entering, tail, survive = chunk_decays(ids, cum, c)
        scaled = (expand(steps[0, here, :], width, offset) * acted[0, 0, here, :].astype(F32)).astype(BF16)
        if c:
            held = carried[...]
            held_low = held.astype(BF16)
            states[0, 0, c - 1] = held_low
            outside = dot(c_part, held_low) * expand(entering, width, offset)
        for pair in range(width // LANES):
            lanes = slice(pair * LANES, (pair + 1) * LANES)
            mixing = []
            for h in (2 * pair, 2 * pair + 1):
                spread = jnp.minimum(column(value, offset + h) - turned[pl.ds(offset + h, 1), :], 0.0)
                mixing.append((scores * jnp.exp(spread)).astype(BF16))
            result = dot(jnp.concatenate(mixing, axis=1), lane_halves(scaled[:, lanes]))
            mixed[0, 0, here, lanes] = result + outside[:, lanes] if c else result
        if c + 1 < length // CHUNK:
            fresh = dot_tn(b_part, (expand(tail, width, offset) * scaled.astype(F32)).astype(BF16))
            if c:
                fresh = fresh + held * expand_row(survive, width, offset)[0:1]
            carried[...] = fresh


def inside_call(acted, bc, ids, id_rows, steps, cum, per_block):
    blocks, n, length, width = acted.shape
    chunks = length // CHUNK
    four = lambda a, b: pl.BlockSpec((1, 1, a, b), lambda s, g: (g, s, 0, 0))
    per_seq = lambda a: pl.BlockSpec((1,) + a.shape[1:], lambda s, g: (s, 0, 0))
    return pl.pallas_call(
        functools.partial(inside_kernel, per_block),
        grid=(n, blocks),
        in_specs=[four(length, width), per_seq(bc), per_seq(ids), per_seq(id_rows), per_seq(steps), per_seq(cum)],
        out_specs=[
            four(length, width),
            pl.BlockSpec((1, 1, chunks - 1, LANES, width), lambda s, g: (g, s, 0, 0, 0)),
        ],
        out_shape=[
            jax.ShapeDtypeStruct((blocks, n, length, width), F32),
            jax.ShapeDtypeStruct((blocks, n, chunks - 1, LANES, width), BF16),
        ],
        scratch_shapes=[pltpu.VMEM((LANES, width), F32), pltpu.VMEM((LANES, LANES), F32)],
        compiler_params=pltpu.CompilerParams(vmem_limit_bytes=VMEM),
        name="inside",
    )(acted, bc, ids, id_rows, steps, cum)


def relay_kernel(backward, message, carried):
    ranges, rows, width = carried.shape
    state = jnp.zeros((rows, width), F32)
    order = range(ranges - 1, -1, -1) if backward else range(ranges)
    for q in order:
        carried[q] = state.astype(BF16)
        decay = message[q, rows : rows + 1, :].astype(F32)
        state = state * decay + message[q, :rows, :].astype(F32)


def after(value, *others):
    return lax.optimization_barrier((value,) + others)[0]


def relay_out(message, backward, meanwhile):
    blocks, n, cuts, rows, width = message.shape
    ranges = lax.axis_size("seq")
    arrived = lax.all_to_all(message.reshape(ranges, rows, width), "seq", 0, 0, tiled=True)
    return pl.pallas_call(
        functools.partial(relay_kernel, backward),
        out_shape=jax.ShapeDtypeStruct((ranges, rows - 16, width), BF16),
        compiler_params=pltpu.CompilerParams(vmem_limit_bytes=VMEM),
        name="relay",
    )(after(arrived, *meanwhile))


def relay_back(carried, message):
    blocks, n, _, _, width = message.shape
    return lax.all_to_all(carried, "seq", 0, 0, tiled=True).reshape(blocks, n, LANES, width)


def middle_kernel(
    blocks, per_block, total_width, mixed, gate, acted, cum, cum_end, bc, ids, ids_before, ids_after, tokens, cotangent,
    params, entered, *refs
):
    weights, refs = refs[:blocks], refs[blocks:]
    output, normed_out, d_gate, d_summed, pulled, gain_grad, skip_grad = refs[:7]
    summed_s, gated_s, grad_s, first_s, second_s, low_s, row_s, pull_s = refs[7:]
    tile, width = mixed.shape[2:]
    t = pl.program_id(0)
    before = ids_before[0, PAD - 1 : PAD, :]
    marks = ids[0]
    c_part = bc[0, :, LANES:]
    slabs = tile // 16
    same = (marks == before).astype(F32)
    decay = jnp.exp(cum[0]) * same
    row_s[...] = jnp.zeros_like(row_s)

    def lanes_sum(value):
        total = value[:, :LANES]
        for i in range(1, width // LANES):
            total = total + value[:, i * LANES : (i + 1) * LANES]
        return total

    @pl.when(t == 0)
    def _():
        gain_grad[...] = jnp.zeros_like(gain_grad)
        skip_grad[...] = jnp.zeros_like(skip_grad)
        pull_s[...] = jnp.zeros_like(pull_s)

    for r in range(blocks):
        first_s[...] = dot(c_part, entered[r, 0])
        second_s[r] = expand(decay, width, r * per_block)
        skip = params[r, 6:7, :]

        def step(i, carry, r=r, skip=skip):
            here = rows_at(i * 16, 16)
            value = mixed[r, 0, here, :] + first_s[here, :] * second_s[r, here, :]
            summed = value + skip * acted[r, 0, here, :].astype(F32)
            g = gate[r, 0, here, :].astype(F32)
            gated = summed * (g * sigmoid(g))
            summed_s[r, here, :] = summed
            gated_s[r, here, :] = gated
            row_s[here, :] = row_s[here, :] + lanes_sum(gated * gated)
            return carry

        lax.fori_loop(0, slabs, step, 0, unroll=4)
    squares = jnp.sum(row_s[...], axis=1, keepdims=True)
    rescale = jnp.broadcast_to(lax.rsqrt(squares / total_width + EPS), (tile, LANES))
    row_s[...] = rescale
    for r in range(blocks):
        gain = params[r, 5:6, :]

        def step(i, carry, r=r, gain=gain):
            here = rows_at(i * 16, 16)
            normed_out[r, 0, here, :] = (gated_s[r, here, :] * widen(row_s[here, :], width) * gain).astype(BF16)
            return carry

        lax.fori_loop(0, slabs, step, 0, unroll=4)
    branch = tokens[0].astype(F32)
    for r in range(blocks):
        branch = branch + dot(normed_out[r, 0], weights[r][...])
    output[0] = branch.astype(BF16)
    first_s[:, :LANES] = jnp.zeros((tile, LANES), F32)
    for r in range(blocks):
        grad_s[r] = dot_nt(cotangent[0], weights[r][...])
        gain = params[r, 5:6, :]

        def step(i, total, r=r, gain=gain):
            here = rows_at(i * 16, 16)
            both = grad_s[r, here, :] * gated_s[r, here, :]
            first_s[here, :LANES] = first_s[here, :LANES] + lanes_sum(both * gain)
            return total + fold8(both * widen(row_s[here, :], width))

        gain_grad[r] = gain_grad[r] + lax.fori_loop(0, slabs, step, jnp.zeros((8, width), F32), unroll=4)
    cross = jnp.sum(first_s[:, :LANES], axis=1, keepdims=True) / total_width
    first_s[:, :LANES] = rescale * rescale * rescale * cross
    for r in range(blocks):
        gain = params[r, 5:6, :]

        def step(i, total, r=r, gain=gain):
            here = rows_at(i * 16, 16)
            g = gate[r, 0, here, :].astype(F32)
            sigma = sigmoid(g)
            d_gated = widen(row_s[here, :], width) * (grad_s[r, here, :] * gain) - gated_s[r, here, :] * widen(
                first_s[here, :LANES], width
            )
            d_sum = d_gated * (g * sigma)
            d_gate[r, 0, here, :] = (d_gated * summed_s[r, here, :] * (sigma * (1.0 + g * (1.0 - sigma)))).astype(BF16)
            low = d_sum.astype(BF16)
            d_summed[r, 0, here, :] = low
            low_s[here, :] = (d_sum * second_s[r, here, :]).astype(BF16)
            return total + fold8(d_sum * acted[r, 0, here, :].astype(F32))

        skip_grad[r] = skip_grad[r] + lax.fori_loop(0, slabs, step, jnp.zeros((8, width), F32), unroll=4)
        pull_s[r] = pull_s[r] + dot_tn(c_part, low_s[...])

    @pl.when(t == pl.num_programs(0) - 1)
    def _():
        survive = jnp.exp(cum_end[0, 7:8, :]) * (ids_after[0, PAD - 1 : PAD, :] == before).astype(F32)
        for r in range(blocks):
            write_message(pulled.at[r, 0], pull_s[r], expand_row(survive, width, r * per_block))


def middle_call(s, mixed, gate, acted, cum, entered, bc, ids, tokens, cotangent, params, weights, per_block, cuts):
    blocks, n, length, width = mixed.shape
    model = tokens.shape[2]
    tile = min(256, length)
    wide = lambda w: pl.BlockSpec((blocks, 1, tile, w), lambda t: (0, s, t, 0))
    wide_out = lambda w: pl.BlockSpec((blocks, 1, tile, w), lambda t: (0, 0, t, 0))
    rows = lambda w: pl.BlockSpec((1, tile, w), lambda t: (s, t, 0))
    one = lambda a: pl.BlockSpec((a.shape[0], 1) + a.shape[2:], lambda t: (0, s, 0, 0), pipeline_mode=pl.Buffered(1))
    whole = lambda a: pl.BlockSpec(a.shape, lambda t: (0,) * a.ndim, pipeline_mode=pl.Buffered(1))
    kept = lambda *shape: pl.BlockSpec(shape, lambda t: (0,) * len(shape))
    piece = LANES // cuts + 16
    edge = lambda a: pl.BlockSpec((1, PAD, LANES), lambda t: (s, a, 0))
    ids_here = ids[:, PAD : PAD + length]
    wide_shape = jax.ShapeDtypeStruct((blocks, 1, length, width), BF16)
    return pl.pallas_call(
        functools.partial(middle_kernel, blocks, per_block, width * blocks),
        grid=(length // tile,),
        in_specs=[
            wide(width), wide(width), wide(width), rows(LANES),
            pl.BlockSpec((1, 8, LANES), lambda t: (s, length // 8 - 1, 0)), rows(2 * LANES), rows(LANES),
            edge(0), edge(length // PAD), rows(model), rows(model), whole(params),
            one(entered),
        ] + [whole(v) for v in weights],
        out_specs=[
            pl.BlockSpec((1, tile, model), lambda t: (0, t, 0)), wide_out(width), wide_out(width), wide_out(width),
            kept(blocks, 1, cuts, piece, width), kept(blocks, 8, width), kept(blocks, 8, width),
        ],
        out_shape=[
            jax.ShapeDtypeStruct((1, length, model), BF16),
            wide_shape, wide_shape, wide_shape,
            jax.ShapeDtypeStruct((blocks, 1, cuts, piece, width), BF16),
            jax.ShapeDtypeStruct((blocks, 8, width), F32),
            jax.ShapeDtypeStruct((blocks, 8, width), F32),
        ],
        scratch_shapes=[
            pltpu.VMEM((blocks, tile, width), F32),
            pltpu.VMEM((blocks, tile, width), F32),
            pltpu.VMEM((blocks, tile, width), F32),
            pltpu.VMEM((tile, width), F32),
            pltpu.VMEM((blocks, tile, width), F32),
            pltpu.VMEM((tile, width), BF16),
            pltpu.VMEM((tile, LANES), F32),
            pltpu.VMEM((blocks, LANES, width), F32),
        ],
        compiler_params=pltpu.CompilerParams(vmem_limit_bytes=VMEM),
        name="middle",
    )(mixed, gate, acted, cum, cum, bc, ids_here, ids, ids, tokens, cotangent, params, entered, *weights)


def inside_back_kernel(
    per_block, acted, d_summed, mixed, bc, ids, id_rows, steps, cum, states, entered, d_scaled, d_b, d_c, d_cum,
    carried, turned,
):
    length, width = acted.shape[2:]
    chunks = length // CHUNK
    g = pl.program_id(0)
    offset = g * per_block
    heads = head_map(width, offset)
    sooner = triangle(False)
    first_before = ids[0, PAD - 1 : PAD, :]
    came = entered[0, 0]

    @pl.when(g == 0)
    def _():
        d_b[...] = jnp.zeros_like(d_b)
        d_c[...] = jnp.zeros_like(d_c)
        d_cum[...] = jnp.zeros_like(d_cum)

    for c in range(chunks - 1, -1, -1):
        here = slice(c * CHUNK, (c + 1) * CHUNK)
        b_part, c_part = bc[0, here, :LANES], bc[0, here, LANES:]
        marks, _, _ = chunk_marks(ids, c)
        same = sooner & (marks == id_rows[0, 0:1, PAD + c * CHUNK : PAD + (c + 1) * CHUNK])
        scores_t = jnp.where(same, dot_nt(b_part, c_part), 0.0)
        value = cum[0, here, :]
        turned[...] = jnp.transpose(value)
        entering, tail, survive = chunk_decays(ids, cum, c)
        scaled = (expand(steps[0, here, :], width, offset) * acted[0, 0, here, :].astype(F32)).astype(BF16)
        grad = d_summed[0, 0, here, :]
        grad_wide = grad.astype(F32)
        from_start = jnp.exp(value) * (marks == first_before).astype(F32)
        start_wide = expand(from_start, width, offset)
        d_c_part = dot_nt((grad_wide * start_wide).astype(BF16), came)
        dots = grad_wide * (mixed[0, 0, here, :] + start_wide * dot(c_part, came))
        if c < chunks - 1:
            held = carried[...]
            held_low = held.astype(BF16)
            tail_wide = expand(tail, width, offset)
            later = dot(b_part, held_low) * tail_wide
            d_b_part = dot_nt((tail_wide * scaled.astype(F32)).astype(BF16), held_low)
        if c:
            entering_grad = (expand(entering, width, offset) * grad_wide).astype(BF16)
            d_c_part = d_c_part + dot_nt(entering_grad, states[0, 0, c - 1])
        d_scores_t = jnp.zeros((CHUNK, CHUNK), F32)
        results = []
        for pair in range(width // LANES):
            lanes = slice(pair * LANES, (pair + 1) * LANES)
            products = dot_nt(lane_halves(scaled[:, lanes]), grad[:, lanes])
            mixing = []
            for half, h in enumerate((2 * pair, 2 * pair + 1)):
                spread = jnp.minimum(turned[pl.ds(offset + h, 1), :] - column(value, offset + h), 0.0)
                decay = jnp.exp(spread)
                mixing.append((scores_t * decay).astype(BF16))
                d_scores_t = d_scores_t + products[half * CHUNK : (half + 1) * CHUNK] * decay
            results.append(dot(jnp.concatenate(mixing, axis=1), lane_halves(grad[:, lanes])))
        result = jnp.concatenate(results, axis=1)
        if c < chunks - 1:
            result = result + later
        d_scaled[0, 0, here, :] = result.astype(BF16)
        d_cum[0, here, :] = d_cum[0, here, :] + by_head(dots - scaled.astype(F32) * result, heads)
        d_scores_t = jnp.where(same, d_scores_t, 0.0).astype(BF16)
        d_b_here = dot(d_scores_t, c_part)
        if c < chunks - 1:
            d_b_here = d_b_here + d_b_part
        d_b[0, here, :] = d_b[0, here, :] + d_b_here
        d_c[0, here, :] = d_c[0, here, :] + d_c_part + dot_tn(d_scores_t, b_part)
        if c:
            pulled = dot_tn(c_part, entering_grad)
            if c < chunks - 1:
                pulled = pulled + held * expand_row(survive, width, offset)[0:1]
            carried[...] = pulled


def inside_back_call(s, acted, d_summed, mixed, bc, ids, id_rows, steps, cum, states, entered, per_block):
    blocks, n, length, width = acted.shape
    four = lambda a, b: pl.BlockSpec((1, 1, a, b), lambda g: (g, s, 0, 0))
    own = lambda a, b: pl.BlockSpec((1, 1, a, b), lambda g: (g, 0, 0, 0))
    per_seq = lambda a: pl.BlockSpec((1,) + a.shape[1:], lambda g: (s, 0, 0))
    summed = pl.BlockSpec((1, length, LANES), lambda g: (0, 0, 0))
    lanes = jax.ShapeDtypeStruct((1, length, LANES), F32)
    return pl.pallas_call(
        functools.partial(inside_back_kernel, per_block),
        grid=(blocks,),
        in_specs=[
            four(length, width), own(length, width), four(length, width), per_seq(bc), per_seq(ids), per_seq(id_rows),
            per_seq(steps), per_seq(cum),
            pl.BlockSpec((1, 1) + states.shape[2:], lambda g: (g, s, 0, 0, 0)),
            four(LANES, width),
        ],
        out_specs=[own(length, width), summed, summed, summed],
        out_shape=[jax.ShapeDtypeStruct((blocks, 1, length, width), BF16), lanes, lanes, lanes],
        scratch_shapes=[pltpu.VMEM((LANES, width), F32), pltpu.VMEM((LANES, LANES), F32)],
        compiler_params=pltpu.CompilerParams(vmem_limit_bytes=VMEM),
        name="inside_back",
    )(acted, d_summed, mixed, bc, ids, id_rows, steps, cum, states, entered)


def close_kernel(
    per_block, rows, acted, d_summed, d_scaled, bc, ids, id_rows, steps, raw, log_decay, cum, d_cum, leaving, entered,
    params, small, state_rows, state_taps, d_b, d_c,
    d_rows, d_raw, d_state, taps_grad, state_taps_grad, small_grad, d_pre, d_acted, d_log, d_step, ends, d_bc, d_pre_bc,
):
    length, width = acted.shape[2:]
    chunks = length // CHUNK
    g = pl.program_id(0)
    offset = g * per_block
    heads = head_map(width, offset)
    last = ids[0, PAD + length - 1 : PAD + length, :]
    before = ids[0, PAD - 1 : PAD, :]
    end = cum[0, length - 1 : length, :]
    skip = params[0, 6:7, :]
    held = leaving[0, 0]
    came = entered[0, 0]

    @pl.when(g == 0)
    def _():
        d_bc[:, :LANES] = d_b[0]
        d_bc[:, LANES:] = d_c[0]
        d_log[...] = d_cum[0]
        d_step[...] = jnp.zeros_like(d_step)
        ends[...] = jnp.zeros_like(ends)

    boundary = jnp.zeros((1, LANES), F32)
    for c in range(chunks):
        here = slice(c * CHUNK, (c + 1) * CHUNK)
        marks, _, _ = chunk_marks(ids, c)
        tail = jnp.exp(end - cum[0, here, :]) * (marks == last).astype(F32)
        tail_wide = expand(tail, width, offset)
        steps_wide = expand(steps[0, here, :], width, offset)
        x = acted[0, 0, here, :].astype(F32)
        scaled = (steps_wide * x).astype(BF16).astype(F32)
        later = dot(bc[0, here, :LANES], held) * tail_wide
        total = d_scaled[0, 0, here, :].astype(F32) + later
        d_acted[here, :] = steps_wide * total + skip * d_summed[0, 0, here, :].astype(F32)
        d_bc[here, :LANES] = d_bc[here, :LANES] + dot_nt((tail_wide * scaled).astype(BF16), held)
        from_later = by_head_low(scaled * later, heads)
        boundary = boundary + jnp.sum(from_later, axis=0, keepdims=True)
        d_log[here, :] = d_log[here, :] - from_later
        d_step[here, :] = d_step[here, :] + by_head_low(x * total, heads)
    product = held.astype(F32) * came.astype(F32)
    product = jnp.sum(product.reshape(LANES // 8, 8, width), axis=0)
    survive = jnp.exp(end) * (last == before).astype(F32)
    boundary = boundary + survive * jnp.sum(by_head(jnp.concatenate([product, product * 0.0], axis=0), heads), axis=0, keepdims=True)
    ends[0:1, :] = ends[0:1, :] + boundary

    def store(here, lanes, value):
        d_rows[0, 0, here, lanes] = value

    sums = conv_backward(
        rows.at[0, 0],
        ids,
        id_rows,
        params[0],
        lambda c, lanes: d_acted[c * CHUNK : (c + 1) * CHUNK, lanes],
        d_pre,
        store,
        length,
    )
    taps_grad[0] = jnp.concatenate(sums + [jnp.zeros((3, width), F32)], axis=0)

    @pl.when(g == pl.num_programs(0) - 1)
    def _():
        rate = jnp.exp(small[1:2, :])
        ones = triangle(False).astype(F32)
        carry = ends[0:1, :]
        decay_sum = jnp.zeros((1, LANES), F32)
        bias_sum = jnp.zeros((1, LANES), F32)
        for c in range(chunks - 1, -1, -1):
            here = slice(c * CHUNK, (c + 1) * CHUNK)
            grads = exact_dot(ones, d_log[here, :]) + carry
            carry = grads[0:1]
            decay_sum = decay_sum + jnp.sum(grads * log_decay[0, here, :], axis=0, keepdims=True)
            value = (d_step[here, :] - grads * rate) * sigmoid(raw[0, here, :] + small[0:1, :])
            bias_sum = bias_sum + jnp.sum(value, axis=0, keepdims=True)
            d_raw[0, here, :] = value.astype(BF16)
        small_grad[...] = jnp.concatenate([bias_sum, decay_sum, jnp.zeros((6, LANES), F32)], axis=0)

        def store_state(here, lanes, value):
            d_state[0, here, lanes] = value

        sums = conv_backward(
            state_rows.at[0],
            ids,
            id_rows,
            state_taps[...],
            lambda c, lanes: d_bc[c * CHUNK : (c + 1) * CHUNK, lanes],
            d_pre_bc,
            store_state,
            length,
        )
        state_taps_grad[...] = jnp.concatenate(sums + [jnp.zeros((3, 2 * LANES), F32)], axis=0)


def close_call(
    s, rows, acted, d_summed, d_scaled, bc, ids, id_rows, steps, raw, log_decay, cum, d_cum, leaving, entered, params,
    small, state_rows, state_taps, d_b, d_c, per_block,
):
    blocks, n, length, width = acted.shape
    four = lambda a, b: pl.BlockSpec((1, 1, a, b), lambda g: (g, s, 0, 0))
    own = lambda a, b: pl.BlockSpec((1, 1, a, b), lambda g: (g, 0, 0, 0))
    per_seq = lambda a: pl.BlockSpec((1,) + a.shape[1:], lambda g: (s, 0, 0))
    kept = lambda *shape: pl.BlockSpec(shape, lambda g: (0,) * len(shape))
    whole = lambda a: kept(*a.shape)
    wide = own(length, width)
    return pl.pallas_call(
        functools.partial(close_kernel, per_block),
        grid=(blocks,),
        in_specs=[
            four(length + PAD, width), four(length, width), wide, wide, per_seq(bc), per_seq(ids), per_seq(id_rows),
            per_seq(steps), per_seq(raw), per_seq(log_decay), per_seq(cum), kept(1, length, LANES), own(LANES, width),
            four(LANES, width),
            pl.BlockSpec((1,) + params.shape[1:], lambda g: (g, 0, 0)), whole(small), per_seq(state_rows),
            whole(state_taps), whole(d_b), whole(d_c),
        ],
        out_specs=[
            own(length + PAD, width), kept(1, length, LANES), kept(1, length + PAD, 2 * LANES),
            pl.BlockSpec((1, 8, width), lambda g: (g, 0, 0)), kept(8, 2 * LANES), kept(8, LANES),
        ],
        out_shape=[
            jax.ShapeDtypeStruct((blocks, 1, length + PAD, width), BF16),
            jax.ShapeDtypeStruct((1, length, LANES), BF16),
            jax.ShapeDtypeStruct((1, length + PAD, 2 * LANES), BF16),
            jax.ShapeDtypeStruct((blocks, 8, width), F32),
            jax.ShapeDtypeStruct((8, 2 * LANES), F32),
            jax.ShapeDtypeStruct((8, LANES), F32),
        ],
        scratch_shapes=[
            pltpu.VMEM((length + 2 * PAD, width), BF16),
            pltpu.VMEM((length, width), F32),
            pltpu.VMEM((length, LANES), F32),
            pltpu.VMEM((length, LANES), F32),
            pltpu.VMEM((8, LANES), F32),
            pltpu.VMEM((length, 2 * LANES), F32),
            pltpu.VMEM((length + 2 * PAD, 2 * LANES), BF16),
        ],
        compiler_params=pltpu.CompilerParams(vmem_limit_bytes=VMEM),
        name="close",
    )(
        rows, acted, d_summed, d_scaled, bc, ids, id_rows, steps, raw, log_decay, cum, d_cum, leaving, entered, params,
        small, state_rows, state_taps, d_b, d_c,
    )


def input_kernel(blocks, d_gate, d_rows, d_raw, d_state, tokens, cotangent, gain, state_w, step_w, *refs):
    row_weights, refs = refs[:blocks], refs[blocks:]
    gate_weights, refs = refs[:blocks], refs[blocks:]
    input_grad, edge, halo, gain_grad, main_s, halo_s = refs
    length = d_gate.shape[2]
    total = dot_nt(d_state[0], state_w[...])
    halo_s[...] = total[:PAD]
    main_s[...] = total[PAD:] + dot(d_raw[0], step_w[...])
    for r in range(blocks):
        halo_s[...] = halo_s[...] + dot_nt(d_rows[r, 0, :PAD, :], row_weights[r][...])
        main_s[...] = main_s[...] + (
            dot_nt(d_rows[r, 0, PAD:, :], row_weights[r][...]) + dot_nt(d_gate[r, 0], gate_weights[r][...])
        )

    def norm_back(value, token):
        scale = lax.rsqrt(jnp.mean(token * token, axis=1, keepdims=True) + EPS)
        unit = value * gain[...]
        inner = jnp.mean(unit * token, axis=1, keepdims=True)
        return scale * unit - token * (scale * scale * scale * inner), fold8(value * token * scale)

    grad, sums = norm_back(halo_s[...], tokens[0, :PAD, :].astype(F32))
    halo[0] = grad.astype(BF16)

    def step(i, carry):
        here = rows_at(i * 16, 16)
        grad, more = norm_back(main_s[here, :], tokens[0, rows_at(PAD + i * 16, 16), :].astype(F32))
        value = grad + cotangent[0, here, :].astype(F32)
        edge[0] = value
        input_grad[0, here, :] = value.astype(BF16)
        return carry + more

    gain_grad[...] = lax.fori_loop(0, length // 16, step, sums, unroll=4)


def input_call(s, d_gate, d_rows, d_raw, d_state, tokens, cotangent, gain, state_w, step_w, row_weights, gate_weights):
    blocks, _, length, width = d_gate.shape
    padded, model = tokens.shape[1:]
    whole = lambda a: pl.BlockSpec(a.shape, lambda t: (0,) * a.ndim, pipeline_mode=pl.Buffered(1))
    one = lambda a, b: pl.BlockSpec((1, a, b), lambda t: (s, 0, 0), pipeline_mode=pl.Buffered(1))
    kept = lambda *shape: pl.BlockSpec(shape, lambda t: (0,) * len(shape), pipeline_mode=pl.Buffered(1))
    return pl.pallas_call(
        functools.partial(input_kernel, blocks),
        grid=(1,),
        in_specs=[
            whole(d_gate), whole(d_rows), whole(d_raw), whole(d_state), one(padded, model), one(length, model),
            whole(gain), whole(state_w), whole(step_w),
        ] + [whole(v) for v in row_weights] + [whole(v) for v in gate_weights],
        out_specs=[kept(1, length, model), kept(1, PAD, model), kept(1, PAD, model), kept(8, model)],
        out_shape=[
            jax.ShapeDtypeStruct((1, length, model), BF16),
            jax.ShapeDtypeStruct((1, PAD, model), F32),
            jax.ShapeDtypeStruct((1, PAD, model), BF16),
            jax.ShapeDtypeStruct((8, model), F32),
        ],
        scratch_shapes=[pltpu.VMEM((length, model), F32), pltpu.VMEM((PAD, model), F32)],
        compiler_params=pltpu.CompilerParams(vmem_limit_bytes=VMEM),
        name="input_gradient",
    )(d_gate, d_rows, d_raw, d_state, tokens, cotangent, gain, state_w, step_w, *row_weights, *gate_weights)


def assemble_kernel(count, places, *refs):
    parts, refs = refs[:count], refs[count:]
    edges, refs = (refs[:count], refs[count:]) if len(refs) > 2 * count else ((), refs)
    whole, buffers, (in_sem, out_sem) = refs[0], refs[1:-2], refs[-2:]
    length = parts[0].shape[1]
    reads = [pltpu.make_async_copy(p.at[0], b, in_sem.at[i]) for i, (p, b) in enumerate(zip(parts, buffers))]
    writes = [pltpu.make_async_copy(b, whole.at[places[i]], out_sem.at[i]) for i, b in enumerate(buffers)]
    for read in reads:
        read.start()
    for i, (read, write) in enumerate(zip(reads, writes)):
        read.wait()
        if edges:
            buffers[i][length - PAD :, :] = edges[i][0]
        write.start()
    for write in writes:
        write.wait()


def assemble(parts, edges, places):
    count = len(parts)
    _, length, model = parts[0].shape
    return pl.pallas_call(
        functools.partial(assemble_kernel, count),
        grid_spec=pltpu.PrefetchScalarGridSpec(
            num_scalar_prefetch=1,
            grid=(1,),
            in_specs=[pl.BlockSpec(memory_space=pl.ANY) for _ in parts]
            + [pl.BlockSpec((1, PAD, model), lambda t, i: (0, 0, 0)) for _ in edges],
            out_specs=pl.BlockSpec(memory_space=pl.ANY),
            scratch_shapes=[pltpu.VMEM((length, model), BF16) for _ in parts]
            + [pltpu.SemaphoreType.DMA((count,)), pltpu.SemaphoreType.DMA((count,))],
        ),
        out_shape=jax.ShapeDtypeStruct((count, length, model), BF16),
        compiler_params=pltpu.CompilerParams(vmem_limit_bytes=VMEM),
        name="assemble",
    )(jnp.stack(places).astype(jnp.int32), *parts, *edges)


def weight_grad_kernel(n, halo, *refs):
    turned, refs = refs[:n], refs[n:]
    grads, refs = refs[:n], refs[n:]
    total = None
    if halo:
        before, refs = refs[0], refs[1:]
    (out,) = refs
    for s in range(n):
        part = dot(turned[s][...], grads[s][0, 0, PAD if halo else 0 :, :])
        if halo:
            part = part + dot_tn(before[s], grads[s][0, 0, :PAD, :])
        total = part if total is None else total + part
    out[0] = total.astype(BF16)


def weight_grad(turned, grads, before=None):
    n = len(turned)
    model, length = turned[0].shape
    blocks, _, tokens, width = grads[0].shape
    halo = [] if before is None else [before]
    return pl.pallas_call(
        functools.partial(weight_grad_kernel, n, len(halo)),
        grid=(blocks,),
        in_specs=[pl.BlockSpec(v.shape, lambda g: (0, 0), pipeline_mode=pl.Buffered(1)) for v in turned]
        + [pl.BlockSpec((1, 1, tokens, width), lambda g: (g, 0, 0, 0)) for _ in grads]
        + [pl.BlockSpec(v.shape, lambda g: (0, 0, 0), pipeline_mode=pl.Buffered(1)) for v in halo],
        out_specs=pl.BlockSpec((1, model, width), lambda g: (g, 0, 0)),
        out_shape=jax.ShapeDtypeStruct((blocks, model, width), BF16),
        compiler_params=pltpu.CompilerParams(vmem_limit_bytes=VMEM),
        name="weight_gradient",
    )(*turned, *grads, *halo)


def small_grad_kernel(n, *refs):
    turned, refs = refs[:n], refs[n:]
    plain, refs = refs[:n], refs[n:]
    states, refs = refs[:n], refs[n:]
    steps, (before, state_out, step_out) = refs[:n], refs[n:]
    state, step = None, None
    for s in range(n):
        part = dot(turned[s][...], states[s][0, PAD:, :]) + dot_tn(before[s], states[s][0, :PAD, :])
        state = part if state is None else state + part
        part = dot_tn(steps[s][0], plain[s][...])
        step = part if step is None else step + part
    state_out[...] = state.astype(BF16)
    step_out[...] = step


def small_grad(turned, plain, states, steps, before):
    n = len(turned)
    model = turned[0].shape[0]
    return pl.pallas_call(
        functools.partial(small_grad_kernel, n),
        out_shape=[
            jax.ShapeDtypeStruct((model, 2 * LANES), BF16),
            jax.ShapeDtypeStruct((LANES, model), F32),
        ],
        compiler_params=pltpu.CompilerParams(vmem_limit_bytes=VMEM),
        name="small_weight_gradient",
    )(*turned, *plain, *states, *steps, before)


def swapped(value, axis, step):
    return lax.ppermute(value, axis, [(i, i ^ step) for i in range(lax.axis_size(axis))])


def gathered(value):
    parts = [value]
    for r in range(1, lax.axis_size("head")):
        parts.append(swapped(parts[r - 1], "head", 1) if r % 2 else swapped(value, "head", r))
    return parts


def scattered(parts, bits, shared=None):
    parts = list(parts)
    for bit in bits:
        kept = [r for r in range(len(parts)) if parts[r] is not None and not r & bit]
        send = [parts[r + bit] for r in kept] + ([] if shared is None else [shared])
        arrived = swapped(jnp.concatenate(send, axis=0), "head", bit)
        rows = parts[0].shape[0]
        for i, r in enumerate(kept):
            parts[r] = (parts[r].astype(F32) + arrived[i * rows : (i + 1) * rows].astype(F32)).astype(parts[r].dtype)
            parts[r + bit] = None
        if shared is not None:
            shared = shared + arrived[len(kept) * rows :]
    return parts, shared


def head_bits():
    return [1 << i for i in range((lax.axis_size("head") - 1).bit_length())]


def summed_weights(blocks_grads, ranges_first):
    bits = head_bits()
    parts, _ = scattered([blocks_grads[r] for r in range(blocks_grads.shape[0])], bits[:1])
    if ranges_first and len(bits) > 1:
        left = [r for r, part in enumerate(parts) if part is not None]
        width = blocks_grads.shape[2]
        total = ranges_sum(jnp.concatenate([parts[r] for r in left], axis=1))
        for i, r in enumerate(left):
            parts[r] = total[:, i * width : (i + 1) * width]
        return scattered(parts, bits[1:])[0][0]
    return ranges_sum(scattered(parts, bits[1:])[0][0])


def summed_over(value, axis):
    bit = 1
    while bit < lax.axis_size(axis):
        value = value + swapped(value, axis, bit)
        bit *= 2
    return value


def ranges_sum(value):
    ranges = lax.axis_size("seq")
    me = lax.axis_index("seq")
    rest = value.shape[1:]
    bit = 1
    while bit < ranges:
        mine = (me // bit) % 2
        halves = value.reshape((ranges // bit // 2, 2, -1) + rest)
        send = lax.dynamic_index_in_dim(halves, 1 - mine, 1, keepdims=False)
        keep = lax.dynamic_index_in_dim(halves, mine, 1, keepdims=False)
        total = keep.astype(F32) + swapped(send, "seq", bit).astype(F32)
        bit *= 2
        value = total.reshape((-1,) + rest).astype(value.dtype if bit < ranges else F32)
    return value


def assembled(parts, edges=None):
    n = len(parts)
    me = lax.axis_index("head")
    pieces, places, last_rows = [], [], []
    around = None if edges is None else gathered(jnp.concatenate(edges, axis=0))
    for s, value in enumerate(parts):
        for r, part in enumerate(gathered(value)):
            pieces.append(part)
            places.append((me ^ r) * n + s)
            if edges is not None:
                last_rows.append(around[r][s : s + 1])
    return assemble(pieces, last_rows, places)


def padded_lanes(value, size):
    return jnp.pad(value, ((0, 0), (0, size - value.shape[1])))


def shards(
    tokens,
    doc_ids,
    norm_gain,
    head_input_weight,
    state_input_weight,
    timestep_input_weight,
    conv_x,
    conv_state,
    head_params,
    gated_gain,
    output_weight,
    cotangent,
):
    seqs, length, model = tokens.shape
    blocks = lax.axis_size("head")
    ranges = lax.axis_size("seq")
    n = seqs // blocks
    width = gated_gain.shape[0]
    heads = head_params.shape[1]
    me = lax.axis_index("head")
    tokens = lax.dynamic_slice_in_dim(tokens, me * n, n, 0)
    cotangent = lax.dynamic_slice_in_dim(cotangent, me * n, n, 0)
    before = lax.ppermute(tokens[:, length - PAD :], "seq", [(i, i + 1) for i in range(ranges - 1)])
    padded = jnp.concatenate([before, tokens], axis=1)

    start = lax.axis_index("seq") * length
    lead = jnp.concatenate(
        [jnp.full((seqs, PAD), -1, jnp.int32), doc_ids, jnp.full((seqs, PAD), -2, jnp.int32)], axis=1
    )
    ids = lax.dynamic_slice(lead, (me * n, start), (n, length + 2 * PAD)).astype(F32)
    id_rows = jnp.broadcast_to(ids[:, None], (n, 8, length + 2 * PAD))
    ids = jnp.broadcast_to(ids[:, :, None], (n, length + 2 * PAD, LANES))

    pack = jnp.concatenate(
        [
            conv_x,
            gated_gain[None],
            padded_lanes(head_params, width),
            jnp.transpose(timestep_input_weight).astype(F32).reshape(heads * model // width, width),
        ],
        axis=0,
    )
    half = blocks // 2
    packs = gathered(pack)
    row_weights = gathered(head_input_weight[:, 1])
    gate_own = after(head_input_weight[:, 0], row_weights[half])
    out_own = after(output_weight, row_weights[half])
    packed = lambda rows: jnp.pad(jnp.concatenate(rows, axis=1), ((0, 0), (0, LANES - heads * blocks)))
    small = jnp.pad(packed([v[6:9, :heads] for v in packs]), ((0, 5), (0, 0)))
    step_weights = jnp.pad(
        jnp.concatenate([v[9:].reshape(heads, model) for v in packs]).astype(BF16), ((0, LANES - heads * blocks), (0, 0))
    )
    params = jnp.stack(
        [
            jnp.concatenate([v[:6], jnp.repeat(v[8, :heads], HEAD_DIM)[None], jnp.zeros((1, width), F32)], axis=0)
            for v in packs
        ]
    )
    state_taps = jnp.pad(conv_state, ((0, 3), (0, 0)))

    tok_float = padded.astype(F32)
    scale = lax.rsqrt(jnp.mean(tok_float * tok_float, axis=-1, keepdims=True) + EPS)
    normed = (tok_float * scale * norm_gain).astype(BF16)
    turned = [jnp.transpose(normed[s, PAD:]) for s in range(n)]
    turned_cotangent = [jnp.transpose(cotangent[s]) for s in range(n)]
    rows, raw, steps, log_decay, cum, state_rows, bc = project_first(
        normed, state_input_weight, step_weights, small, ids, id_rows, state_taps, row_weights[:half], blocks,
        heads * blocks,
    )
    cuts = ranges // (blocks * n)
    held = state_call(rows, bc, ids, id_rows, steps, cum, params, (), 0, half, heads, cuts)
    rows = project_more(normed, rows, row_weights[half:], half)
    acted, message = state_call(rows, bc, ids, id_rows, steps, cum, params, held, half, half, heads, cuts)
    mixed, states = inside_call(acted, bc, ids, id_rows, steps, cum, heads)
    entered = relay_back(relay_out(message, False, [mixed]), message)
    gate_weights = gathered(gate_own)
    out_weights = gathered(out_own)
    gate = project_gate(normed, gate_weights)
    entered = after(entered, gate)

    cuts = ranges // blocks
    middles, insides, closes, leaving = [], [], [], []
    ready = entered
    for s in range(n):
        middles.append(
            middle_call(s, mixed, gate, acted, cum, ready, bc, ids, tokens, cotangent, params, out_weights, heads, cuts)
        )
        ready = after(entered, middles[-1][4])
    whole_output = assembled([m[0] for m in middles])

    def inside_back(s, *others):
        d_summed = after(middles[s][3], *others)
        return inside_back_call(s, acted, d_summed, mixed, bc, ids, id_rows, steps, cum, states, entered, heads)

    def close(s, *others):
        d_scaled, d_b, d_c, d_cum = insides[s]
        return close_call(
            s, rows, acted, middles[s][3], d_scaled, bc, ids, id_rows, steps, raw, log_decay, cum, d_cum,
            after(leaving[s], *others), entered, params, small, state_rows, state_taps, d_b, d_c, heads,
        )

    for s, m in enumerate(middles):
        message = after(m[4], *leaving[-1:])
        meanwhile = [v[4] for v in middles[1:]]
        if s:
            insides.append(inside_back(s, leaving[-1]))
            meanwhile = [insides[s][3]]
        if s == n - 1:
            gate_grads = weight_grad([after(turned[0], message)] + turned[1:], [v[2] for v in middles])
            meanwhile.append(gate_grads)
        carried = relay_out(message, True, meanwhile)
        if s:
            closes.append(close(s - 1, carried))
            meanwhile = [closes[-1][0]]
        else:
            insides.append(inside_back(0, carried))
            out_grads = weight_grad(
                [after(turned_cotangent[0], carried)] + turned_cotangent[1:], [v[1] for v in middles]
            )
            meanwhile = [insides[0][3], out_grads]
        if s == n - 1:
            meanwhile.append(whole_output)
        leaving.append(after(relay_back(carried, message), *meanwhile))
    closes.append(close(n - 1))
    before = normed[:, :PAD]
    rows_grads = weight_grad(turned, [c[0] for c in closes], before)

    input_parts, edges, norm_parts = [], [], []
    gain = after(norm_gain[None], rows_grads)
    for s, (m, (d_rows, d_raw, d_state, *_)) in enumerate(zip(middles, closes)):
        input_grad, edge, halo, gain_part = input_call(
            s, m[2], d_rows, d_raw, d_state, padded, cotangent, gain, state_input_weight, step_weights,
            row_weights, gate_weights,
        )
        halo = lax.ppermute(halo, "seq", [(i + 1, i) for i in range(ranges - 1)])
        edges.append((edge + halo.astype(F32)).astype(BF16))
        input_parts.append(input_grad)
        norm_parts.append(gain_part)
    whole_input = assembled(input_parts, edges)

    plain = [normed[s, PAD:] for s in range(n)]
    out_grad = jnp.transpose(summed_weights(out_grads, False))
    heads_grad = jnp.stack([summed_weights(gate_grads, False), summed_weights(rows_grads, True)], axis=1)
    state_total, step_grads = small_grad(turned, plain, [c[2] for c in closes], [c[1] for c in closes], before)
    state_grad = summed_over(ranges_sum(state_total), "head")

    taps = sum(c[3] for c in closes)
    state_taps_grad = sum(c[4] for c in closes)
    rest = sum(c[5] for c in closes)
    gains = jnp.sum(sum(m[5] for m in middles), axis=1)
    skip_grads = jnp.sum(jnp.sum(sum(m[6] for m in middles), axis=1).reshape(blocks, heads, HEAD_DIM), axis=2)
    smalls = []
    for r in range(blocks):
        mine = slice(r * heads, (r + 1) * heads)
        head_rows = padded_lanes(jnp.concatenate([rest[:2, mine], skip_grads[r : r + 1]], axis=0), width)
        smalls.append(
            jnp.concatenate([taps[r, :5], gains[r : r + 1], head_rows, step_grads[mine].reshape(-1, width)], axis=0)
        )
    shared = jnp.concatenate([jnp.sum(sum(norm_parts), axis=0), state_taps_grad[:5].reshape(-1)])
    shared = jnp.pad(shared, (0, -shared.shape[0] % width)).reshape(-1, width)
    parts, shared = scattered(smalls, head_bits(), shared)
    own = parts[0]
    count = own.shape[0]
    both = summed_over(jnp.concatenate([own, shared], axis=0), "seq")
    own, shared = both[:count], both[count:].reshape(-1)
    return (
        whole_output,
        whole_input,
        shared[:model],
        heads_grad,
        state_grad,
        jnp.transpose(own[9:].reshape(heads, model)),
        own[:5],
        shared[model : model + 10 * LANES].reshape(5, 2 * LANES),
        own[6:9, :heads],
        own[5],
        out_grad,
    )


def solution(mesh):
    return jax.shard_map(
        shards,
        mesh=mesh,
        in_specs=(
            P(None, "seq", None),
            P(),
            P(),
            P(None, None, "head"),
            P(),
            P(None, "head"),
            P(None, "head"),
            P(),
            P(None, "head"),
            P("head"),
            P("head", None),
            P(None, "seq", None),
        ),
        out_specs=(
            P(None, "seq", None),
            P(None, "seq", None),
            P(),
            P("seq", None, "head"),
            P("seq", None),
            P(None, "head"),
            P(None, "head"),
            P(),
            P(None, "head"),
            P("head"),
            P("head", "seq"),
        ),
        check_vma=False,
    )
```

```python
import functools

import jax
import jax.numpy as jnp
from jax import lax
from jax.experimental import pallas as pl
from jax.experimental.pallas import tpu as pltpu
from jax.sharding import PartitionSpec as P

F32 = jnp.float32
BF16 = jnp.bfloat16
EPS = 1e-5
CHUNK = 128
PAD = 16
LANES = 128
HEAD_DIM = 64
VMEM = 60 * 1024 * 1024


def dot(a, b):
    return lax.dot_general(a, b, (((1,), (0,)), ((), ())), preferred_element_type=F32)


def dot_nt(a, b):
    return lax.dot_general(a, b, (((1,), (1,)), ((), ())), preferred_element_type=F32)


def dot_tn(a, b):
    return lax.dot_general(a, b, (((0,), (0,)), ((), ())), preferred_element_type=F32)


def split(value):
    high = value.astype(BF16)
    return high, (value - high.astype(F32)).astype(BF16)


def head_map(width, offset):
    lane = lax.broadcasted_iota(jnp.int32, (LANES, width), 1)
    row = lax.broadcasted_iota(jnp.int32, (LANES, width), 0)
    return (lax.shift_right_logical(lane, 6) + offset == row).astype(F32).astype(BF16)


def expand(value, width, offset):
    lane = lax.shift_right_logical(lax.broadcasted_iota(jnp.int32, value.shape, 1), 6) + offset
    return jnp.concatenate(
        [jnp.take_along_axis(value, lane + 2 * p, axis=1) for p in range(width // LANES)], axis=1
    )


def expand_row(value, width, offset):
    return expand(jnp.broadcast_to(value, (8, LANES)), width, offset)


def column(value, index):
    return jnp.take_along_axis(value, jnp.zeros(value.shape, jnp.int32) + index, axis=1)


def by_head(value, heads):
    high, low = split(value)
    return dot_nt(high, heads) + dot_nt(low, heads)


def by_head_low(value, heads):
    return dot_nt(value.astype(BF16), heads)


def widen(value, width):
    return jnp.concatenate([value] * (width // LANES), axis=1)


def fold8(value):
    return value[0:8] + value[8:16]


def sigmoid(value):
    return 0.5 * jnp.tanh(0.5 * value) + 0.5


def triangle(lower):
    row = lax.broadcasted_iota(jnp.int32, (CHUNK, CHUNK), 0)
    column = lax.broadcasted_iota(jnp.int32, (CHUNK, CHUNK), 1)
    return (row >= column if lower else row <= column)


def exact_dot(ones, value):
    return jnp.dot(ones, value, precision=lax.Precision.HIGHEST, preferred_element_type=F32)


def rows_at(start, count):
    return pl.ds(pl.multiple_of(start, 16), count)


def entering_maps(columns, rows, first, count):
    window = count + PAD
    token = lax.broadcasted_iota(jnp.int32, (count, window), 0)
    entry = lax.broadcasted_iota(jnp.int32, (count, window), 1)
    same = wide_marks(columns[0, first : first + count, :], window) == rows[0, 0:1, first - PAD : first + count]
    distance = entry - token
    return jnp.concatenate(
        [jnp.where(same & (distance == PAD - 3 + k), 1.0, 0.0).astype(BF16) for k in range(3)], axis=0
    )


def leaving_maps(columns, rows, first, count):
    window = count + PAD
    row = lax.broadcasted_iota(jnp.int32, (count, window), 0)
    token = lax.broadcasted_iota(jnp.int32, (count, window), 1)
    same = wide_marks(columns[0, first : first + count, :], window) == rows[0, 0:1, first : first + window]
    distance = token - row
    return jnp.concatenate(
        [jnp.where(same & (distance == 3 - k), 1.0, 0.0).astype(BF16) for k in range(3)], axis=0
    )


def wide_marks(columns, window):
    whole = jnp.concatenate([columns] * -(-window // LANES), axis=1)
    return whole[:, :window]


def conv_sum(rows, maps, taps, first, lanes):
    moved = dot(maps, rows[first - PAD : first + CHUNK, lanes])
    entering = [moved[k * CHUNK : (k + 1) * CHUNK] for k in range(3)]
    entering.append(rows[first : first + CHUNK, lanes].astype(F32))
    total = taps[4:5, lanes]
    for k in range(4):
        total = total + taps[k : k + 1, lanes] * entering[k]
    return total, entering


def lane_groups(width):
    step = min(width, 2 * LANES)
    return [slice(i, i + step) for i in range(0, width, step)]


def conv_forward(rows, ids, id_rows, taps, store, length):
    for c in range(length // CHUNK):
        first = PAD + c * CHUNK
        maps = entering_maps(ids, id_rows, first, CHUNK)
        for lanes in lane_groups(rows.shape[1]):
            total, _ = conv_sum(rows, maps, taps, first, lanes)
            store(slice(c * CHUNK, (c + 1) * CHUNK), lanes, (total * sigmoid(total)).astype(BF16))


def conv_backward(rows, ids, id_rows, taps, d_acted, d_pre, d_rows, length):
    width = d_pre.shape[1]
    zero = jnp.zeros((16, width), BF16)
    d_pre[0:16, :] = zero
    d_pre[length + PAD : length + PAD + 16, :] = zero
    groups = lane_groups(width)
    sums = [[jnp.zeros((8, g.stop - g.start), F32) for _ in range(5)] for g in groups]
    for c in range(length // CHUNK - 1, -1, -1):
        first = PAD + c * CHUNK
        here = slice(first, first + CHUNK)
        maps = entering_maps(ids, id_rows, first, CHUNK)
        back = leaving_maps(ids, id_rows, first, CHUNK)
        for i, lanes in enumerate(groups):
            total, entering = conv_sum(rows, maps, taps, first, lanes)
            sigma = sigmoid(total)
            grad = d_acted(c, lanes) * (sigma * (1.0 + total * (1.0 - sigma)))
            d_pre[here, lanes] = grad.astype(BF16)
            for k in range(5):
                product = grad * entering[k] if k < 4 else grad
                sums[i][k] = sums[i][k] + jnp.sum(product.reshape(CHUNK // 8, 8, -1), axis=0)
            moved = dot(back, d_pre[first : first + CHUNK + PAD, lanes])
            result = taps[3:4, lanes] * grad
            for k in range(3):
                result = result + taps[k : k + 1, lanes] * moved[k * CHUNK : (k + 1) * CHUNK]
            d_rows(here, lanes, result.astype(BF16))
    back = leaving_maps(ids, id_rows, 0, PAD)
    for lanes in groups:
        moved = dot(back, d_pre[0 : 2 * PAD, lanes])
        result = taps[0:1, lanes] * moved[0:PAD]
        for k in range(1, 3):
            result = result + taps[k : k + 1, lanes] * moved[k * PAD : (k + 1) * PAD]
        d_rows(slice(0, PAD), lanes, result.astype(BF16))
    return [
        jnp.concatenate([jnp.sum(part[k], axis=0, keepdims=True) for part in sums], axis=1) for k in range(5)
    ]


def softplus(value):
    return jnp.maximum(value, 0.0) + jnp.log1p(jnp.exp(-jnp.abs(value)))


def project_rows(values, weights, rows):
    for r, weight in enumerate(weights):
        rows[r, 0] = dot(values, weight[...]).astype(BF16)


def project_first_kernel(blocks, heads, normed, state_w, step_w, small, ids, id_rows, taps, *refs):
    weights, refs = refs[:blocks], refs[blocks:]
    rows, raw, steps, log_decay, cum, state_rows, bc = refs
    length = bc.shape[1]
    values = normed[0]
    state_rows[0] = dot(values, state_w[...]).astype(BF16)
    part = dot_nt(values[PAD:], step_w[...])
    raw[0] = part
    lane = lax.broadcasted_iota(jnp.int32, (length, LANES), 1)
    size = jnp.where(lane < heads, softplus(part + small[0:1, :]), 0.0)
    steps[0] = size
    log_decay[0] = -size * jnp.exp(small[1:2, :])
    ones = triangle(True).astype(F32)
    total = jnp.zeros((1, LANES), F32)
    for c in range(length // CHUNK):
        here = slice(c * CHUNK, (c + 1) * CHUNK)
        value = exact_dot(ones, log_decay[0, here, :]) + total
        cum[0, here, :] = value
        total = value[CHUNK - 1 : CHUNK]

    def store(here, lanes, value):
        bc[0, here, lanes] = value

    conv_forward(state_rows.at[0], ids, id_rows, taps[...], store, length)
    project_rows(values, weights, rows)


def project_more_kernel(blocks, normed, held, *refs):
    project_rows(normed[0], refs[:blocks], refs[blocks])


def project_first(normed, state_w, step_w, small, ids, id_rows, taps, weights, blocks, heads):
    n, padded, model = normed.shape
    width = weights[0].shape[1]
    length = padded - PAD
    whole = lambda a: pl.BlockSpec(a.shape, lambda s: (0,) * a.ndim, pipeline_mode=pl.Buffered(1))
    per_seq = lambda a, b: pl.BlockSpec((1, a, b), lambda s: (s, 0, 0))
    lanes = jax.ShapeDtypeStruct((n, length, LANES), F32)
    return pl.pallas_call(
        functools.partial(project_first_kernel, len(weights), heads),
        grid=(n,),
        in_specs=[
            per_seq(padded, model), whole(state_w), whole(step_w), whole(small), per_seq(*ids.shape[1:]),
            per_seq(*id_rows.shape[1:]), whole(taps),
        ] + [whole(v) for v in weights],
        out_specs=[pl.BlockSpec((len(weights), 1, padded, width), lambda s: (0, s, 0, 0))]
        + [per_seq(length, LANES)] * 4
        + [per_seq(padded, 2 * LANES), per_seq(length, 2 * LANES)],
        out_shape=[
            jax.ShapeDtypeStruct((blocks, n, padded, width), BF16), lanes, lanes, lanes, lanes,
            jax.ShapeDtypeStruct((n, padded, 2 * LANES), BF16),
            jax.ShapeDtypeStruct((n, length, 2 * LANES), BF16),
        ],
        compiler_params=pltpu.CompilerParams(vmem_limit_bytes=VMEM),
        name="project_first",
    )(normed, state_w, step_w, small, ids, id_rows, taps, *weights)


def project_more(normed, rows, weights, first):
    n, padded, model = normed.shape
    width = weights[0].shape[1]
    count = len(weights)
    return pl.pallas_call(
        functools.partial(project_more_kernel, count),
        grid=(n,),
        in_specs=[pl.BlockSpec((1, padded, model), lambda s: (s, 0, 0)), pl.BlockSpec(memory_space=pl.ANY)]
        + [pl.BlockSpec(v.shape, lambda s: (0, 0), pipeline_mode=pl.Buffered(1)) for v in weights],
        out_specs=pl.BlockSpec((count, 1, padded, width), lambda s: (first // count, s, 0, 0)),
        out_shape=jax.ShapeDtypeStruct(rows.shape, BF16),
        input_output_aliases={1: 0},
        compiler_params=pltpu.CompilerParams(vmem_limit_bytes=VMEM),
        name="project_more",
    )(normed, rows, *weights)


def project_gate_kernel(blocks, normed, *refs):
    for r in range(blocks):
        refs[blocks][r, 0] = dot(normed[0, PAD:, :], refs[r][...]).astype(BF16)


def project_gate(normed, weights):
    n, padded, model = normed.shape
    width = weights[0].shape[1]
    count = len(weights)
    return pl.pallas_call(
        functools.partial(project_gate_kernel, count),
        grid=(n,),
        in_specs=[pl.BlockSpec((1, padded, model), lambda s: (s, 0, 0))]
        + [pl.BlockSpec(v.shape, lambda s: (0, 0), pipeline_mode=pl.Buffered(1)) for v in weights],
        out_specs=pl.BlockSpec((count, 1, padded - PAD, width), lambda s: (0, s, 0, 0)),
        out_shape=jax.ShapeDtypeStruct((count, n, padded - PAD, width), BF16),
        compiler_params=pltpu.CompilerParams(vmem_limit_bytes=VMEM),
        name="project_gate",
    )(normed, *weights)


def write_message(message, state, survive):
    cuts, rows, width = message.shape
    own = rows - 16
    survive = jnp.concatenate([survive, survive], axis=0).astype(BF16)
    for i in range(cuts):
        message[i, :own, :] = state[i * own : (i + 1) * own].astype(BF16)
        message[i, own:, :] = survive


def state_kernel(first, per_block, rows, bc, ids, id_rows, steps, cum, taps, *refs):
    acted, message = refs[-2:]
    length, width = acted.shape[2:]
    offset = (pl.program_id(0) + first) * per_block

    def store(here, lanes, value):
        acted[0, 0, here, lanes] = value

    conv_forward(rows.at[0, 0], ids, id_rows, taps[0], store, length)
    total = cum[0, length - 1 : length, :]
    last = ids[0, PAD + length - 1 : PAD + length, :]
    before = ids[0, PAD - 1 : PAD, :]
    state = jnp.zeros((LANES, width), F32)
    for c in range(length // CHUNK):
        here = slice(c * CHUNK, (c + 1) * CHUNK)
        same = (ids[0, PAD + c * CHUNK : PAD + (c + 1) * CHUNK, :] == last).astype(F32)
        tail = jnp.exp(total - cum[0, here, :]) * same * steps[0, here, :]
        scaled = (expand(tail, width, offset) * acted[0, 0, here, :].astype(F32)).astype(BF16)
        state = state + dot_tn(bc[0, here, :LANES], scaled)
    survive = jnp.exp(total) * (last == before).astype(F32)
    write_message(message.at[0, 0], state, expand_row(survive, width, offset))


def state_call(rows, bc, ids, id_rows, steps, cum, taps, held, first, count, per_block, cuts):
    blocks, n, padded, width = rows.shape
    length = padded - PAD
    four = lambda a, b: pl.BlockSpec((1, 1, a, b), lambda g, s: (g + first, s, 0, 0))
    per_seq = lambda a: pl.BlockSpec((1,) + a.shape[1:], lambda g, s: (s, 0, 0))
    piece = LANES // cuts + 16
    return pl.pallas_call(
        functools.partial(state_kernel, first, per_block),
        grid=(count, n),
        in_specs=[
            four(padded, width), per_seq(bc), per_seq(ids), per_seq(id_rows), per_seq(steps), per_seq(cum),
            pl.BlockSpec((1,) + taps.shape[1:], lambda g, s: (g + first, 0, 0)),
        ] + [pl.BlockSpec(memory_space=pl.ANY) for _ in held],
        out_specs=[
            four(length, width),
            pl.BlockSpec((1, 1, cuts, piece, width), lambda g, s: (g + first, s, 0, 0, 0)),
        ],
        out_shape=[
            jax.ShapeDtypeStruct((blocks, n, length, width), BF16),
            jax.ShapeDtypeStruct((blocks, n, cuts, piece, width), BF16),
        ],
        input_output_aliases={7: 0, 8: 1} if held else {},
        compiler_params=pltpu.CompilerParams(vmem_limit_bytes=VMEM),
        name="range_state",
    )(rows, bc, ids, id_rows, steps, cum, taps, *held)


def chunk_marks(ids, c):
    first = PAD + c * CHUNK
    return ids[0, first : first + CHUNK, :], ids[0, first + CHUNK - 1 : first + CHUNK, :], ids[0, first - 1 : first, :]


def chunk_decays(ids, cum, c):
    here, last, before = chunk_marks(ids, c)
    value = cum[0, c * CHUNK : (c + 1) * CHUNK, :]
    base = cum[0, c * CHUNK - 1 : c * CHUNK, :] if c else jnp.zeros((1, LANES), F32)
    end = value[CHUNK - 1 : CHUNK]
    entering = jnp.exp(value - base) * (here == before).astype(F32)
    tail = jnp.exp(end - value) * (here == last).astype(F32)
    survive = jnp.exp(end - base) * (last == before).astype(F32)
    return entering, tail, survive


def lane_halves(pair):
    lane = lax.broadcasted_iota(jnp.int32, pair.shape, 1)
    zero = jnp.zeros_like(pair)
    return jnp.concatenate([jnp.where(lane < HEAD_DIM, pair, zero), jnp.where(lane < HEAD_DIM, zero, pair)], axis=0)


def inside_kernel(per_block, acted, bc, ids, id_rows, steps, cum, mixed, states, carried, turned):
    length, width = acted.shape[2:]
    offset = pl.program_id(1) * per_block
    later = triangle(True)
    for c in range(length // CHUNK):
        here = slice(c * CHUNK, (c + 1) * CHUNK)
        b_part, c_part = bc[0, here, :LANES], bc[0, here, LANES:]
        marks, _, _ = chunk_marks(ids, c)
        same = later & (marks == id_rows[0, 0:1, PAD + c * CHUNK : PAD + (c + 1) * CHUNK])
        scores = jnp.where(same, dot_nt(c_part, b_part), 0.0)
        value = cum[0, here, :]
        turned[...] = jnp.transpose(value)
        entering, tail, survive = chunk_decays(ids, cum, c)
        scaled = (expand(steps[0, here, :], width, offset) * acted[0, 0, here, :].astype(F32)).astype(BF16)
        if c:
            held = carried[...]
            held_low = held.astype(BF16)
            states[0, 0, c - 1] = held_low
            outside = dot(c_part, held_low) * expand(entering, width, offset)
        for pair in range(width // LANES):
            lanes = slice(pair * LANES, (pair + 1) * LANES)
            mixing = []
            for h in (2 * pair, 2 * pair + 1):
                spread = jnp.minimum(column(value, offset + h) - turned[pl.ds(offset + h, 1), :], 0.0)
                mixing.append((scores * jnp.exp(spread)).astype(BF16))
            result = dot(jnp.concatenate(mixing, axis=1), lane_halves(scaled[:, lanes]))
            mixed[0, 0, here, lanes] = result + outside[:, lanes] if c else result
        if c + 1 < length // CHUNK:
            fresh = dot_tn(b_part, (expand(tail, width, offset) * scaled.astype(F32)).astype(BF16))
            if c:
                fresh = fresh + held * expand_row(survive, width, offset)[0:1]
            carried[...] = fresh


def inside_call(acted, bc, ids, id_rows, steps, cum, per_block):
    blocks, n, length, width = acted.shape
    chunks = length // CHUNK
    four = lambda a, b: pl.BlockSpec((1, 1, a, b), lambda s, g: (g, s, 0, 0))
    per_seq = lambda a: pl.BlockSpec((1,) + a.shape[1:], lambda s, g: (s, 0, 0))
    return pl.pallas_call(
        functools.partial(inside_kernel, per_block),
        grid=(n, blocks),
        in_specs=[four(length, width), per_seq(bc), per_seq(ids), per_seq(id_rows), per_seq(steps), per_seq(cum)],
        out_specs=[
            four(length, width),
            pl.BlockSpec((1, 1, chunks - 1, LANES, width), lambda s, g: (g, s, 0, 0, 0)),
        ],
        out_shape=[
            jax.ShapeDtypeStruct((blocks, n, length, width), F32),
            jax.ShapeDtypeStruct((blocks, n, chunks - 1, LANES, width), BF16),
        ],
        scratch_shapes=[pltpu.VMEM((LANES, width), F32), pltpu.VMEM((LANES, LANES), F32)],
        compiler_params=pltpu.CompilerParams(vmem_limit_bytes=VMEM),
        name="inside",
    )(acted, bc, ids, id_rows, steps, cum)


def relay_kernel(backward, message, carried):
    ranges, rows, width = carried.shape
    state = jnp.zeros((rows, width), F32)
    order = range(ranges - 1, -1, -1) if backward else range(ranges)
    for q in order:
        carried[q] = state.astype(BF16)
        decay = message[q, rows : rows + 1, :].astype(F32)
        state = state * decay + message[q, :rows, :].astype(F32)


class Values(dict):
    def meet(self, *names):
        names = [name for name in names if name in self]
        self.update(zip(names, lax.optimization_barrier(tuple(self[name] for name in names))))


def over_ranges(value):
    return lax.all_to_all(value, "seq", 0, 0, tiled=True)


def send_message(message):
    return over_ranges(message.reshape(lax.axis_size("seq"), message.shape[3], message.shape[4]))


def relay(arrived, backward):
    ranges, rows, width = arrived.shape
    return pl.pallas_call(
        functools.partial(relay_kernel, backward),
        out_shape=jax.ShapeDtypeStruct((ranges, rows - 16, width), BF16),
        compiler_params=pltpu.CompilerParams(vmem_limit_bytes=VMEM),
        name="relay",
    )(arrived)


def send_back(carried, blocks, n):
    return over_ranges(carried).reshape(blocks, n, LANES, carried.shape[2])


def middle_kernel(
    blocks, per_block, total_width, mixed, gate, acted, cum, cum_end, bc, ids, ids_before, ids_after, tokens, cotangent,
    params, entered, *refs
):
    weights, refs = refs[:blocks], refs[blocks:]
    output, normed_out, d_gate, d_summed, pulled, gain_grad, skip_grad = refs[:7]
    summed_s, gated_s, grad_s, first_s, second_s, low_s, row_s, pull_s = refs[7:]
    tile, width = mixed.shape[2:]
    t = pl.program_id(0)
    before = ids_before[0, PAD - 1 : PAD, :]
    marks = ids[0]
    c_part = bc[0, :, LANES:]
    slabs = tile // 16
    same = (marks == before).astype(F32)
    decay = jnp.exp(cum[0]) * same
    row_s[...] = jnp.zeros_like(row_s)

    def lanes_sum(value):
        total = value[:, :LANES]
        for i in range(1, width // LANES):
            total = total + value[:, i * LANES : (i + 1) * LANES]
        return total

    @pl.when(t == 0)
    def _():
        gain_grad[...] = jnp.zeros_like(gain_grad)
        skip_grad[...] = jnp.zeros_like(skip_grad)
        pull_s[...] = jnp.zeros_like(pull_s)

    for r in range(blocks):
        first_s[...] = dot(c_part, entered[r, 0])
        second_s[r] = expand(decay, width, r * per_block)
        skip = params[r, 6:7, :]

        def step(i, carry, r=r, skip=skip):
            here = rows_at(i * 16, 16)
            value = mixed[r, 0, here, :] + first_s[here, :] * second_s[r, here, :]
            summed = value + skip * acted[r, 0, here, :].astype(F32)
            g = gate[r, 0, here, :].astype(F32)
            gated = summed * (g * sigmoid(g))
            summed_s[r, here, :] = summed
            gated_s[r, here, :] = gated
            row_s[here, :] = row_s[here, :] + lanes_sum(gated * gated)
            return carry

        lax.fori_loop(0, slabs, step, 0, unroll=4)
    squares = jnp.sum(row_s[...], axis=1, keepdims=True)
    rescale = jnp.broadcast_to(lax.rsqrt(squares / total_width + EPS), (tile, LANES))
    row_s[...] = rescale
    for r in range(blocks):
        gain = params[r, 5:6, :]

        def step(i, carry, r=r, gain=gain):
            here = rows_at(i * 16, 16)
            normed_out[r, 0, here, :] = (gated_s[r, here, :] * widen(row_s[here, :], width) * gain).astype(BF16)
            return carry

        lax.fori_loop(0, slabs, step, 0, unroll=4)
    branch = tokens[0].astype(F32)
    for r in range(blocks):
        branch = branch + dot(normed_out[r, 0], weights[r][...])
    output[0] = branch.astype(BF16)
    first_s[:, :LANES] = jnp.zeros((tile, LANES), F32)
    for r in range(blocks):
        grad_s[r] = dot_nt(cotangent[0], weights[r][...])
        gain = params[r, 5:6, :]

        def step(i, total, r=r, gain=gain):
            here = rows_at(i * 16, 16)
            both = grad_s[r, here, :] * gated_s[r, here, :]
            first_s[here, :LANES] = first_s[here, :LANES] + lanes_sum(both * gain)
            return total + fold8(both * widen(row_s[here, :], width))

        gain_grad[r] = gain_grad[r] + lax.fori_loop(0, slabs, step, jnp.zeros((8, width), F32), unroll=4)
    cross = jnp.sum(first_s[:, :LANES], axis=1, keepdims=True) / total_width
    first_s[:, :LANES] = rescale * rescale * rescale * cross
    for r in range(blocks):
        gain = params[r, 5:6, :]

        def step(i, total, r=r, gain=gain):
            here = rows_at(i * 16, 16)
            g = gate[r, 0, here, :].astype(F32)
            sigma = sigmoid(g)
            d_gated = widen(row_s[here, :], width) * (grad_s[r, here, :] * gain) - gated_s[r, here, :] * widen(
                first_s[here, :LANES], width
            )
            d_sum = d_gated * (g * sigma)
            d_gate[r, 0, here, :] = (d_gated * summed_s[r, here, :] * (sigma * (1.0 + g * (1.0 - sigma)))).astype(BF16)
            low = d_sum.astype(BF16)
            d_summed[r, 0, here, :] = low
            low_s[here, :] = (d_sum * second_s[r, here, :]).astype(BF16)
            return total + fold8(d_sum * acted[r, 0, here, :].astype(F32))

        skip_grad[r] = skip_grad[r] + lax.fori_loop(0, slabs, step, jnp.zeros((8, width), F32), unroll=4)
        pull_s[r] = pull_s[r] + dot_tn(c_part, low_s[...])

    @pl.when(t == pl.num_programs(0) - 1)
    def _():
        survive = jnp.exp(cum_end[0, 7:8, :]) * (ids_after[0, PAD - 1 : PAD, :] == before).astype(F32)
        for r in range(blocks):
            write_message(pulled.at[r, 0], pull_s[r], expand_row(survive, width, r * per_block))


def middle_call(s, mixed, gate, acted, cum, entered, bc, ids, tokens, cotangent, params, weights, per_block, cuts):
    blocks, n, length, width = mixed.shape
    model = tokens.shape[2]
    tile = min(256, length)
    wide = lambda w: pl.BlockSpec((blocks, 1, tile, w), lambda t: (0, s, t, 0))
    wide_out = lambda w: pl.BlockSpec((blocks, 1, tile, w), lambda t: (0, 0, t, 0))
    rows = lambda w: pl.BlockSpec((1, tile, w), lambda t: (s, t, 0))
    one = lambda a: pl.BlockSpec((a.shape[0], 1) + a.shape[2:], lambda t: (0, s, 0, 0), pipeline_mode=pl.Buffered(1))
    whole = lambda a: pl.BlockSpec(a.shape, lambda t: (0,) * a.ndim, pipeline_mode=pl.Buffered(1))
    kept = lambda *shape: pl.BlockSpec(shape, lambda t: (0,) * len(shape))
    piece = LANES // cuts + 16
    edge = lambda a: pl.BlockSpec((1, PAD, LANES), lambda t: (s, a, 0))
    ids_here = ids[:, PAD : PAD + length]
    wide_shape = jax.ShapeDtypeStruct((blocks, 1, length, width), BF16)
    return pl.pallas_call(
        functools.partial(middle_kernel, blocks, per_block, width * blocks),
        grid=(length // tile,),
        in_specs=[
            wide(width), wide(width), wide(width), rows(LANES),
            pl.BlockSpec((1, 8, LANES), lambda t: (s, length // 8 - 1, 0)), rows(2 * LANES), rows(LANES),
            edge(0), edge(length // PAD), rows(model), rows(model), whole(params),
            one(entered),
        ] + [whole(v) for v in weights],
        out_specs=[
            pl.BlockSpec((1, tile, model), lambda t: (0, t, 0)), wide_out(width), wide_out(width), wide_out(width),
            kept(blocks, 1, cuts, piece, width), kept(blocks, 8, width), kept(blocks, 8, width),
        ],
        out_shape=[
            jax.ShapeDtypeStruct((1, length, model), BF16),
            wide_shape, wide_shape, wide_shape,
            jax.ShapeDtypeStruct((blocks, 1, cuts, piece, width), BF16),
            jax.ShapeDtypeStruct((blocks, 8, width), F32),
            jax.ShapeDtypeStruct((blocks, 8, width), F32),
        ],
        scratch_shapes=[
            pltpu.VMEM((blocks, tile, width), F32),
            pltpu.VMEM((blocks, tile, width), F32),
            pltpu.VMEM((blocks, tile, width), F32),
            pltpu.VMEM((tile, width), F32),
            pltpu.VMEM((blocks, tile, width), F32),
            pltpu.VMEM((tile, width), BF16),
            pltpu.VMEM((tile, LANES), F32),
            pltpu.VMEM((blocks, LANES, width), F32),
        ],
        compiler_params=pltpu.CompilerParams(vmem_limit_bytes=VMEM),
        name="middle",
    )(mixed, gate, acted, cum, cum, bc, ids_here, ids, ids, tokens, cotangent, params, entered, *weights)


def inside_back_kernel(
    per_block, acted, d_summed, mixed, bc, ids, id_rows, steps, cum, states, entered, d_scaled, d_b, d_c, d_cum,
    carried, turned,
):
    length, width = acted.shape[2:]
    chunks = length // CHUNK
    g = pl.program_id(0)
    offset = g * per_block
    heads = head_map(width, offset)
    sooner = triangle(False)
    first_before = ids[0, PAD - 1 : PAD, :]
    came = entered[0, 0]

    @pl.when(g == 0)
    def _():
        d_b[...] = jnp.zeros_like(d_b)
        d_c[...] = jnp.zeros_like(d_c)
        d_cum[...] = jnp.zeros_like(d_cum)

    for c in range(chunks - 1, -1, -1):
        here = slice(c * CHUNK, (c + 1) * CHUNK)
        b_part, c_part = bc[0, here, :LANES], bc[0, here, LANES:]
        marks, _, _ = chunk_marks(ids, c)
        same = sooner & (marks == id_rows[0, 0:1, PAD + c * CHUNK : PAD + (c + 1) * CHUNK])
        scores_t = jnp.where(same, dot_nt(b_part, c_part), 0.0)
        value = cum[0, here, :]
        turned[...] = jnp.transpose(value)
        entering, tail, survive = chunk_decays(ids, cum, c)
        scaled = (expand(steps[0, here, :], width, offset) * acted[0, 0, here, :].astype(F32)).astype(BF16)
        grad = d_summed[0, 0, here, :]
        grad_wide = grad.astype(F32)
        from_start = jnp.exp(value) * (marks == first_before).astype(F32)
        start_wide = expand(from_start, width, offset)
        d_c_part = dot_nt((grad_wide * start_wide).astype(BF16), came)
        dots = grad_wide * (mixed[0, 0, here, :] + start_wide * dot(c_part, came))
        if c < chunks - 1:
            held = carried[...]
            held_low = held.astype(BF16)
            tail_wide = expand(tail, width, offset)
            later = dot(b_part, held_low) * tail_wide
            d_b_part = dot_nt((tail_wide * scaled.astype(F32)).astype(BF16), held_low)
        if c:
            entering_grad = (expand(entering, width, offset) * grad_wide).astype(BF16)
            d_c_part = d_c_part + dot_nt(entering_grad, states[0, 0, c - 1])
        d_scores_t = jnp.zeros((CHUNK, CHUNK), F32)
        results = []
        for pair in range(width // LANES):
            lanes = slice(pair * LANES, (pair + 1) * LANES)
            products = dot_nt(lane_halves(scaled[:, lanes]), grad[:, lanes])
            mixing = []
            for half, h in enumerate((2 * pair, 2 * pair + 1)):
                spread = jnp.minimum(turned[pl.ds(offset + h, 1), :] - column(value, offset + h), 0.0)
                decay = jnp.exp(spread)
                mixing.append((scores_t * decay).astype(BF16))
                d_scores_t = d_scores_t + products[half * CHUNK : (half + 1) * CHUNK] * decay
            results.append(dot(jnp.concatenate(mixing, axis=1), lane_halves(grad[:, lanes])))
        result = jnp.concatenate(results, axis=1)
        if c < chunks - 1:
            result = result + later
        d_scaled[0, 0, here, :] = result.astype(BF16)
        d_cum[0, here, :] = d_cum[0, here, :] + by_head(dots - scaled.astype(F32) * result, heads)
        d_scores_t = jnp.where(same, d_scores_t, 0.0).astype(BF16)
        d_b_here = dot(d_scores_t, c_part)
        if c < chunks - 1:
            d_b_here = d_b_here + d_b_part
        d_b[0, here, :] = d_b[0, here, :] + d_b_here
        d_c[0, here, :] = d_c[0, here, :] + d_c_part + dot_tn(d_scores_t, b_part)
        if c:
            pulled = dot_tn(c_part, entering_grad)
            if c < chunks - 1:
                pulled = pulled + held * expand_row(survive, width, offset)[0:1]
            carried[...] = pulled


def inside_back_call(s, acted, d_summed, mixed, bc, ids, id_rows, steps, cum, states, entered, per_block):
    blocks, n, length, width = acted.shape
    four = lambda a, b: pl.BlockSpec((1, 1, a, b), lambda g: (g, s, 0, 0))
    own = lambda a, b: pl.BlockSpec((1, 1, a, b), lambda g: (g, 0, 0, 0))
    per_seq = lambda a: pl.BlockSpec((1,) + a.shape[1:], lambda g: (s, 0, 0))
    summed = pl.BlockSpec((1, length, LANES), lambda g: (0, 0, 0))
    lanes = jax.ShapeDtypeStruct((1, length, LANES), F32)
    return pl.pallas_call(
        functools.partial(inside_back_kernel, per_block),
        grid=(blocks,),
        in_specs=[
            four(length, width), own(length, width), four(length, width), per_seq(bc), per_seq(ids), per_seq(id_rows),
            per_seq(steps), per_seq(cum),
            pl.BlockSpec((1, 1) + states.shape[2:], lambda g: (g, s, 0, 0, 0)),
            four(LANES, width),
        ],
        out_specs=[own(length, width), summed, summed, summed],
        out_shape=[jax.ShapeDtypeStruct((blocks, 1, length, width), BF16), lanes, lanes, lanes],
        scratch_shapes=[pltpu.VMEM((LANES, width), F32), pltpu.VMEM((LANES, LANES), F32)],
        compiler_params=pltpu.CompilerParams(vmem_limit_bytes=VMEM),
        name="inside_back",
    )(acted, d_summed, mixed, bc, ids, id_rows, steps, cum, states, entered)


def close_kernel(
    per_block, rows, acted, d_summed, d_scaled, bc, ids, id_rows, steps, raw, log_decay, cum, d_cum, leaving, entered,
    params, small, state_rows, state_taps, d_b, d_c,
    d_rows, d_raw, d_state, taps_grad, state_taps_grad, small_grad, d_pre, d_acted, d_log, d_step, ends, d_bc, d_pre_bc,
):
    length, width = acted.shape[2:]
    chunks = length // CHUNK
    g = pl.program_id(0)
    offset = g * per_block
    heads = head_map(width, offset)
    last = ids[0, PAD + length - 1 : PAD + length, :]
    before = ids[0, PAD - 1 : PAD, :]
    end = cum[0, length - 1 : length, :]
    skip = params[0, 6:7, :]
    held = leaving[0, 0]
    came = entered[0, 0]

    @pl.when(g == 0)
    def _():
        d_bc[:, :LANES] = d_b[0]
        d_bc[:, LANES:] = d_c[0]
        d_log[...] = d_cum[0]
        d_step[...] = jnp.zeros_like(d_step)
        ends[...] = jnp.zeros_like(ends)

    boundary = jnp.zeros((1, LANES), F32)
    for c in range(chunks):
        here = slice(c * CHUNK, (c + 1) * CHUNK)
        marks, _, _ = chunk_marks(ids, c)
        tail = jnp.exp(end - cum[0, here, :]) * (marks == last).astype(F32)
        tail_wide = expand(tail, width, offset)
        steps_wide = expand(steps[0, here, :], width, offset)
        x = acted[0, 0, here, :].astype(F32)
        scaled = (steps_wide * x).astype(BF16).astype(F32)
        later = dot(bc[0, here, :LANES], held) * tail_wide
        total = d_scaled[0, 0, here, :].astype(F32) + later
        d_acted[here, :] = steps_wide * total + skip * d_summed[0, 0, here, :].astype(F32)
        d_bc[here, :LANES] = d_bc[here, :LANES] + dot_nt((tail_wide * scaled).astype(BF16), held)
        from_later = by_head_low(scaled * later, heads)
        boundary = boundary + jnp.sum(from_later, axis=0, keepdims=True)
        d_log[here, :] = d_log[here, :] - from_later
        d_step[here, :] = d_step[here, :] + by_head_low(x * total, heads)
    product = held.astype(F32) * came.astype(F32)
    product = jnp.sum(product.reshape(LANES // 8, 8, width), axis=0)
    survive = jnp.exp(end) * (last == before).astype(F32)
    boundary = boundary + survive * jnp.sum(by_head(jnp.concatenate([product, product * 0.0], axis=0), heads), axis=0, keepdims=True)
    ends[0:1, :] = ends[0:1, :] + boundary

    def store(here, lanes, value):
        d_rows[0, 0, here, lanes] = value

    sums = conv_backward(
        rows.at[0, 0],
        ids,
        id_rows,
        params[0],
        lambda c, lanes: d_acted[c * CHUNK : (c + 1) * CHUNK, lanes],
        d_pre,
        store,
        length,
    )
    taps_grad[0] = jnp.concatenate(sums + [jnp.zeros((3, width), F32)], axis=0)

    @pl.when(g == pl.num_programs(0) - 1)
    def _():
        rate = jnp.exp(small[1:2, :])
        ones = triangle(False).astype(F32)
        carry = ends[0:1, :]
        decay_sum = jnp.zeros((1, LANES), F32)
        bias_sum = jnp.zeros((1, LANES), F32)
        for c in range(chunks - 1, -1, -1):
            here = slice(c * CHUNK, (c + 1) * CHUNK)
            grads = exact_dot(ones, d_log[here, :]) + carry
            carry = grads[0:1]
            decay_sum = decay_sum + jnp.sum(grads * log_decay[0, here, :], axis=0, keepdims=True)
            value = (d_step[here, :] - grads * rate) * sigmoid(raw[0, here, :] + small[0:1, :])
            bias_sum = bias_sum + jnp.sum(value, axis=0, keepdims=True)
            d_raw[0, here, :] = value.astype(BF16)
        small_grad[...] = jnp.concatenate([bias_sum, decay_sum, jnp.zeros((6, LANES), F32)], axis=0)

        def store_state(here, lanes, value):
            d_state[0, here, lanes] = value

        sums = conv_backward(
            state_rows.at[0],
            ids,
            id_rows,
            state_taps[...],
            lambda c, lanes: d_bc[c * CHUNK : (c + 1) * CHUNK, lanes],
            d_pre_bc,
            store_state,
            length,
        )
        state_taps_grad[...] = jnp.concatenate(sums + [jnp.zeros((3, 2 * LANES), F32)], axis=0)


def close_call(
    s, rows, acted, d_summed, d_scaled, bc, ids, id_rows, steps, raw, log_decay, cum, d_cum, leaving, entered, params,
    small, state_rows, state_taps, d_b, d_c, per_block,
):
    blocks, n, length, width = acted.shape
    four = lambda a, b: pl.BlockSpec((1, 1, a, b), lambda g: (g, s, 0, 0))
    own = lambda a, b: pl.BlockSpec((1, 1, a, b), lambda g: (g, 0, 0, 0))
    per_seq = lambda a: pl.BlockSpec((1,) + a.shape[1:], lambda g: (s, 0, 0))
    kept = lambda *shape: pl.BlockSpec(shape, lambda g: (0,) * len(shape))
    whole = lambda a: kept(*a.shape)
    wide = own(length, width)
    return pl.pallas_call(
        functools.partial(close_kernel, per_block),
        grid=(blocks,),
        in_specs=[
            four(length + PAD, width), four(length, width), wide, wide, per_seq(bc), per_seq(ids), per_seq(id_rows),
            per_seq(steps), per_seq(raw), per_seq(log_decay), per_seq(cum), kept(1, length, LANES), own(LANES, width),
            four(LANES, width),
            pl.BlockSpec((1,) + params.shape[1:], lambda g: (g, 0, 0)), whole(small), per_seq(state_rows),
            whole(state_taps), whole(d_b), whole(d_c),
        ],
        out_specs=[
            own(length + PAD, width), kept(1, length, LANES), kept(1, length + PAD, 2 * LANES),
            pl.BlockSpec((1, 8, width), lambda g: (g, 0, 0)), kept(8, 2 * LANES), kept(8, LANES),
        ],
        out_shape=[
            jax.ShapeDtypeStruct((blocks, 1, length + PAD, width), BF16),
            jax.ShapeDtypeStruct((1, length, LANES), BF16),
            jax.ShapeDtypeStruct((1, length + PAD, 2 * LANES), BF16),
            jax.ShapeDtypeStruct((blocks, 8, width), F32),
            jax.ShapeDtypeStruct((8, 2 * LANES), F32),
            jax.ShapeDtypeStruct((8, LANES), F32),
        ],
        scratch_shapes=[
            pltpu.VMEM((length + 2 * PAD, width), BF16),
            pltpu.VMEM((length, width), F32),
            pltpu.VMEM((length, LANES), F32),
            pltpu.VMEM((length, LANES), F32),
            pltpu.VMEM((8, LANES), F32),
            pltpu.VMEM((length, 2 * LANES), F32),
            pltpu.VMEM((length + 2 * PAD, 2 * LANES), BF16),
        ],
        compiler_params=pltpu.CompilerParams(vmem_limit_bytes=VMEM),
        name="close",
    )(
        rows, acted, d_summed, d_scaled, bc, ids, id_rows, steps, raw, log_decay, cum, d_cum, leaving, entered, params,
        small, state_rows, state_taps, d_b, d_c,
    )


def input_kernel(blocks, d_gate, d_rows, d_raw, d_state, tokens, cotangent, gain, state_w, step_w, *refs):
    row_weights, refs = refs[:blocks], refs[blocks:]
    gate_weights, refs = refs[:blocks], refs[blocks:]
    input_grad, edge, halo, gain_grad, main_s, halo_s = refs
    length = d_gate.shape[2]
    total = dot_nt(d_state[0], state_w[...])
    halo_s[...] = total[:PAD]
    main_s[...] = total[PAD:] + dot(d_raw[0], step_w[...])
    for r in range(blocks):
        halo_s[...] = halo_s[...] + dot_nt(d_rows[r, 0, :PAD, :], row_weights[r][...])
        main_s[...] = main_s[...] + (
            dot_nt(d_rows[r, 0, PAD:, :], row_weights[r][...]) + dot_nt(d_gate[r, 0], gate_weights[r][...])
        )

    def norm_back(value, token):
        scale = lax.rsqrt(jnp.mean(token * token, axis=1, keepdims=True) + EPS)
        unit = value * gain[...]
        inner = jnp.mean(unit * token, axis=1, keepdims=True)
        return scale * unit - token * (scale * scale * scale * inner), fold8(value * token * scale)

    grad, sums = norm_back(halo_s[...], tokens[0, :PAD, :].astype(F32))
    halo[0] = grad.astype(BF16)

    def step(i, carry):
        here = rows_at(i * 16, 16)
        grad, more = norm_back(main_s[here, :], tokens[0, rows_at(PAD + i * 16, 16), :].astype(F32))
        value = grad + cotangent[0, here, :].astype(F32)
        edge[0] = value
        input_grad[0, here, :] = value.astype(BF16)
        return carry + more

    gain_grad[...] = lax.fori_loop(0, length // 16, step, sums, unroll=4)


def input_call(s, d_gate, d_rows, d_raw, d_state, tokens, cotangent, gain, state_w, step_w, row_weights, gate_weights):
    blocks, _, length, width = d_gate.shape
    padded, model = tokens.shape[1:]
    whole = lambda a: pl.BlockSpec(a.shape, lambda t: (0,) * a.ndim, pipeline_mode=pl.Buffered(1))
    one = lambda a, b: pl.BlockSpec((1, a, b), lambda t: (s, 0, 0), pipeline_mode=pl.Buffered(1))
    kept = lambda *shape: pl.BlockSpec(shape, lambda t: (0,) * len(shape), pipeline_mode=pl.Buffered(1))
    return pl.pallas_call(
        functools.partial(input_kernel, blocks),
        grid=(1,),
        in_specs=[
            whole(d_gate), whole(d_rows), whole(d_raw), whole(d_state), one(padded, model), one(length, model),
            whole(gain), whole(state_w), whole(step_w),
        ] + [whole(v) for v in row_weights] + [whole(v) for v in gate_weights],
        out_specs=[kept(1, length, model), kept(1, PAD, model), kept(1, PAD, model), kept(8, model)],
        out_shape=[
            jax.ShapeDtypeStruct((1, length, model), BF16),
            jax.ShapeDtypeStruct((1, PAD, model), F32),
            jax.ShapeDtypeStruct((1, PAD, model), BF16),
            jax.ShapeDtypeStruct((8, model), F32),
        ],
        scratch_shapes=[pltpu.VMEM((length, model), F32), pltpu.VMEM((PAD, model), F32)],
        compiler_params=pltpu.CompilerParams(vmem_limit_bytes=VMEM),
        name="input_gradient",
    )(d_gate, d_rows, d_raw, d_state, tokens, cotangent, gain, state_w, step_w, *row_weights, *gate_weights)


def assemble_kernel(count, places, *refs):
    parts, refs = refs[:count], refs[count:]
    edges, refs = (refs[:count], refs[count:]) if len(refs) > 2 * count else ((), refs)
    whole, buffers, (in_sem, out_sem) = refs[0], refs[1:-2], refs[-2:]
    length = parts[0].shape[1]
    reads = [pltpu.make_async_copy(p.at[0], b, in_sem.at[i]) for i, (p, b) in enumerate(zip(parts, buffers))]
    writes = [pltpu.make_async_copy(b, whole.at[places[i]], out_sem.at[i]) for i, b in enumerate(buffers)]
    for read in reads:
        read.start()
    for i, (read, write) in enumerate(zip(reads, writes)):
        read.wait()
        if edges:
            buffers[i][length - PAD :, :] = edges[i][0]
        write.start()
    for write in writes:
        write.wait()


def assemble(parts, edges, places):
    count = len(parts)
    _, length, model = parts[0].shape
    return pl.pallas_call(
        functools.partial(assemble_kernel, count),
        grid_spec=pltpu.PrefetchScalarGridSpec(
            num_scalar_prefetch=1,
            grid=(1,),
            in_specs=[pl.BlockSpec(memory_space=pl.ANY) for _ in parts]
            + [pl.BlockSpec((1, PAD, model), lambda t, i: (0, 0, 0)) for _ in edges],
            out_specs=pl.BlockSpec(memory_space=pl.ANY),
            scratch_shapes=[pltpu.VMEM((length, model), BF16) for _ in parts]
            + [pltpu.SemaphoreType.DMA((count,)), pltpu.SemaphoreType.DMA((count,))],
        ),
        out_shape=jax.ShapeDtypeStruct((count, length, model), BF16),
        compiler_params=pltpu.CompilerParams(vmem_limit_bytes=VMEM),
        name="assemble",
    )(jnp.stack(places).astype(jnp.int32), *parts, *edges)


def weight_grad_kernel(n, skip, values, *refs):
    grads, (kept, sent) = refs[:n], refs[n:]
    odd = pl.program_id(0) % 2 == 1
    total = dot_tn(values[0, skip:, :], grads[0][0, 0])
    for s in range(1, n):
        total = total + dot_tn(values[s, skip:, :], grads[s][0, 0])
    total = total.astype(BF16)

    @pl.when(odd)
    def _():
        sent[0] = total

    @pl.when(jnp.logical_not(odd))
    def _():
        kept[0] = total


def weight_grad(values, grads):
    n, padded, model = values.shape
    blocks, _, tokens, width = grads[0].shape
    return pl.pallas_call(
        functools.partial(weight_grad_kernel, n, padded - tokens),
        grid=(blocks,),
        in_specs=[pl.BlockSpec(values.shape, lambda g: (0, 0, 0), pipeline_mode=pl.Buffered(1))]
        + [pl.BlockSpec((1, 1, tokens, width), lambda g: (g, 0, 0, 0)) for _ in grads],
        out_specs=[pl.BlockSpec((1, model, width), lambda g: (g // 2, 0, 0))] * 2,
        out_shape=[jax.ShapeDtypeStruct((blocks // 2, model, width), BF16)] * 2,
        compiler_params=pltpu.CompilerParams(vmem_limit_bytes=VMEM),
        name="weight_gradient",
    )(values, *grads)


def state_grad_kernel(n, values, *refs):
    states, (out,) = refs[:n], refs[n:]
    total = dot_tn(values[0], states[0][0])
    for s in range(1, n):
        total = total + dot_tn(values[s], states[s][0])
    out[...] = total.astype(BF16)


def state_grad(values, states):
    return pl.pallas_call(
        functools.partial(state_grad_kernel, len(states)),
        out_shape=jax.ShapeDtypeStruct((values.shape[2], states[0].shape[2]), BF16),
        compiler_params=pltpu.CompilerParams(vmem_limit_bytes=VMEM),
        name="state_weight_gradient",
    )(values, *states)


def pack_kernel(n, per_block, values, *refs):
    groups, outs = [refs[i * n : (i + 1) * n] for i in range(7)], refs[7 * n :]
    steps, taps, state_taps, rest, gains, skips, norms = groups
    add = lambda refs, *at: functools.reduce(lambda a, b: a + b, [ref[at] for ref in refs])
    column_sum = lambda value: jnp.sum(value, axis=0, keepdims=True)
    step = dot_tn(steps[0][0], values[0, PAD:, :])
    for s in range(1, n):
        step = step + dot_tn(steps[s][0], values[s, PAD:, :])
    model = step.shape[1]
    width = outs[0].shape[1]
    norm = column_sum(add(norms, Ellipsis))
    rest = add(rest, Ellipsis)
    state = add(state_taps, Ellipsis)
    for r, out in enumerate(outs):
        out[...] = jnp.zeros_like(out)
        out[0:5, :] = add(taps, r)[0:5]
        out[5:6, :] = column_sum(add(gains, r))
        out[6:7, :] = column_sum(add(skips, r))
        mine = pltpu.roll(rest, (LANES - r * per_block) % LANES, 1) if r else rest
        out[7:8, :LANES] = mine[0:1]
        out[7:8, LANES : 2 * LANES] = mine[1:2]
        row = 8
        for q in range(0, model, width):
            out[row : row + per_block, :] = step[r * per_block : (r + 1) * per_block, q : q + width]
            row += per_block
        for q in range(0, model, width):
            out[row : row + 1, :] = norm[:, q : q + width]
            row += 1
        out[row : row + 5, : 2 * LANES] = state[0:5]


def pack_sums(values, width, per_block, blocks, *groups):
    n, _, model = values.shape
    rows = 8 + per_block * (model // width) + model // width + 5
    return pl.pallas_call(
        functools.partial(pack_kernel, n, per_block),
        out_shape=[jax.ShapeDtypeStruct((-(-rows // 8) * 8, width), F32)] * blocks,
        compiler_params=pltpu.CompilerParams(vmem_limit_bytes=VMEM),
        name="pack",
    )(values, *[v for group in groups for v in group])


def swapped(value, axis, step):
    return lax.ppermute(value, axis, [(i, i ^ step) for i in range(lax.axis_size(axis))])


def reached(value):
    return {r: swapped(value, "head", r) if r else value for r in [0, 1] + list(range(2, lax.axis_size("head"), 2))}


def forwarded(parts):
    rest = {r + 1: swapped(parts[r], "head", 1) for r in parts if r and r % 2 == 0}
    return [{**parts, **rest}[r] for r in range(lax.axis_size("head"))]


def gathered(value):
    return forwarded(reached(value))


def bits_of(axis):
    return [1 << i for i in range((lax.axis_size(axis) - 1).bit_length())]


def added(a, b, dtype=None):
    return (a.astype(F32) + b.astype(F32)).astype(dtype or a.dtype)


def tree_sum(values):
    while len(values) > 1:
        values = [a + b for a, b in zip(values[::2], values[1::2])]
    return values[0]


def head_sum(value, bits):
    for bit in reversed(bits):
        half = value.shape[0] // 2
        arrived = yield value[half:], "head", bit
        value = added(value[:half], arrived)
    return value[0]


def ranges_sum(value):
    ranges = lax.axis_size("seq")
    me = lax.axis_index("seq")
    lead, rest = value.shape[0], value.shape[2:]
    piece = (value.shape[1] // ranges,) + rest
    for bit in bits_of("seq"):
        mine = (me // bit) % 2
        halves = value.reshape((lead, ranges // bit // 2, 2) + piece)
        arrived = yield lax.dynamic_index_in_dim(halves, 1 - mine, 2, keepdims=False), "seq", bit
        kept = lax.dynamic_index_in_dim(halves, mine, 2, keepdims=False)
        value = added(kept, arrived, F32 if 2 * bit == ranges else value.dtype)
    return value.reshape((lead,) + piece)


def whole_sum(value, axis):
    for bit in bits_of(axis):
        arrived = yield value, axis, bit
        value = value + arrived
    return value


def weight_sum(kept, sent, ranges_first):
    arrived = yield sent, "head", 1
    value = added(kept, arrived)
    bits = bits_of("head")[1:]
    if ranges_first:
        value = yield from ranges_sum(value)
        return (yield from head_sum(value, bits))
    value = yield from head_sum(value, bits)
    return (yield from ranges_sum(value[None]))[0]


def state_sum(value):
    value = yield from ranges_sum(value[None])
    return (yield from whole_sum(value[0], "head"))


class Chain:
    def __init__(self, v, name, steps):
        self.v, self.name, self.steps, self.done = v, name, steps, False
        v[name] = None
        self.advance()

    def advance(self):
        if self.done:
            return
        try:
            self.v[self.name] = swapped(*self.steps.send(self.v[self.name]))
        except StopIteration as end:
            self.v[self.name], self.done = end.value, True

    def finish(self):
        while not self.done:
            self.advance()
        return self.v[self.name]


def assembled(parts, edges=None):
    n = len(parts)
    me = lax.axis_index("head")
    pieces, places, last_rows = [], [], []
    for s in range(n):
        for r, part in enumerate(parts[s]):
            pieces.append(part)
            places.append((me ^ r) * n + s)
            if edges is not None:
                last_rows.append(edges[r][s : s + 1])
    return assemble(pieces, last_rows, places)


def padded_lanes(value, size):
    return jnp.pad(value, ((0, 0), (0, size - value.shape[1])))


def shards(
    tokens,
    doc_ids,
    norm_gain,
    head_input_weight,
    state_input_weight,
    timestep_input_weight,
    conv_x,
    conv_state,
    head_params,
    gated_gain,
    output_weight,
    cotangent,
):
    seqs, length, model = tokens.shape
    blocks = lax.axis_size("head")
    ranges = lax.axis_size("seq")
    n = seqs // blocks
    width = gated_gain.shape[0]
    heads = head_params.shape[1]
    me = lax.axis_index("head")
    tokens = lax.dynamic_slice_in_dim(tokens, me * n, n, 0)
    cotangent = lax.dynamic_slice_in_dim(cotangent, me * n, n, 0)
    before = lax.ppermute(tokens[:, length - PAD :], "seq", [(i, i + 1) for i in range(ranges - 1)])
    padded = jnp.concatenate([before, tokens], axis=1)

    start = lax.axis_index("seq") * length
    lead = jnp.concatenate(
        [jnp.full((seqs, PAD), -1, jnp.int32), doc_ids, jnp.full((seqs, PAD), -2, jnp.int32)], axis=1
    )
    ids = lax.dynamic_slice(lead, (me * n, start), (n, length + 2 * PAD)).astype(F32)
    id_rows = jnp.broadcast_to(ids[:, None], (n, 8, length + 2 * PAD))
    ids = jnp.broadcast_to(ids[:, :, None], (n, length + 2 * PAD, LANES))

    pack = jnp.concatenate(
        [
            conv_x,
            gated_gain[None],
            padded_lanes(head_params, width),
            jnp.transpose(timestep_input_weight).astype(F32).reshape(heads * model // width, width),
        ],
        axis=0,
    )
    half = blocks // 2
    packs, side = lax.optimization_barrier((reached(pack), head_input_weight.reshape(model, 2 * width)))
    packs = forwarded(packs)
    row_parts = reached(side[:, width:])
    packed = lambda rows: jnp.pad(jnp.concatenate(rows, axis=1), ((0, 0), (0, LANES - heads * blocks)))
    small = jnp.pad(packed([v[6:9, :heads] for v in packs]), ((0, 5), (0, 0)))
    step_weights = jnp.pad(
        jnp.concatenate([v[9:].reshape(heads, model) for v in packs]).astype(BF16), ((0, LANES - heads * blocks), (0, 0))
    )
    params = jnp.stack(
        [
            jnp.concatenate([v[:6], jnp.repeat(v[8, :heads], HEAD_DIM)[None], jnp.zeros((1, width), F32)], axis=0)
            for v in packs
        ]
    )
    state_taps = jnp.pad(conv_state, ((0, 3), (0, 0)))

    tok_float = padded.astype(F32)
    scale = lax.rsqrt(jnp.mean(tok_float * tok_float, axis=-1, keepdims=True) + EPS)
    normed = (tok_float * scale * norm_gain).astype(BF16)
    rows, raw, steps, log_decay, cum, state_rows, bc = project_first(
        normed, state_input_weight, step_weights, small, ids, id_rows, state_taps, [row_parts[0], row_parts[1]], blocks,
        heads * blocks,
    )
    row_parts, rows, gate_own, out_own = lax.optimization_barrier(
        (row_parts, rows, side[:, :width], output_weight)
    )
    row_weights = forwarded(row_parts)
    cuts = ranges // (blocks * n)
    held = state_call(rows, bc, ids, id_rows, steps, cum, params, (), 0, 2, heads, cuts)
    held, rows = lax.optimization_barrier((held, rows))
    acted, message = held
    for r in range(2, blocks, 2):
        rows = project_more(normed, rows, row_weights[r : r + 2], r)
        acted, message = state_call(rows, bc, ids, id_rows, steps, cum, params, (acted, message), r, 2, heads, cuts)
    mixed, states = inside_call(acted, bc, ids, id_rows, steps, cum, heads)
    v = Values(mixed=mixed, arrived=send_message(message))
    v.meet("arrived", "mixed")
    v["entered"] = send_back(relay(v["arrived"], False), blocks, n)
    gate_weights = gathered(gate_own)
    out_weights = gathered(out_own)
    v["gate"] = project_gate(normed, gate_weights)
    v.meet("entered", "gate")

    cuts = ranges // blocks
    gain_parts, skip_parts = [], []
    for s in range(n):
        v[f"out{s}"], v[f"normed{s}"], v[f"d_gate{s}"], v[f"d_sum{s}"], v[f"message{s}"], gains, skips = middle_call(
            s, v["mixed"], v["gate"], acted, cum, v["entered"], bc, ids, tokens, cotangent, params, out_weights, heads, cuts
        )
        gain_parts.append(gains)
        skip_parts.append(skips)
        v.meet("entered", f"message{s}")
    every = lambda name: [f"{name}{s}" for s in range(n)]
    listed = lambda name: [v[k] for k in every(name)]
    for name in every("out"):
        v[name] = reached(v[name])

    def inside_back(s):
        v[f"d_scaled{s}"], *rest = inside_back_call(
            s, acted, v[f"d_sum{s}"], v["mixed"], bc, ids, id_rows, steps, cum, states, v["entered"], heads
        )
        v[f"inside{s}"] = tuple(rest)

    def close(s):
        d_b, d_c, d_cum = v[f"inside{s}"]
        v[f"d_rows{s}"], v[f"d_raw{s}"], v[f"d_state{s}"], *rest = close_call(
            s, rows, acted, v[f"d_sum{s}"], v[f"d_scaled{s}"], bc, ids, id_rows, steps, raw, log_decay, cum, d_cum,
            v[f"leaving{s}"], v["entered"], params, small, state_rows, state_taps, d_b, d_c, heads,
        )
        v[f"closed{s}"] = tuple(rest)

    for s in range(n):
        last = s == n - 1
        v["arrived"] = send_message(v[f"message{s}"])
        names = ["arrived"]
        if s:
            inside_back(s)
            names += [f"d_scaled{s}", "out_sum", "gate_sum"]
        else:
            names += every("message")[1:]
        v.meet(*names)
        v["carried"] = relay(v["arrived"], True)
        if s:
            out_chain.advance()
            v.meet("carried", f"leaving{s - 1}")
        else:
            v.meet("carried", "d_sum0", *every("normed"), *every("d_gate"))
        v[f"leaving{s}"] = send_back(v["carried"], blocks, 1)
        if s:
            close(s - 1)
            v.meet(f"leaving{s}", f"d_rows{s - 1}", "out_sum")
            out_chain.advance()
            gate_chain.advance()
        else:
            inside_back(0)
            v["out_grads"] = weight_grad(cotangent, listed("normed"))
            v["gate_grads"] = weight_grad(normed, listed("d_gate"))
            v.meet(
                "leaving0", "d_scaled0", "out_grads", "gate_grads", *every("out"), *every("message")[1:],
                *every("d_sum")[1:],
            )
            out_chain = Chain(v, "out_sum", weight_sum(*v["out_grads"], False))
            gate_chain = Chain(v, "gate_sum", weight_sum(*v["gate_grads"], False))
    close(n - 1)
    v.meet(f"d_rows{n - 1}", "out_sum")
    out_chain.advance()

    v["rows_grads"] = weight_grad(normed, listed("d_rows"))
    v["state_grad"] = state_grad(normed, listed("d_state"))
    v["gain"] = norm_gain[None]
    v.meet("rows_grads", "state_grad", "out_sum", "gate_sum", "gain")
    out_chain.advance()
    gate_chain.advance()
    rows_chain = Chain(v, "rows_sum", weight_sum(*v["rows_grads"], True))
    state_chain = Chain(v, "state_sum", state_sum(v["state_grad"]))
    halos, last_rows, norm_parts = [], [], []
    for s in range(n):
        input_grad, edge, halo, gain_part = input_call(
            s, v[f"d_gate{s}"], v[f"d_rows{s}"], v[f"d_raw{s}"], v[f"d_state{s}"], padded, cotangent, v["gain"],
            state_input_weight, step_weights, row_weights, gate_weights,
        )
        v[f"input{s}"] = input_grad
        halos.append(halo)
        last_rows.append(edge)
        norm_parts.append(gain_part)
        if s == 0:
            v.meet("rows_sum", "gain", "input0", "gate_sum", "out_sum", "state_sum")
            for chain in (rows_chain, gate_chain, out_chain, state_chain):
                chain.advance()
        if s == n - 1:
            v.meet("gate_sum", "state_sum", f"input{s}", *every("out"))
            gate_chain.advance()
            state_chain.advance()
        v[f"input{s}"] = reached(v[f"input{s}"])

    closes = listed("closed")
    smalls = pack_sums(
        normed, width, heads, blocks, listed("d_raw"), *[[c[i] for c in closes] for i in range(3)], gain_parts, skip_parts,
        norm_parts,
    )
    v["halo"] = lax.ppermute(jnp.concatenate(halos, axis=0), "seq", [(i + 1, i) for i in range(ranges - 1)])
    v["small"] = tuple(swapped(part, "head", r) if r else part for r, part in enumerate(smalls))
    v.meet("halo", "small", "rows_sum", "gate_sum", "state_sum", "input0")
    rows_chain.advance()
    gate_chain.advance()
    state_chain.advance()
    v["first"] = tuple(forwarded(v["input0"]))
    v["edges"] = reached(added(jnp.concatenate(last_rows, axis=0), v["halo"], BF16))
    v["small"] = tree_sum(list(v["small"]))
    rounds = [["edges", "first", *every("input")[1:]]]
    for i, bit in enumerate(bits_of("seq")):
        v["came"] = swapped(v["small"], "seq", bit)
        v.meet("came", "small", "rows_sum", "state_sum", *(rounds[i] if i < len(rounds) else []))
        rows_chain.advance()
        state_chain.advance()
        v["small"] = v["small"] + v["came"]
        if i == 0:
            v["output"] = assembled([forwarded(part) for part in listed("out")])
    v.meet("small", "rows_sum", "output")
    out_grad = jnp.transpose(out_chain.finish())
    gate_sum, rows_sum, in_state = gate_chain.finish(), rows_chain.finish(), state_chain.finish()
    both = v["small"]
    whole_input = assembled(
        [list(v["first"])] + [forwarded(v[f"input{s}"]) for s in range(1, n)], forwarded(v["edges"])
    )
    per_row = model // width
    row = 8 + heads * per_row
    steps_end = both[8:row].reshape(per_row, heads, width).transpose(0, 2, 1).reshape(model, heads)
    skip_sum = jnp.sum(both[6].reshape(heads, HEAD_DIM), axis=1)
    return (
        v["output"],
        whole_input,
        both[row : row + per_row].reshape(model),
        jnp.stack([gate_sum, rows_sum], axis=1),
        in_state,
        steps_end,
        both[:5],
        both[row + per_row : row + per_row + 5, : 2 * LANES],
        jnp.stack([both[7, :heads], both[7, LANES : LANES + heads], skip_sum]),
        both[5],
        out_grad,
    )


def solution(mesh):
    return jax.shard_map(
        shards,
        mesh=mesh,
        in_specs=(
            P(None, "seq", None),
            P(),
            P(),
            P(None, None, "head"),
            P(),
            P(None, "head"),
            P(None, "head"),
            P(),
            P(None, "head"),
            P("head"),
            P("head", None),
            P(None, "seq", None),
        ),
        out_specs=(
            P(None, "seq", None),
            P(None, "seq", None),
            P(),
            P("seq", None, "head"),
            P("seq", None),
            P(None, "head"),
            P(None, "head"),
            P(),
            P(None, "head"),
            P("head"),
            P("head", "seq"),
        ),
        check_vma=False,
    )
```

```python
import functools

import jax
import jax.numpy as jnp
from jax import lax
from jax.experimental import pallas as pl
from jax.experimental.pallas import tpu as pltpu
from jax.sharding import PartitionSpec as P

F32 = jnp.float32
BF16 = jnp.bfloat16
EPS = 1e-5
CHUNK = 128
PAD = 16
LANES = 128
HEAD_DIM = 64
VMEM = 60 * 1024 * 1024


def dot(a, b):
    return lax.dot_general(a, b, (((1,), (0,)), ((), ())), preferred_element_type=F32)


def dot_nt(a, b):
    return lax.dot_general(a, b, (((1,), (1,)), ((), ())), preferred_element_type=F32)


def dot_tn(a, b):
    return lax.dot_general(a, b, (((0,), (0,)), ((), ())), preferred_element_type=F32)


def split(value):
    high = value.astype(BF16)
    return high, (value - high.astype(F32)).astype(BF16)


def head_map(width, offset):
    lane = lax.broadcasted_iota(jnp.int32, (LANES, width), 1)
    row = lax.broadcasted_iota(jnp.int32, (LANES, width), 0)
    return (lax.shift_right_logical(lane, 6) + offset == row).astype(F32).astype(BF16)


def expand(value, width, offset):
    lane = lax.shift_right_logical(lax.broadcasted_iota(jnp.int32, value.shape, 1), 6) + offset
    return jnp.concatenate(
        [jnp.take_along_axis(value, lane + 2 * p, axis=1) for p in range(width // LANES)], axis=1
    )


def expand_row(value, width, offset):
    return expand(jnp.broadcast_to(value, (8, LANES)), width, offset)


def column(value, index):
    return jnp.take_along_axis(value, jnp.zeros(value.shape, jnp.int32) + index, axis=1)


def by_head(value, heads):
    high, low = split(value)
    return dot_nt(high, heads) + dot_nt(low, heads)


def by_head_low(value, heads):
    return dot_nt(value.astype(BF16), heads)


def widen(value, width):
    return jnp.concatenate([value] * (width // LANES), axis=1)


def fold8(value):
    return value[0:8] + value[8:16]


def sigmoid(value):
    return 0.5 * jnp.tanh(0.5 * value) + 0.5


def triangle(lower):
    row = lax.broadcasted_iota(jnp.int32, (CHUNK, CHUNK), 0)
    column = lax.broadcasted_iota(jnp.int32, (CHUNK, CHUNK), 1)
    return (row >= column if lower else row <= column)


def exact_dot(ones, value):
    return jnp.dot(ones, value, precision=lax.Precision.HIGHEST, preferred_element_type=F32)


def rows_at(start, count):
    return pl.ds(pl.multiple_of(start, 16), count)


def entering_maps(columns, rows, first, count):
    window = count + PAD
    token = lax.broadcasted_iota(jnp.int32, (count, window), 0)
    entry = lax.broadcasted_iota(jnp.int32, (count, window), 1)
    same = wide_marks(columns[0, first : first + count, :], window) == rows[0, 0:1, first - PAD : first + count]
    distance = entry - token
    return jnp.concatenate(
        [jnp.where(same & (distance == PAD - 3 + k), 1.0, 0.0).astype(BF16) for k in range(3)], axis=0
    )


def leaving_maps(columns, rows, first, count):
    window = count + PAD
    row = lax.broadcasted_iota(jnp.int32, (count, window), 0)
    token = lax.broadcasted_iota(jnp.int32, (count, window), 1)
    same = wide_marks(columns[0, first : first + count, :], window) == rows[0, 0:1, first : first + window]
    distance = token - row
    return jnp.concatenate(
        [jnp.where(same & (distance == 3 - k), 1.0, 0.0).astype(BF16) for k in range(3)], axis=0
    )


def wide_marks(columns, window):
    whole = jnp.concatenate([columns] * -(-window // LANES), axis=1)
    return whole[:, :window]


def conv_sum(rows, maps, taps, first, lanes):
    moved = dot(maps, rows[first - PAD : first + CHUNK, lanes])
    entering = [moved[k * CHUNK : (k + 1) * CHUNK] for k in range(3)]
    entering.append(rows[first : first + CHUNK, lanes].astype(F32))
    total = taps[4:5, lanes]
    for k in range(4):
        total = total + taps[k : k + 1, lanes] * entering[k]
    return total, entering


def lane_groups(width):
    step = min(width, 2 * LANES)
    return [slice(i, i + step) for i in range(0, width, step)]


def conv_forward(rows, ids, id_rows, taps, store, length):
    for c in range(length // CHUNK):
        first = PAD + c * CHUNK
        maps = entering_maps(ids, id_rows, first, CHUNK)
        for lanes in lane_groups(rows.shape[1]):
            total, _ = conv_sum(rows, maps, taps, first, lanes)
            store(slice(c * CHUNK, (c + 1) * CHUNK), lanes, (total * sigmoid(total)).astype(BF16))


def conv_backward(rows, ids, id_rows, taps, d_acted, d_pre, d_rows, length):
    width = d_pre.shape[1]
    zero = jnp.zeros((16, width), BF16)
    d_pre[0:16, :] = zero
    d_pre[length + PAD : length + PAD + 16, :] = zero
    groups = lane_groups(width)
    sums = [[jnp.zeros((8, g.stop - g.start), F32) for _ in range(5)] for g in groups]
    for c in range(length // CHUNK - 1, -1, -1):
        first = PAD + c * CHUNK
        here = slice(first, first + CHUNK)
        maps = entering_maps(ids, id_rows, first, CHUNK)
        back = leaving_maps(ids, id_rows, first, CHUNK)
        for i, lanes in enumerate(groups):
            total, entering = conv_sum(rows, maps, taps, first, lanes)
            sigma = sigmoid(total)
            grad = d_acted(c, lanes) * (sigma * (1.0 + total * (1.0 - sigma)))
            d_pre[here, lanes] = grad.astype(BF16)
            for k in range(5):
                product = grad * entering[k] if k < 4 else grad
                sums[i][k] = sums[i][k] + jnp.sum(product.reshape(CHUNK // 8, 8, -1), axis=0)
            moved = dot(back, d_pre[first : first + CHUNK + PAD, lanes])
            result = taps[3:4, lanes] * grad
            for k in range(3):
                result = result + taps[k : k + 1, lanes] * moved[k * CHUNK : (k + 1) * CHUNK]
            d_rows(here, lanes, result.astype(BF16))
    back = leaving_maps(ids, id_rows, 0, PAD)
    for lanes in groups:
        moved = dot(back, d_pre[0 : 2 * PAD, lanes])
        result = taps[0:1, lanes] * moved[0:PAD]
        for k in range(1, 3):
            result = result + taps[k : k + 1, lanes] * moved[k * PAD : (k + 1) * PAD]
        d_rows(slice(0, PAD), lanes, result.astype(BF16))
    return [
        jnp.concatenate([jnp.sum(part[k], axis=0, keepdims=True) for part in sums], axis=1) for k in range(5)
    ]


def softplus(value):
    return jnp.maximum(value, 0.0) + jnp.log1p(jnp.exp(-jnp.abs(value)))


def project_rows(values, weights, rows):
    for r, weight in enumerate(weights):
        rows[r, 0] = dot(values, weight[...]).astype(BF16)


def project_first_kernel(blocks, heads, normed, state_w, step_w, small, ids, id_rows, taps, *refs):
    weights, refs = refs[:blocks], refs[blocks:]
    rows, raw, steps, log_decay, cum, state_rows, bc = refs
    length = bc.shape[1]
    values = normed[0]
    state_rows[0] = dot(values, state_w[...]).astype(BF16)
    part = dot_nt(values[PAD:], step_w[...])
    raw[0] = part
    lane = lax.broadcasted_iota(jnp.int32, (length, LANES), 1)
    size = jnp.where(lane < heads, softplus(part + small[0:1, :]), 0.0)
    steps[0] = size
    log_decay[0] = -size * jnp.exp(small[1:2, :])
    ones = triangle(True).astype(F32)
    total = jnp.zeros((1, LANES), F32)
    for c in range(length // CHUNK):
        here = slice(c * CHUNK, (c + 1) * CHUNK)
        value = exact_dot(ones, log_decay[0, here, :]) + total
        cum[0, here, :] = value
        total = value[CHUNK - 1 : CHUNK]

    def store(here, lanes, value):
        bc[0, here, lanes] = value

    conv_forward(state_rows.at[0], ids, id_rows, taps[...], store, length)
    project_rows(values, weights, rows)


def project_more_kernel(blocks, normed, held, *refs):
    project_rows(normed[0], refs[:blocks], refs[blocks])


def project_first(normed, state_w, step_w, small, ids, id_rows, taps, weights, blocks, heads):
    n, padded, model = normed.shape
    width = weights[0].shape[1]
    length = padded - PAD
    whole = lambda a: pl.BlockSpec(a.shape, lambda s: (0,) * a.ndim, pipeline_mode=pl.Buffered(1))
    per_seq = lambda a, b: pl.BlockSpec((1, a, b), lambda s: (s, 0, 0))
    lanes = jax.ShapeDtypeStruct((n, length, LANES), F32)
    return pl.pallas_call(
        functools.partial(project_first_kernel, len(weights), heads),
        grid=(n,),
        in_specs=[
            per_seq(padded, model), whole(state_w), whole(step_w), whole(small), per_seq(*ids.shape[1:]),
            per_seq(*id_rows.shape[1:]), whole(taps),
        ] + [whole(v) for v in weights],
        out_specs=[pl.BlockSpec((len(weights), 1, padded, width), lambda s: (0, s, 0, 0))]
        + [per_seq(length, LANES)] * 4
        + [per_seq(padded, 2 * LANES), per_seq(length, 2 * LANES)],
        out_shape=[
            jax.ShapeDtypeStruct((blocks, n, padded, width), BF16), lanes, lanes, lanes, lanes,
            jax.ShapeDtypeStruct((n, padded, 2 * LANES), BF16),
            jax.ShapeDtypeStruct((n, length, 2 * LANES), BF16),
        ],
        compiler_params=pltpu.CompilerParams(vmem_limit_bytes=VMEM),
        name="project_first",
    )(normed, state_w, step_w, small, ids, id_rows, taps, *weights)


def project_more(normed, rows, weights, first):
    n, padded, model = normed.shape
    width = weights[0].shape[1]
    count = len(weights)
    return pl.pallas_call(
        functools.partial(project_more_kernel, count),
        grid=(n,),
        in_specs=[pl.BlockSpec((1, padded, model), lambda s: (s, 0, 0)), pl.BlockSpec(memory_space=pl.ANY)]
        + [pl.BlockSpec(v.shape, lambda s: (0, 0), pipeline_mode=pl.Buffered(1)) for v in weights],
        out_specs=pl.BlockSpec((count, 1, padded, width), lambda s: (first // count, s, 0, 0)),
        out_shape=jax.ShapeDtypeStruct(rows.shape, BF16),
        input_output_aliases={1: 0},
        compiler_params=pltpu.CompilerParams(vmem_limit_bytes=VMEM),
        name="project_more",
    )(normed, rows, *weights)


def project_gate_kernel(blocks, normed, *refs):
    for r in range(blocks):
        refs[blocks][r, 0] = dot(normed[0, PAD:, :], refs[r][...]).astype(BF16)


def project_gate(normed, weights):
    n, padded, model = normed.shape
    width = weights[0].shape[1]
    count = len(weights)
    return pl.pallas_call(
        functools.partial(project_gate_kernel, count),
        grid=(n,),
        in_specs=[pl.BlockSpec((1, padded, model), lambda s: (s, 0, 0))]
        + [pl.BlockSpec(v.shape, lambda s: (0, 0), pipeline_mode=pl.Buffered(1)) for v in weights],
        out_specs=pl.BlockSpec((count, 1, padded - PAD, width), lambda s: (0, s, 0, 0)),
        out_shape=jax.ShapeDtypeStruct((count, n, padded - PAD, width), BF16),
        compiler_params=pltpu.CompilerParams(vmem_limit_bytes=VMEM),
        name="project_gate",
    )(normed, *weights)


def write_message(message, state, survive):
    cuts, rows, width = message.shape
    own = rows - 16
    survive = jnp.concatenate([survive, survive], axis=0).astype(BF16)
    for i in range(cuts):
        message[i, :own, :] = state[i * own : (i + 1) * own].astype(BF16)
        message[i, own:, :] = survive


def state_kernel(first, per_block, rows, bc, ids, id_rows, steps, cum, taps, *refs):
    acted, message = refs[-2:]
    length, width = acted.shape[2:]
    offset = (pl.program_id(0) + first) * per_block

    def store(here, lanes, value):
        acted[0, 0, here, lanes] = value

    conv_forward(rows.at[0, 0], ids, id_rows, taps[0], store, length)
    total = cum[0, length - 1 : length, :]
    last = ids[0, PAD + length - 1 : PAD + length, :]
    before = ids[0, PAD - 1 : PAD, :]
    state = jnp.zeros((LANES, width), F32)
    for c in range(length // CHUNK):
        here = slice(c * CHUNK, (c + 1) * CHUNK)
        same = (ids[0, PAD + c * CHUNK : PAD + (c + 1) * CHUNK, :] == last).astype(F32)
        tail = jnp.exp(total - cum[0, here, :]) * same * steps[0, here, :]
        scaled = (expand(tail, width, offset) * acted[0, 0, here, :].astype(F32)).astype(BF16)
        state = state + dot_tn(bc[0, here, :LANES], scaled)
    survive = jnp.exp(total) * (last == before).astype(F32)
    write_message(message.at[0, 0], state, expand_row(survive, width, offset))


def state_call(rows, bc, ids, id_rows, steps, cum, taps, held, first, count, per_block, cuts):
    blocks, n, padded, width = rows.shape
    length = padded - PAD
    four = lambda a, b: pl.BlockSpec((1, 1, a, b), lambda g, s: (g + first, s, 0, 0))
    per_seq = lambda a: pl.BlockSpec((1,) + a.shape[1:], lambda g, s: (s, 0, 0))
    piece = LANES // cuts + 16
    return pl.pallas_call(
        functools.partial(state_kernel, first, per_block),
        grid=(count, n),
        in_specs=[
            four(padded, width), per_seq(bc), per_seq(ids), per_seq(id_rows), per_seq(steps), per_seq(cum),
            pl.BlockSpec((1,) + taps.shape[1:], lambda g, s: (g + first, 0, 0)),
        ] + [pl.BlockSpec(memory_space=pl.ANY) for _ in held],
        out_specs=[
            four(length, width),
            pl.BlockSpec((1, 1, cuts, piece, width), lambda g, s: (g + first, s, 0, 0, 0)),
        ],
        out_shape=[
            jax.ShapeDtypeStruct((blocks, n, length, width), BF16),
            jax.ShapeDtypeStruct((blocks, n, cuts, piece, width), BF16),
        ],
        input_output_aliases={7: 0, 8: 1} if held else {},
        compiler_params=pltpu.CompilerParams(vmem_limit_bytes=VMEM),
        name="range_state",
    )(rows, bc, ids, id_rows, steps, cum, taps, *held)


def chunk_marks(ids, c):
    first = PAD + c * CHUNK
    return ids[0, first : first + CHUNK, :], ids[0, first + CHUNK - 1 : first + CHUNK, :], ids[0, first - 1 : first, :]


def chunk_decays(ids, cum, c):
    here, last, before = chunk_marks(ids, c)
    value = cum[0, c * CHUNK : (c + 1) * CHUNK, :]
    base = cum[0, c * CHUNK - 1 : c * CHUNK, :] if c else jnp.zeros((1, LANES), F32)
    end = value[CHUNK - 1 : CHUNK]
    entering = jnp.exp(value - base) * (here == before).astype(F32)
    tail = jnp.exp(end - value) * (here == last).astype(F32)
    survive = jnp.exp(end - base) * (last == before).astype(F32)
    return entering, tail, survive


def lane_halves(pair):
    lane = lax.broadcasted_iota(jnp.int32, pair.shape, 1)
    zero = jnp.zeros_like(pair)
    return jnp.concatenate([jnp.where(lane < HEAD_DIM, pair, zero), jnp.where(lane < HEAD_DIM, zero, pair)], axis=0)


def inside_kernel(per_block, acted, bc, ids, id_rows, steps, cum, mixed, states, carried, turned):
    length, width = acted.shape[2:]
    offset = pl.program_id(1) * per_block
    later = triangle(True)
    for c in range(length // CHUNK):
        here = slice(c * CHUNK, (c + 1) * CHUNK)
        b_part, c_part = bc[0, here, :LANES], bc[0, here, LANES:]
        marks, _, _ = chunk_marks(ids, c)
        same = later & (marks == id_rows[0, 0:1, PAD + c * CHUNK : PAD + (c + 1) * CHUNK])
        scores = jnp.where(same, dot_nt(c_part, b_part), 0.0)
        value = cum[0, here, :]
        turned[...] = jnp.transpose(value)
        entering, tail, survive = chunk_decays(ids, cum, c)
        scaled = (expand(steps[0, here, :], width, offset) * acted[0, 0, here, :].astype(F32)).astype(BF16)
        if c:
            held = carried[...]
            held_low = held.astype(BF16)
            states[0, 0, c - 1] = held_low
            outside = dot(c_part, held_low) * expand(entering, width, offset)
        for pair in range(width // LANES):
            lanes = slice(pair * LANES, (pair + 1) * LANES)
            mixing = []
            for h in (2 * pair, 2 * pair + 1):
                spread = jnp.minimum(column(value, offset + h) - turned[pl.ds(offset + h, 1), :], 0.0)
                mixing.append((scores * jnp.exp(spread)).astype(BF16))
            result = dot(jnp.concatenate(mixing, axis=1), lane_halves(scaled[:, lanes]))
            mixed[0, 0, here, lanes] = result + outside[:, lanes] if c else result
        if c + 1 < length // CHUNK:
            fresh = dot_tn(b_part, (expand(tail, width, offset) * scaled.astype(F32)).astype(BF16))
            if c:
                fresh = fresh + held * expand_row(survive, width, offset)[0:1]
            carried[...] = fresh


def inside_call(acted, bc, ids, id_rows, steps, cum, per_block):
    blocks, n, length, width = acted.shape
    chunks = length // CHUNK
    four = lambda a, b: pl.BlockSpec((1, 1, a, b), lambda s, g: (g, s, 0, 0))
    per_seq = lambda a: pl.BlockSpec((1,) + a.shape[1:], lambda s, g: (s, 0, 0))
    return pl.pallas_call(
        functools.partial(inside_kernel, per_block),
        grid=(n, blocks),
        in_specs=[four(length, width), per_seq(bc), per_seq(ids), per_seq(id_rows), per_seq(steps), per_seq(cum)],
        out_specs=[
            four(length, width),
            pl.BlockSpec((1, 1, chunks - 1, LANES, width), lambda s, g: (g, s, 0, 0, 0)),
        ],
        out_shape=[
            jax.ShapeDtypeStruct((blocks, n, length, width), F32),
            jax.ShapeDtypeStruct((blocks, n, chunks - 1, LANES, width), BF16),
        ],
        scratch_shapes=[pltpu.VMEM((LANES, width), F32), pltpu.VMEM((LANES, LANES), F32)],
        compiler_params=pltpu.CompilerParams(vmem_limit_bytes=VMEM),
        name="inside",
    )(acted, bc, ids, id_rows, steps, cum)


def relay_kernel(backward, message, carried):
    ranges, rows, width = carried.shape
    state = jnp.zeros((rows, width), F32)
    order = range(ranges - 1, -1, -1) if backward else range(ranges)
    for q in order:
        carried[q] = state.astype(BF16)
        decay = message[q, rows : rows + 1, :].astype(F32)
        state = state * decay + message[q, :rows, :].astype(F32)


class Held:
    def __init__(self, value=None):
        self.value = value


def meet(*held):
    for h, value in zip(held, lax.optimization_barrier(tuple(h.value for h in held))):
        h.value = value


def values(held):
    return [h.value for h in held]


def over_ranges(value):
    return lax.all_to_all(value, "seq", 0, 0, tiled=True)


def send_message(message):
    return over_ranges(message.reshape(lax.axis_size("seq"), message.shape[3], message.shape[4]))


def relay(arrived, backward):
    ranges, rows, width = arrived.shape
    return pl.pallas_call(
        functools.partial(relay_kernel, backward),
        out_shape=jax.ShapeDtypeStruct((ranges, rows - 16, width), BF16),
        compiler_params=pltpu.CompilerParams(vmem_limit_bytes=VMEM),
        name="relay",
    )(arrived)


def send_back(carried, blocks, n):
    return over_ranges(carried).reshape(blocks, n, LANES, carried.shape[2])


def middle_kernel(
    blocks, per_block, total_width, mixed, gate, acted, cum, cum_end, bc, ids, ids_before, ids_after, tokens, cotangent,
    params, entered, *refs
):
    weights, refs = refs[:blocks], refs[blocks:]
    output, normed_out, d_gate, d_summed, pulled, gain_grad, skip_grad = refs[:7]
    summed_s, gated_s, grad_s, first_s, second_s, low_s, row_s, pull_s = refs[7:]
    tile, width = mixed.shape[2:]
    t = pl.program_id(0)
    before = ids_before[0, PAD - 1 : PAD, :]
    marks = ids[0]
    c_part = bc[0, :, LANES:]
    slabs = tile // 16
    same = (marks == before).astype(F32)
    decay = jnp.exp(cum[0]) * same
    row_s[...] = jnp.zeros_like(row_s)

    def lanes_sum(value):
        total = value[:, :LANES]
        for i in range(1, width // LANES):
            total = total + value[:, i * LANES : (i + 1) * LANES]
        return total

    @pl.when(t == 0)
    def _():
        gain_grad[...] = jnp.zeros_like(gain_grad)
        skip_grad[...] = jnp.zeros_like(skip_grad)
        pull_s[...] = jnp.zeros_like(pull_s)

    for r in range(blocks):
        first_s[...] = dot(c_part, entered[r, 0])
        second_s[r] = expand(decay, width, r * per_block)
        skip = params[r, 6:7, :]

        def step(i, carry, r=r, skip=skip):
            here = rows_at(i * 16, 16)
            value = mixed[r, 0, here, :] + first_s[here, :] * second_s[r, here, :]
            summed = value + skip * acted[r, 0, here, :].astype(F32)
            g = gate[r, 0, here, :].astype(F32)
            gated = summed * (g * sigmoid(g))
            summed_s[r, here, :] = summed
            gated_s[r, here, :] = gated
            row_s[here, :] = row_s[here, :] + lanes_sum(gated * gated)
            return carry

        lax.fori_loop(0, slabs, step, 0, unroll=4)
    squares = jnp.sum(row_s[...], axis=1, keepdims=True)
    rescale = jnp.broadcast_to(lax.rsqrt(squares / total_width + EPS), (tile, LANES))
    row_s[...] = rescale
    for r in range(blocks):
        gain = params[r, 5:6, :]

        def step(i, carry, r=r, gain=gain):
            here = rows_at(i * 16, 16)
            normed_out[r, 0, here, :] = (gated_s[r, here, :] * widen(row_s[here, :], width) * gain).astype(BF16)
            return carry

        lax.fori_loop(0, slabs, step, 0, unroll=4)
    branch = tokens[0].astype(F32)
    for r in range(blocks):
        branch = branch + dot(normed_out[r, 0], weights[r][...])
    output[0] = branch.astype(BF16)
    first_s[:, :LANES] = jnp.zeros((tile, LANES), F32)
    for r in range(blocks):
        grad_s[r] = dot_nt(cotangent[0], weights[r][...])
        gain = params[r, 5:6, :]

        def step(i, total, r=r, gain=gain):
            here = rows_at(i * 16, 16)
            both = grad_s[r, here, :] * gated_s[r, here, :]
            first_s[here, :LANES] = first_s[here, :LANES] + lanes_sum(both * gain)
            return total + fold8(both * widen(row_s[here, :], width))

        gain_grad[r] = gain_grad[r] + lax.fori_loop(0, slabs, step, jnp.zeros((8, width), F32), unroll=4)
    cross = jnp.sum(first_s[:, :LANES], axis=1, keepdims=True) / total_width
    first_s[:, :LANES] = rescale * rescale * rescale * cross
    for r in range(blocks):
        gain = params[r, 5:6, :]

        def step(i, total, r=r, gain=gain):
            here = rows_at(i * 16, 16)
            g = gate[r, 0, here, :].astype(F32)
            sigma = sigmoid(g)
            d_gated = widen(row_s[here, :], width) * (grad_s[r, here, :] * gain) - gated_s[r, here, :] * widen(
                first_s[here, :LANES], width
            )
            d_sum = d_gated * (g * sigma)
            d_gate[r, 0, here, :] = (d_gated * summed_s[r, here, :] * (sigma * (1.0 + g * (1.0 - sigma)))).astype(BF16)
            low = d_sum.astype(BF16)
            d_summed[r, 0, here, :] = low
            low_s[here, :] = (d_sum * second_s[r, here, :]).astype(BF16)
            return total + fold8(d_sum * acted[r, 0, here, :].astype(F32))

        skip_grad[r] = skip_grad[r] + lax.fori_loop(0, slabs, step, jnp.zeros((8, width), F32), unroll=4)
        pull_s[r] = pull_s[r] + dot_tn(c_part, low_s[...])

    @pl.when(t == pl.num_programs(0) - 1)
    def _():
        survive = jnp.exp(cum_end[0, 7:8, :]) * (ids_after[0, PAD - 1 : PAD, :] == before).astype(F32)
        for r in range(blocks):
            write_message(pulled.at[r, 0], pull_s[r], expand_row(survive, width, r * per_block))


def middle_call(s, mixed, gate, acted, cum, entered, bc, ids, tokens, cotangent, params, weights, per_block, cuts):
    blocks, n, length, width = mixed.shape
    model = tokens.shape[2]
    tile = min(256, length)
    wide = lambda w: pl.BlockSpec((blocks, 1, tile, w), lambda t: (0, s, t, 0))
    wide_out = lambda w: pl.BlockSpec((blocks, 1, tile, w), lambda t: (0, 0, t, 0))
    rows = lambda w: pl.BlockSpec((1, tile, w), lambda t: (s, t, 0))
    one = lambda a: pl.BlockSpec((a.shape[0], 1) + a.shape[2:], lambda t: (0, s, 0, 0), pipeline_mode=pl.Buffered(1))
    whole = lambda a: pl.BlockSpec(a.shape, lambda t: (0,) * a.ndim, pipeline_mode=pl.Buffered(1))
    kept = lambda *shape: pl.BlockSpec(shape, lambda t: (0,) * len(shape))
    piece = LANES // cuts + 16
    edge = lambda a: pl.BlockSpec((1, PAD, LANES), lambda t: (s, a, 0))
    ids_here = ids[:, PAD : PAD + length]
    wide_shape = jax.ShapeDtypeStruct((blocks, 1, length, width), BF16)
    return pl.pallas_call(
        functools.partial(middle_kernel, blocks, per_block, width * blocks),
        grid=(length // tile,),
        in_specs=[
            wide(width), wide(width), wide(width), rows(LANES),
            pl.BlockSpec((1, 8, LANES), lambda t: (s, length // 8 - 1, 0)), rows(2 * LANES), rows(LANES),
            edge(0), edge(length // PAD), rows(model), rows(model), whole(params),
            one(entered),
        ] + [whole(v) for v in weights],
        out_specs=[
            pl.BlockSpec((1, tile, model), lambda t: (0, t, 0)), wide_out(width), wide_out(width), wide_out(width),
            kept(blocks, 1, cuts, piece, width), kept(blocks, 8, width), kept(blocks, 8, width),
        ],
        out_shape=[
            jax.ShapeDtypeStruct((1, length, model), BF16),
            wide_shape, wide_shape, wide_shape,
            jax.ShapeDtypeStruct((blocks, 1, cuts, piece, width), BF16),
            jax.ShapeDtypeStruct((blocks, 8, width), F32),
            jax.ShapeDtypeStruct((blocks, 8, width), F32),
        ],
        scratch_shapes=[
            pltpu.VMEM((blocks, tile, width), F32),
            pltpu.VMEM((blocks, tile, width), F32),
            pltpu.VMEM((blocks, tile, width), F32),
            pltpu.VMEM((tile, width), F32),
            pltpu.VMEM((blocks, tile, width), F32),
            pltpu.VMEM((tile, width), BF16),
            pltpu.VMEM((tile, LANES), F32),
            pltpu.VMEM((blocks, LANES, width), F32),
        ],
        compiler_params=pltpu.CompilerParams(vmem_limit_bytes=VMEM),
        name="middle",
    )(mixed, gate, acted, cum, cum, bc, ids_here, ids, ids, tokens, cotangent, params, entered, *weights)


def inside_back_kernel(
    per_block, acted, d_summed, mixed, bc, ids, id_rows, steps, cum, states, entered, d_scaled, d_b, d_c, d_cum,
    carried, turned,
):
    length, width = acted.shape[2:]
    chunks = length // CHUNK
    g = pl.program_id(0)
    offset = g * per_block
    heads = head_map(width, offset)
    sooner = triangle(False)
    first_before = ids[0, PAD - 1 : PAD, :]
    came = entered[0, 0]

    @pl.when(g == 0)
    def _():
        d_b[...] = jnp.zeros_like(d_b)
        d_c[...] = jnp.zeros_like(d_c)
        d_cum[...] = jnp.zeros_like(d_cum)

    for c in range(chunks - 1, -1, -1):
        here = slice(c * CHUNK, (c + 1) * CHUNK)
        b_part, c_part = bc[0, here, :LANES], bc[0, here, LANES:]
        marks, _, _ = chunk_marks(ids, c)
        same = sooner & (marks == id_rows[0, 0:1, PAD + c * CHUNK : PAD + (c + 1) * CHUNK])
        scores_t = jnp.where(same, dot_nt(b_part, c_part), 0.0)
        value = cum[0, here, :]
        turned[...] = jnp.transpose(value)
        entering, tail, survive = chunk_decays(ids, cum, c)
        scaled = (expand(steps[0, here, :], width, offset) * acted[0, 0, here, :].astype(F32)).astype(BF16)
        grad = d_summed[0, 0, here, :]
        grad_wide = grad.astype(F32)
        from_start = jnp.exp(value) * (marks == first_before).astype(F32)
        start_wide = expand(from_start, width, offset)
        d_c_part = dot_nt((grad_wide * start_wide).astype(BF16), came)
        dots = grad_wide * (mixed[0, 0, here, :] + start_wide * dot(c_part, came))
        if c < chunks - 1:
            held = carried[...]
            held_low = held.astype(BF16)
            tail_wide = expand(tail, width, offset)
            later = dot(b_part, held_low) * tail_wide
            d_b_part = dot_nt((tail_wide * scaled.astype(F32)).astype(BF16), held_low)
        if c:
            entering_grad = (expand(entering, width, offset) * grad_wide).astype(BF16)
            d_c_part = d_c_part + dot_nt(entering_grad, states[0, 0, c - 1])
        d_scores_t = jnp.zeros((CHUNK, CHUNK), F32)
        results = []
        for pair in range(width // LANES):
            lanes = slice(pair * LANES, (pair + 1) * LANES)
            products = dot_nt(lane_halves(scaled[:, lanes]), grad[:, lanes])
            mixing = []
            for half, h in enumerate((2 * pair, 2 * pair + 1)):
                spread = jnp.minimum(turned[pl.ds(offset + h, 1), :] - column(value, offset + h), 0.0)
                decay = jnp.exp(spread)
                mixing.append((scores_t * decay).astype(BF16))
                d_scores_t = d_scores_t + products[half * CHUNK : (half + 1) * CHUNK] * decay
            results.append(dot(jnp.concatenate(mixing, axis=1), lane_halves(grad[:, lanes])))
        result = jnp.concatenate(results, axis=1)
        if c < chunks - 1:
            result = result + later
        d_scaled[0, 0, here, :] = result.astype(BF16)
        d_cum[0, here, :] = d_cum[0, here, :] + by_head(dots - scaled.astype(F32) * result, heads)
        d_scores_t = jnp.where(same, d_scores_t, 0.0).astype(BF16)
        d_b_here = dot(d_scores_t, c_part)
        if c < chunks - 1:
            d_b_here = d_b_here + d_b_part
        d_b[0, here, :] = d_b[0, here, :] + d_b_here
        d_c[0, here, :] = d_c[0, here, :] + d_c_part + dot_tn(d_scores_t, b_part)
        if c:
            pulled = dot_tn(c_part, entering_grad)
            if c < chunks - 1:
                pulled = pulled + held * expand_row(survive, width, offset)[0:1]
            carried[...] = pulled


def inside_back_call(s, acted, d_summed, mixed, bc, ids, id_rows, steps, cum, states, entered, per_block):
    blocks, n, length, width = acted.shape
    four = lambda a, b: pl.BlockSpec((1, 1, a, b), lambda g: (g, s, 0, 0))
    own = lambda a, b: pl.BlockSpec((1, 1, a, b), lambda g: (g, 0, 0, 0))
    per_seq = lambda a: pl.BlockSpec((1,) + a.shape[1:], lambda g: (s, 0, 0))
    summed = pl.BlockSpec((1, length, LANES), lambda g: (0, 0, 0))
    lanes = jax.ShapeDtypeStruct((1, length, LANES), F32)
    return pl.pallas_call(
        functools.partial(inside_back_kernel, per_block),
        grid=(blocks,),
        in_specs=[
            four(length, width), own(length, width), four(length, width), per_seq(bc), per_seq(ids), per_seq(id_rows),
            per_seq(steps), per_seq(cum),
            pl.BlockSpec((1, 1) + states.shape[2:], lambda g: (g, s, 0, 0, 0)),
            four(LANES, width),
        ],
        out_specs=[own(length, width), summed, summed, summed],
        out_shape=[jax.ShapeDtypeStruct((blocks, 1, length, width), BF16), lanes, lanes, lanes],
        scratch_shapes=[pltpu.VMEM((LANES, width), F32), pltpu.VMEM((LANES, LANES), F32)],
        compiler_params=pltpu.CompilerParams(vmem_limit_bytes=VMEM),
        name="inside_back",
    )(acted, d_summed, mixed, bc, ids, id_rows, steps, cum, states, entered)


def close_kernel(
    per_block, rows, acted, d_summed, d_scaled, bc, ids, id_rows, steps, raw, log_decay, cum, d_cum, leaving, entered,
    params, small, state_rows, state_taps, d_b, d_c,
    d_rows, d_raw, d_state, taps_grad, state_taps_grad, small_grad, d_pre, d_acted, d_log, d_step, ends, d_bc, d_pre_bc,
):
    length, width = acted.shape[2:]
    chunks = length // CHUNK
    g = pl.program_id(0)
    offset = g * per_block
    heads = head_map(width, offset)
    last = ids[0, PAD + length - 1 : PAD + length, :]
    before = ids[0, PAD - 1 : PAD, :]
    end = cum[0, length - 1 : length, :]
    skip = params[0, 6:7, :]
    held = leaving[0, 0]
    came = entered[0, 0]

    @pl.when(g == 0)
    def _():
        d_bc[:, :LANES] = d_b[0]
        d_bc[:, LANES:] = d_c[0]
        d_log[...] = d_cum[0]
        d_step[...] = jnp.zeros_like(d_step)
        ends[...] = jnp.zeros_like(ends)

    boundary = jnp.zeros((1, LANES), F32)
    for c in range(chunks):
        here = slice(c * CHUNK, (c + 1) * CHUNK)
        marks, _, _ = chunk_marks(ids, c)
        tail = jnp.exp(end - cum[0, here, :]) * (marks == last).astype(F32)
        tail_wide = expand(tail, width, offset)
        steps_wide = expand(steps[0, here, :], width, offset)
        x = acted[0, 0, here, :].astype(F32)
        scaled = (steps_wide * x).astype(BF16).astype(F32)
        later = dot(bc[0, here, :LANES], held) * tail_wide
        total = d_scaled[0, 0, here, :].astype(F32) + later
        d_acted[here, :] = steps_wide * total + skip * d_summed[0, 0, here, :].astype(F32)
        d_bc[here, :LANES] = d_bc[here, :LANES] + dot_nt((tail_wide * scaled).astype(BF16), held)
        from_later = by_head_low(scaled * later, heads)
        boundary = boundary + jnp.sum(from_later, axis=0, keepdims=True)
        d_log[here, :] = d_log[here, :] - from_later
        d_step[here, :] = d_step[here, :] + by_head_low(x * total, heads)
    product = held.astype(F32) * came.astype(F32)
    product = jnp.sum(product.reshape(LANES // 8, 8, width), axis=0)
    survive = jnp.exp(end) * (last == before).astype(F32)
    boundary = boundary + survive * jnp.sum(by_head(jnp.concatenate([product, product * 0.0], axis=0), heads), axis=0, keepdims=True)
    ends[0:1, :] = ends[0:1, :] + boundary

    def store(here, lanes, value):
        d_rows[0, 0, here, lanes] = value

    sums = conv_backward(
        rows.at[0, 0],
        ids,
        id_rows,
        params[0],
        lambda c, lanes: d_acted[c * CHUNK : (c + 1) * CHUNK, lanes],
        d_pre,
        store,
        length,
    )
    taps_grad[0] = jnp.concatenate(sums + [jnp.zeros((3, width), F32)], axis=0)

    @pl.when(g == pl.num_programs(0) - 1)
    def _():
        rate = jnp.exp(small[1:2, :])
        ones = triangle(False).astype(F32)
        carry = ends[0:1, :]
        decay_sum = jnp.zeros((1, LANES), F32)
        bias_sum = jnp.zeros((1, LANES), F32)
        for c in range(chunks - 1, -1, -1):
            here = slice(c * CHUNK, (c + 1) * CHUNK)
            grads = exact_dot(ones, d_log[here, :]) + carry
            carry = grads[0:1]
            decay_sum = decay_sum + jnp.sum(grads * log_decay[0, here, :], axis=0, keepdims=True)
            value = (d_step[here, :] - grads * rate) * sigmoid(raw[0, here, :] + small[0:1, :])
            bias_sum = bias_sum + jnp.sum(value, axis=0, keepdims=True)
            d_raw[0, here, :] = value.astype(BF16)
        small_grad[...] = jnp.concatenate([bias_sum, decay_sum, jnp.zeros((6, LANES), F32)], axis=0)

        def store_state(here, lanes, value):
            d_state[0, here, lanes] = value

        sums = conv_backward(
            state_rows.at[0],
            ids,
            id_rows,
            state_taps[...],
            lambda c, lanes: d_bc[c * CHUNK : (c + 1) * CHUNK, lanes],
            d_pre_bc,
            store_state,
            length,
        )
        state_taps_grad[...] = jnp.concatenate(sums + [jnp.zeros((3, 2 * LANES), F32)], axis=0)


def close_call(
    s, rows, acted, d_summed, d_scaled, bc, ids, id_rows, steps, raw, log_decay, cum, d_cum, leaving, entered, params,
    small, state_rows, state_taps, d_b, d_c, per_block,
):
    blocks, n, length, width = acted.shape
    four = lambda a, b: pl.BlockSpec((1, 1, a, b), lambda g: (g, s, 0, 0))
    own = lambda a, b: pl.BlockSpec((1, 1, a, b), lambda g: (g, 0, 0, 0))
    per_seq = lambda a: pl.BlockSpec((1,) + a.shape[1:], lambda g: (s, 0, 0))
    kept = lambda *shape: pl.BlockSpec(shape, lambda g: (0,) * len(shape))
    whole = lambda a: kept(*a.shape)
    wide = own(length, width)
    return pl.pallas_call(
        functools.partial(close_kernel, per_block),
        grid=(blocks,),
        in_specs=[
            four(length + PAD, width), four(length, width), wide, wide, per_seq(bc), per_seq(ids), per_seq(id_rows),
            per_seq(steps), per_seq(raw), per_seq(log_decay), per_seq(cum), kept(1, length, LANES), own(LANES, width),
            four(LANES, width),
            pl.BlockSpec((1,) + params.shape[1:], lambda g: (g, 0, 0)), whole(small), per_seq(state_rows),
            whole(state_taps), whole(d_b), whole(d_c),
        ],
        out_specs=[
            own(length + PAD, width), kept(1, length, LANES), kept(1, length + PAD, 2 * LANES),
            pl.BlockSpec((1, 8, width), lambda g: (g, 0, 0)), kept(8, 2 * LANES), kept(8, LANES),
        ],
        out_shape=[
            jax.ShapeDtypeStruct((blocks, 1, length + PAD, width), BF16),
            jax.ShapeDtypeStruct((1, length, LANES), BF16),
            jax.ShapeDtypeStruct((1, length + PAD, 2 * LANES), BF16),
            jax.ShapeDtypeStruct((blocks, 8, width), F32),
            jax.ShapeDtypeStruct((8, 2 * LANES), F32),
            jax.ShapeDtypeStruct((8, LANES), F32),
        ],
        scratch_shapes=[
            pltpu.VMEM((length + 2 * PAD, width), BF16),
            pltpu.VMEM((length, width), F32),
            pltpu.VMEM((length, LANES), F32),
            pltpu.VMEM((length, LANES), F32),
            pltpu.VMEM((8, LANES), F32),
            pltpu.VMEM((length, 2 * LANES), F32),
            pltpu.VMEM((length + 2 * PAD, 2 * LANES), BF16),
        ],
        compiler_params=pltpu.CompilerParams(vmem_limit_bytes=VMEM),
        name="close",
    )(
        rows, acted, d_summed, d_scaled, bc, ids, id_rows, steps, raw, log_decay, cum, d_cum, leaving, entered, params,
        small, state_rows, state_taps, d_b, d_c,
    )


def input_kernel(blocks, d_raw, d_state, tokens, cotangent, gain, state_w, step_w, d_gate, d_rows, *refs):
    row_weights, refs = refs[:blocks], refs[blocks:]
    gate_weights, refs = refs[:blocks], refs[blocks:]
    input_grad, edge, halo, gain_grad, main_s, halo_s, weights_s, gate_s, rows_s, sems = refs
    length = d_gate.shape[2]
    copies = []
    for r in range(blocks):
        moves = [(row_weights[r], weights_s.at[2 * r]), (d_rows.at[r, 0], rows_s.at[r])]
        moves += [(gate_weights[r], weights_s.at[2 * r + 1]), (d_gate.at[r, 0], gate_s.at[r])]
        copies.append([pltpu.make_async_copy(a, b, sems.at[4 * r + i]) for i, (a, b) in enumerate(moves)])
        for copy in copies[r]:
            copy.start()
    total = dot_nt(d_state[0], state_w[...])
    halo_s[...] = total[:PAD]
    main_s[...] = total[PAD:] + dot(d_raw[0], step_w[...])
    for r in range(blocks):
        copies[r][0].wait()
        copies[r][1].wait()
        halo_s[...] = halo_s[...] + dot_nt(rows_s[r, :PAD, :], weights_s[2 * r])
        part = dot_nt(rows_s[r, PAD:, :], weights_s[2 * r])
        copies[r][2].wait()
        copies[r][3].wait()
        main_s[...] = main_s[...] + (part + dot_nt(gate_s[r], weights_s[2 * r + 1]))

    def norm_back(value, token):
        scale = lax.rsqrt(jnp.mean(token * token, axis=1, keepdims=True) + EPS)
        unit = value * gain[...]
        inner = jnp.mean(unit * token, axis=1, keepdims=True)
        return scale * unit - token * (scale * scale * scale * inner), fold8(value * token * scale)

    grad, sums = norm_back(halo_s[...], tokens[0, :PAD, :].astype(F32))
    halo[0] = grad.astype(BF16)

    def step(i, carry):
        here = rows_at(i * 16, 16)
        grad, more = norm_back(main_s[here, :], tokens[0, rows_at(PAD + i * 16, 16), :].astype(F32))
        value = grad + cotangent[0, here, :].astype(F32)
        edge[0] = value
        input_grad[0, here, :] = value.astype(BF16)
        return carry + more

    gain_grad[...] = lax.fori_loop(0, length // 16, step, sums, unroll=4)


def input_call(s, d_gate, d_rows, d_raw, d_state, tokens, cotangent, gain, state_w, step_w, row_weights, gate_weights):
    blocks, _, length, width = d_gate.shape
    padded, model = tokens.shape[1:]
    whole = lambda a: pl.BlockSpec(a.shape, lambda t: (0,) * a.ndim, pipeline_mode=pl.Buffered(1))
    one = lambda a, b: pl.BlockSpec((1, a, b), lambda t: (s, 0, 0), pipeline_mode=pl.Buffered(1))
    kept = lambda *shape: pl.BlockSpec(shape, lambda t: (0,) * len(shape), pipeline_mode=pl.Buffered(1))
    return pl.pallas_call(
        functools.partial(input_kernel, blocks),
        grid=(1,),
        in_specs=[
            whole(d_raw), whole(d_state), one(padded, model), one(length, model), whole(gain), whole(state_w), whole(step_w),
        ] + [pl.BlockSpec(memory_space=pl.ANY)] * (2 + 2 * blocks),
        out_specs=[kept(1, length, model), kept(1, PAD, model), kept(1, PAD, model), kept(8, model)],
        out_shape=[
            jax.ShapeDtypeStruct((1, length, model), BF16),
            jax.ShapeDtypeStruct((1, PAD, model), F32),
            jax.ShapeDtypeStruct((1, PAD, model), BF16),
            jax.ShapeDtypeStruct((8, model), F32),
        ],
        scratch_shapes=[
            pltpu.VMEM((length, model), F32),
            pltpu.VMEM((PAD, model), F32),
            pltpu.VMEM((2 * blocks, model, width), BF16),
            pltpu.VMEM((blocks, length, width), BF16),
            pltpu.VMEM((blocks, padded, width), BF16),
            pltpu.SemaphoreType.DMA((4 * blocks,)),
        ],
        compiler_params=pltpu.CompilerParams(vmem_limit_bytes=VMEM),
        name="input_gradient",
    )(d_raw, d_state, tokens, cotangent, gain, state_w, step_w, d_gate, d_rows, *row_weights, *gate_weights)


def assemble_kernel(count, places, *refs):
    parts, refs = refs[:count], refs[count:]
    edges, refs = (refs[:count], refs[count:]) if len(refs) > 2 * count else ((), refs)
    whole, buffers, (in_sem, out_sem) = refs[0], refs[1:-2], refs[-2:]
    length = parts[0].shape[1]
    reads = [pltpu.make_async_copy(p.at[0], b, in_sem.at[i]) for i, (p, b) in enumerate(zip(parts, buffers))]
    writes = [pltpu.make_async_copy(b, whole.at[places[i]], out_sem.at[i]) for i, b in enumerate(buffers)]
    for read in reads:
        read.start()
    for i, (read, write) in enumerate(zip(reads, writes)):
        read.wait()
        if edges:
            buffers[i][length - PAD :, :] = edges[i][0]
        write.start()
    for write in writes:
        write.wait()


def assemble(parts, edges, places):
    count = len(parts)
    _, length, model = parts[0].shape
    return pl.pallas_call(
        functools.partial(assemble_kernel, count),
        grid_spec=pltpu.PrefetchScalarGridSpec(
            num_scalar_prefetch=1,
            grid=(1,),
            in_specs=[pl.BlockSpec(memory_space=pl.ANY) for _ in parts]
            + [pl.BlockSpec((1, PAD, model), lambda t, i: (0, 0, 0)) for _ in edges],
            out_specs=pl.BlockSpec(memory_space=pl.ANY),
            scratch_shapes=[pltpu.VMEM((length, model), BF16) for _ in parts]
            + [pltpu.SemaphoreType.DMA((count,)), pltpu.SemaphoreType.DMA((count,))],
        ),
        out_shape=jax.ShapeDtypeStruct((count, length, model), BF16),
        compiler_params=pltpu.CompilerParams(vmem_limit_bytes=VMEM),
        name="assemble",
    )(jnp.stack(places).astype(jnp.int32), *parts, *edges)


def weight_grad_kernel(n, halo, rows, *refs):
    grads, (kept, sent) = refs[:n], refs[n:]
    odd = pl.program_id(0) % 2 == 1
    start = PAD if halo else 0
    length = grads[0].shape[2] - start
    skip = rows.shape[1] - length
    total = None
    if halo:
        before = jnp.concatenate([rows[s, :PAD, :] for s in range(n)], axis=0)
        total = dot_tn(before, jnp.concatenate([grad[0, 0, :PAD, :] for grad in grads], axis=0))
    for s in range(n):
        part = dot_tn(rows[s, skip:, :], grads[s][0, 0, start:, :])
        total = part if total is None else total + part
    total = total.astype(BF16)

    @pl.when(odd)
    def _():
        sent[0] = total

    @pl.when(jnp.logical_not(odd))
    def _():
        kept[0] = total


def weight_grad(values, grads):
    n, padded, model = values.shape
    blocks, _, tokens, width = grads[0].shape
    return pl.pallas_call(
        functools.partial(weight_grad_kernel, n, tokens % CHUNK != 0),
        grid=(blocks,),
        in_specs=[pl.BlockSpec(values.shape, lambda g: (0, 0, 0), pipeline_mode=pl.Buffered(1))]
        + [pl.BlockSpec((1, 1, tokens, width), lambda g: (g, 0, 0, 0)) for _ in grads],
        out_specs=[pl.BlockSpec((1, model, width), lambda g: (g // 2, 0, 0))] * 2,
        out_shape=[jax.ShapeDtypeStruct((blocks // 2, model, width), BF16)] * 2,
        compiler_params=pltpu.CompilerParams(vmem_limit_bytes=VMEM),
        name="weight_gradient",
    )(values, *grads)


def state_grad_kernel(n, values, *refs):
    states, (out,) = refs[:n], refs[n:]
    total = dot_tn(values[0], states[0][0])
    for s in range(1, n):
        total = total + dot_tn(values[s], states[s][0])
    out[...] = total.astype(BF16)


def state_grad(values, states):
    return pl.pallas_call(
        functools.partial(state_grad_kernel, len(states)),
        out_shape=jax.ShapeDtypeStruct((values.shape[2], states[0].shape[2]), BF16),
        compiler_params=pltpu.CompilerParams(vmem_limit_bytes=VMEM),
        name="state_weight_gradient",
    )(values, *states)


def pack_kernel(n, per_block, values, *refs):
    groups, outs = [refs[i * n : (i + 1) * n] for i in range(7)], refs[7 * n :]
    steps, taps, state_taps, rest, gains, skips, norms = groups
    add = lambda refs, *at: functools.reduce(lambda a, b: a + b, [ref[at] for ref in refs])
    column_sum = lambda value: jnp.sum(value, axis=0, keepdims=True)
    step = dot_tn(steps[0][0], values[0, PAD:, :])
    for s in range(1, n):
        step = step + dot_tn(steps[s][0], values[s, PAD:, :])
    model = step.shape[1]
    width = outs[0].shape[1]
    norm = column_sum(add(norms, Ellipsis))
    rest = add(rest, Ellipsis)
    state = add(state_taps, Ellipsis)
    for r, out in enumerate(outs):
        out[...] = jnp.zeros_like(out)
        out[0:5, :] = add(taps, r)[0:5]
        out[5:6, :] = column_sum(add(gains, r))
        out[6:7, :] = column_sum(add(skips, r))
        mine = pltpu.roll(rest, (LANES - r * per_block) % LANES, 1) if r else rest
        out[7:8, :LANES] = mine[0:1]
        out[7:8, LANES : 2 * LANES] = mine[1:2]
        row = 8
        for q in range(0, model, width):
            out[row : row + per_block, :] = step[r * per_block : (r + 1) * per_block, q : q + width]
            row += per_block
        for q in range(0, model, width):
            out[row : row + 1, :] = norm[:, q : q + width]
            row += 1
        out[row : row + 5, : 2 * LANES] = state[0:5]


def pack_sums(values, width, per_block, blocks, *groups):
    n, _, model = values.shape
    rows = 8 + per_block * (model // width) + model // width + 5
    return pl.pallas_call(
        functools.partial(pack_kernel, n, per_block),
        out_shape=[jax.ShapeDtypeStruct((-(-rows // 8) * 8, width), F32)] * blocks,
        compiler_params=pltpu.CompilerParams(vmem_limit_bytes=VMEM),
        name="pack",
    )(values, *[v for group in groups for v in group])


def unpack_kernel(packed, norm, steps, taps, state_taps, params, gains):
    heads, width = params.shape[1], packed.shape[1]
    model = steps.shape[1]
    taps[...] = packed[0:5, :]
    for k in range(width // LANES):
        gains[k : k + 1, :] = packed[5:6, k * LANES : (k + 1) * LANES]
    params[0:1, :] = packed[7:8, :heads]
    params[1:2, :] = packed[7:8, LANES : LANES + heads]
    skips = packed[6:7, :]
    lane = lax.broadcasted_iota(jnp.int32, (heads, width), 1)
    head = lax.broadcasted_iota(jnp.int32, (heads, width), 0)
    mine = lax.shift_right_logical(lane, 6) == head
    column = jnp.sum(jnp.where(mine, skips, 0.0), axis=1, keepdims=True)
    params[2:3, :] = jnp.transpose(jnp.broadcast_to(column, (heads, LANES)))[0:1, :]
    row = 8
    for q in range(0, model, width):
        steps[:, q : q + width] = packed[row : row + heads, :]
        row += heads
    for k in range(model // LANES):
        at = k * LANES
        norm[k : k + 1, :] = packed[row + at // width : row + at // width + 1, at % width : at % width + LANES]
    row += model // width
    state_taps[...] = packed[row : row + 5, : 2 * LANES]


def unpack_sums(packed, heads, model):
    width = packed.shape[1]
    shapes = [(model // LANES, LANES), (heads, model), (5, width), (5, 2 * LANES), (3, heads), (width // LANES, LANES)]
    return pl.pallas_call(
        unpack_kernel, out_shape=[jax.ShapeDtypeStruct(shape, F32) for shape in shapes], name="unpack"
    )(packed)


def swapped(value, axis, step):
    return lax.ppermute(value, axis, [(i, i ^ step) for i in range(lax.axis_size(axis))])


def reached(value):
    return {r: swapped(value, "head", r) if r else value for r in [0, 1] + list(range(2, lax.axis_size("head"), 2))}


def forwarded(parts):
    rest = {r + 1: swapped(parts[r], "head", 1) for r in parts if r and r % 2 == 0}
    return [{**parts, **rest}[r] for r in range(lax.axis_size("head"))]


def gathered(value):
    return forwarded(reached(value))


def crossed(value):
    return {r: swapped(value, "head", r) if r else value for r in range(0, lax.axis_size("head"), 2)}


def completed(parts):
    rest = {r + 1: swapped(part, "head", 1) for r, part in parts.items()}
    return [{**parts, **rest}[r] for r in range(lax.axis_size("head"))]


def bits_of(axis):
    return [1 << i for i in range((lax.axis_size(axis) - 1).bit_length())]


def added(a, b, dtype=None):
    return (a.astype(F32) + b.astype(F32)).astype(dtype or a.dtype)


def tree_sum(values):
    while len(values) > 1:
        values = [a + b for a, b in zip(values[::2], values[1::2])]
    return values[0]


def head_sum(value, bits):
    for bit in reversed(bits):
        half = value.shape[0] // 2
        arrived = yield value[half:], "head", bit
        value = added(value[:half], arrived)
    return value[0]


def ranges_sum(value):
    ranges = lax.axis_size("seq")
    me = lax.axis_index("seq")
    lead, rest = value.shape[0], value.shape[2:]
    piece = (value.shape[1] // ranges,) + rest
    for bit in bits_of("seq"):
        mine = (me // bit) % 2
        halves = value.reshape((lead, ranges // bit // 2, 2) + piece)
        arrived = yield lax.dynamic_index_in_dim(halves, 1 - mine, 2, keepdims=False), "seq", bit
        kept = lax.dynamic_index_in_dim(halves, mine, 2, keepdims=False)
        value = added(kept, arrived, F32 if 2 * bit == ranges else value.dtype)
    return value.reshape((lead,) + piece)


def weight_sum(kept, sent, ranges_first):
    arrived = yield sent, "head", 1
    value = added(kept, arrived)
    bits = bits_of("head")[1:]
    if ranges_first:
        value = yield from ranges_sum(value)
        return (yield from head_sum(value, bits))
    value = yield from head_sum(value, bits)
    return (yield from ranges_sum(value[None]))[0]


def sum_of_state(value):
    for bit in bits_of("head"):
        arrived = yield value, "head", bit
        value = added(value, arrived)
    return (yield from ranges_sum(value[None]))[0]


class Chain(Held):
    def __init__(self, steps):
        super().__init__()
        self.steps, self.done = steps, False
        self.advance()

    def advance(self):
        if self.done:
            return
        try:
            self.value = swapped(*self.steps.send(self.value))
        except StopIteration as end:
            self.value, self.done = end.value, True

    def finish(self):
        while not self.done:
            self.advance()
        return self.value


def assembled(parts, edges=None):
    n = len(parts)
    me = lax.axis_index("head")
    pieces, places, last_rows = [], [], []
    for s in range(n):
        for r, part in enumerate(parts[s]):
            pieces.append(part)
            places.append((me ^ r) * n + s)
            if edges is not None:
                last_rows.append(edges[r][s : s + 1])
    return assemble(pieces, last_rows, places)


def padded_lanes(value, size):
    return jnp.pad(value, ((0, 0), (0, size - value.shape[1])))


def shards(
    tokens,
    doc_ids,
    norm_gain,
    head_input_weight,
    state_input_weight,
    timestep_input_weight,
    conv_x,
    conv_state,
    head_params,
    gated_gain,
    output_weight,
    cotangent,
):
    seqs, length, model = tokens.shape
    blocks = lax.axis_size("head")
    ranges = lax.axis_size("seq")
    n = seqs // blocks
    width = gated_gain.shape[0]
    heads = head_params.shape[1]
    me = lax.axis_index("head")
    tokens = lax.dynamic_slice_in_dim(tokens, me * n, n, 0)
    cotangent = lax.dynamic_slice_in_dim(cotangent, me * n, n, 0)
    before = lax.ppermute(tokens[:, length - PAD :], "seq", [(i, i + 1) for i in range(ranges - 1)])
    padded = jnp.concatenate([before, tokens], axis=1)

    start = lax.axis_index("seq") * length
    lead = jnp.concatenate(
        [jnp.full((seqs, PAD), -1, jnp.int32), doc_ids, jnp.full((seqs, PAD), -2, jnp.int32)], axis=1
    )
    ids = lax.dynamic_slice(lead, (me * n, start), (n, length + 2 * PAD)).astype(F32)
    id_rows = jnp.broadcast_to(ids[:, None], (n, 8, length + 2 * PAD))
    ids = jnp.broadcast_to(ids[:, :, None], (n, length + 2 * PAD, LANES))

    pack = jnp.concatenate(
        [
            conv_x,
            gated_gain[None],
            padded_lanes(head_params, width),
            jnp.transpose(timestep_input_weight).astype(F32).reshape(heads * model // width, width),
        ],
        axis=0,
    )
    half = blocks // 2
    packs, side = lax.optimization_barrier((reached(pack), head_input_weight.reshape(model, 2 * width)))
    packs = forwarded(packs)
    row_parts = reached(side[:, width:])
    packed = lambda rows: jnp.pad(jnp.concatenate(rows, axis=1), ((0, 0), (0, LANES - heads * blocks)))
    small = jnp.pad(packed([v[6:9, :heads] for v in packs]), ((0, 5), (0, 0)))
    step_weights = jnp.pad(
        jnp.concatenate([v[9:].reshape(heads, model) for v in packs]).astype(BF16), ((0, LANES - heads * blocks), (0, 0))
    )
    params = jnp.stack(
        [
            jnp.concatenate([v[:6], jnp.repeat(v[8, :heads], HEAD_DIM)[None], jnp.zeros((1, width), F32)], axis=0)
            for v in packs
        ]
    )
    state_taps = jnp.pad(conv_state, ((0, 3), (0, 0)))

    tok_float = padded.astype(F32)
    scale = lax.rsqrt(jnp.mean(tok_float * tok_float, axis=-1, keepdims=True) + EPS)
    normed = (tok_float * scale * norm_gain).astype(BF16)
    rows, raw, steps, log_decay, cum, state_rows, bc = project_first(
        normed, state_input_weight, step_weights, small, ids, id_rows, state_taps, [row_parts[0], row_parts[1]], blocks,
        heads * blocks,
    )
    row_parts, rows, gate_own, out_own = lax.optimization_barrier(
        (row_parts, rows, side[:, :width], output_weight)
    )
    row_weights = forwarded(row_parts)
    cuts = ranges // (blocks * n)
    held = state_call(rows, bc, ids, id_rows, steps, cum, params, (), 0, 2, heads, cuts)
    held, rows = lax.optimization_barrier((held, rows))
    acted, message = held
    for r in range(2, blocks, 2):
        rows = project_more(normed, rows, row_weights[r : r + 2], r)
        acted, message = state_call(rows, bc, ids, id_rows, steps, cum, params, (acted, message), r, 2, heads, cuts)
    mixed, states = inside_call(acted, bc, ids, id_rows, steps, cum, heads)
    mixed, arrived = Held(mixed), Held(send_message(message))
    meet(arrived, mixed)
    entered = Held(send_back(relay(arrived.value, False), blocks, n))
    gate_weights = gathered(gate_own)
    out_weights = gathered(out_own)
    gate = Held(project_gate(normed, gate_weights))
    meet(entered, gate)

    cuts = ranges // blocks
    every = range(n)
    outs, normed_outs, d_gates, d_sums, messages, gain_parts, skip_parts = [[] for _ in range(7)]
    for s in every:
        parts = middle_call(
            s, mixed.value, gate.value, acted, cum, entered.value, bc, ids, tokens, cotangent, params, out_weights, heads,
            cuts,
        )
        for held, part in zip((outs, normed_outs, d_gates, d_sums, messages), parts):
            held.append(Held(part))
        gain_parts.append(parts[5])
        skip_parts.append(parts[6])
        meet(entered, messages[s])
    for out in outs:
        out.value = crossed(out.value)
    d_scaled, insides, leaving, d_rows, d_raws, d_states, closes = [[] for _ in range(7)]

    def inside_back():
        s = len(d_scaled)
        part, *rest = inside_back_call(
            s, acted, d_sums[s].value, mixed.value, bc, ids, id_rows, steps, cum, states, entered.value, heads
        )
        d_scaled.append(Held(part))
        insides.append(rest)

    def close():
        s = len(d_rows)
        d_b, d_c, d_cum = insides[s]
        parts = close_call(
            s, rows, acted, d_sums[s].value, d_scaled[s].value, bc, ids, id_rows, steps, raw, log_decay, cum, d_cum,
            leaving[s].value, entered.value, params, small, state_rows, state_taps, d_b, d_c, heads,
        )
        for held, part in zip((d_rows, d_raws, d_states), parts):
            held.append(Held(part))
        closes.append(parts[3:])

    for s in every:
        arrived = Held(send_message(messages[s].value))
        if s:
            inside_back()
            meet(arrived, d_scaled[s], out_sum, gate_sum)
        else:
            meet(arrived, *messages[1:])
        carried = Held(relay(arrived.value, True))
        if s:
            out_sum.advance()
            meet(carried, leaving[s - 1])
        else:
            meet(carried, d_sums[0], *normed_outs, *d_gates)
        leaving.append(Held(send_back(carried.value, blocks, 1)))
        if s:
            close()
            meet(leaving[s], d_rows[s - 1], out_sum)
            out_sum.advance()
            gate_sum.advance()
        else:
            inside_back()
            out_grads = Held(weight_grad(cotangent, values(normed_outs)))
            gate_grads = Held(weight_grad(normed, values(d_gates)))
            meet(leaving[0], d_scaled[0], out_grads, gate_grads, *outs, *messages[1:], *d_sums[1:])
            out_sum = Chain(weight_sum(*out_grads.value, False))
            gate_sum = Chain(weight_sum(*gate_grads.value, False))
    close()
    meet(d_rows[-1], out_sum)
    out_sum.advance()

    state_part = Held(state_grad(normed, values(d_states)))
    meet(state_part, *d_rows)
    state_sum = Chain(sum_of_state(state_part.value))
    rows_grads = Held(weight_grad(normed, values(d_rows)))
    gain = Held(norm_gain[None])
    meet(rows_grads, out_sum, gate_sum, gain, state_sum)
    for chain in (out_sum, gate_sum, state_sum):
        chain.advance()
    rows_sum = Chain(weight_sum(*rows_grads.value, True))
    meet(rows_sum, gain)
    rows_sum.advance()
    inputs, edges, halos, norm_parts = [], [], [], []
    for s in every:
        *parts, norm_part = input_call(
            s, d_gates[s].value, d_rows[s].value, d_raws[s].value, d_states[s].value, padded, cotangent, gain.value,
            state_input_weight, step_weights, row_weights, gate_weights,
        )
        for held, part in zip((inputs, edges, halos), parts):
            held.append(Held(part))
        norm_parts.append(norm_part)
        if s < n - 1:
            meet(gain, inputs[s], gate_sum, out_sum, state_sum)
            gate_sum.advance()
            out_sum.advance()
            state_sum.advance()
            inputs[s].value = crossed(inputs[s].value)
    meet(inputs[-1], rows_sum, state_sum, gate_sum, *halos, *edges, *outs)
    for chain in (rows_sum, state_sum, gate_sum):
        chain.advance()
    inputs[-1].value = crossed(inputs[-1].value)
    smalls = pack_sums(
        normed, width, heads, blocks, values(d_raws), *[[c[i] for c in closes] for i in range(3)], gain_parts, skip_parts,
        norm_parts,
    )
    halo = Held(lax.ppermute(jnp.concatenate(values(halos), axis=0), "seq", [(i + 1, i) for i in range(ranges - 1)]))
    own = Held(list(smalls))
    meet(own, *inputs[:-1])
    own.value = [swapped(part, "head", r) if r else part for r, part in enumerate(own.value)]
    output = Held(assembled([completed(part) for part in values(outs)]))
    meet(own, output)
    own.value = tree_sum(own.value)
    steps = bits_of("seq")
    for i, bit in enumerate(steps):
        came = Held(swapped(own.value, "seq", bit))
        also = [gate_sum, halo] if i == 0 else inputs if i == 1 else [whole_input] if i == 2 else []
        meet(came, own, rows_sum, state_sum, *also)
        for chain in (rows_sum, state_sum):
            chain.advance()
        own.value = own.value + came.value
        if i == 0:
            gate_sum.advance()
            edge = crossed(added(jnp.concatenate(values(edges), axis=0), halo.value, BF16))
        if i == 1:
            whole_input = Held(assembled([completed(part) for part in values(inputs)], completed(edge)))
    out_grad = jnp.transpose(out_sum.finish())
    both = own.value
    norm_grad, steps_grad, taps_grad, state_taps_grad, params_grad, gains_grad = unpack_sums(both, heads, model)
    return (
        output.value,
        whole_input.value,
        norm_grad.reshape(model),
        jnp.stack([gate_sum.finish(), rows_sum.finish()], axis=1),
        state_sum.finish(),
        jnp.transpose(steps_grad),
        taps_grad,
        state_taps_grad,
        params_grad,
        gains_grad.reshape(width),
        out_grad,
    )


def solution(mesh):
    return jax.shard_map(
        shards,
        mesh=mesh,
        in_specs=(
            P(None, "seq", None),
            P(),
            P(),
            P(None, None, "head"),
            P(),
            P(None, "head"),
            P(None, "head"),
            P(),
            P(None, "head"),
            P("head"),
            P("head", None),
            P(None, "seq", None),
        ),
        out_specs=(
            P(None, "seq", None),
            P(None, "seq", None),
            P(),
            P("seq", None, "head"),
            P("seq", None),
            P(None, "head"),
            P(None, "head"),
            P(),
            P(None, "head"),
            P("head"),
            P("head", "seq"),
        ),
        check_vma=False,
    )
```

```python
import functools

import jax
import jax.numpy as jnp
from jax import lax
from jax.experimental import pallas as pl
from jax.experimental.pallas import tpu as pltpu
from jax.sharding import PartitionSpec as P

F32 = jnp.float32
BF16 = jnp.bfloat16
EPS = 1e-5
CHUNK = 128
PAD = 16
LANES = 128
HEAD_DIM = 64
VMEM = 60 * 1024 * 1024


def dot(a, b):
    return lax.dot_general(a, b, (((1,), (0,)), ((), ())), preferred_element_type=F32)


def dot_nt(a, b):
    return lax.dot_general(a, b, (((1,), (1,)), ((), ())), preferred_element_type=F32)


def dot_tn(a, b):
    return lax.dot_general(a, b, (((0,), (0,)), ((), ())), preferred_element_type=F32)


def split(value):
    high = value.astype(BF16)
    return high, (value - high.astype(F32)).astype(BF16)


def head_map(width, offset):
    lane = lax.broadcasted_iota(jnp.int32, (LANES, width), 1)
    row = lax.broadcasted_iota(jnp.int32, (LANES, width), 0)
    return (lax.shift_right_logical(lane, 6) + offset == row).astype(F32).astype(BF16)


def expand(value, width, offset):
    lane = lax.shift_right_logical(lax.broadcasted_iota(jnp.int32, value.shape, 1), 6) + offset
    return jnp.concatenate(
        [jnp.take_along_axis(value, lane + 2 * p, axis=1) for p in range(width // LANES)], axis=1
    )


def expand_row(value, width, offset):
    return expand(jnp.broadcast_to(value, (8, LANES)), width, offset)


def column(value, index):
    return jnp.take_along_axis(value, jnp.zeros(value.shape, jnp.int32) + index, axis=1)


def by_head(value, heads):
    high, low = split(value)
    return dot_nt(high, heads) + dot_nt(low, heads)


def by_head_low(value, heads):
    return dot_nt(value.astype(BF16), heads)


def widen(value, width):
    return jnp.concatenate([value] * (width // LANES), axis=1)


def fold8(value):
    return value[0:8] + value[8:16]


def sigmoid(value):
    return 0.5 * jnp.tanh(0.5 * value) + 0.5


def triangle(lower):
    row = lax.broadcasted_iota(jnp.int32, (CHUNK, CHUNK), 0)
    column = lax.broadcasted_iota(jnp.int32, (CHUNK, CHUNK), 1)
    return (row >= column if lower else row <= column)


def exact_dot(ones, value):
    return jnp.dot(ones, value, precision=lax.Precision.HIGHEST, preferred_element_type=F32)


def rows_at(start, count):
    return pl.ds(pl.multiple_of(start, 16), count)


def entering_maps(columns, rows, first, count):
    window = count + PAD
    token = lax.broadcasted_iota(jnp.int32, (count, window), 0)
    entry = lax.broadcasted_iota(jnp.int32, (count, window), 1)
    same = wide_marks(columns[0, first : first + count, :], window) == rows[0, 0:1, first - PAD : first + count]
    distance = entry - token
    return jnp.concatenate(
        [jnp.where(same & (distance == PAD - 3 + k), 1.0, 0.0).astype(BF16) for k in range(3)], axis=0
    )


def leaving_maps(columns, rows, first, count):
    window = count + PAD
    row = lax.broadcasted_iota(jnp.int32, (count, window), 0)
    token = lax.broadcasted_iota(jnp.int32, (count, window), 1)
    same = wide_marks(columns[0, first : first + count, :], window) == rows[0, 0:1, first : first + window]
    distance = token - row
    return jnp.concatenate(
        [jnp.where(same & (distance == 3 - k), 1.0, 0.0).astype(BF16) for k in range(3)], axis=0
    )


def wide_marks(columns, window):
    whole = jnp.concatenate([columns] * -(-window // LANES), axis=1)
    return whole[:, :window]


def conv_sum(rows, maps, taps, first, lanes):
    moved = dot(maps, rows[first - PAD : first + CHUNK, lanes])
    entering = [moved[k * CHUNK : (k + 1) * CHUNK] for k in range(3)]
    entering.append(rows[first : first + CHUNK, lanes].astype(F32))
    total = taps[4:5, lanes]
    for k in range(4):
        total = total + taps[k : k + 1, lanes] * entering[k]
    return total, entering


def lane_groups(width):
    step = min(width, 2 * LANES)
    return [slice(i, i + step) for i in range(0, width, step)]


def conv_forward(rows, ids, id_rows, taps, store, length):
    for c in range(length // CHUNK):
        first = PAD + c * CHUNK
        maps = entering_maps(ids, id_rows, first, CHUNK)
        for lanes in lane_groups(rows.shape[1]):
            total, _ = conv_sum(rows, maps, taps, first, lanes)
            store(slice(c * CHUNK, (c + 1) * CHUNK), lanes, (total * sigmoid(total)).astype(BF16))


def conv_backward(rows, ids, id_rows, taps, d_acted, d_pre, d_rows, length):
    width = d_pre.shape[1]
    zero = jnp.zeros((16, width), BF16)
    d_pre[0:16, :] = zero
    d_pre[length + PAD : length + PAD + 16, :] = zero
    groups = lane_groups(width)
    sums = [[jnp.zeros((8, g.stop - g.start), F32) for _ in range(5)] for g in groups]
    for c in range(length // CHUNK - 1, -1, -1):
        first = PAD + c * CHUNK
        here = slice(first, first + CHUNK)
        maps = entering_maps(ids, id_rows, first, CHUNK)
        back = leaving_maps(ids, id_rows, first, CHUNK)
        for i, lanes in enumerate(groups):
            total, entering = conv_sum(rows, maps, taps, first, lanes)
            sigma = sigmoid(total)
            grad = d_acted(c, lanes) * (sigma * (1.0 + total * (1.0 - sigma)))
            d_pre[here, lanes] = grad.astype(BF16)
            for k in range(5):
                product = grad * entering[k] if k < 4 else grad
                sums[i][k] = sums[i][k] + jnp.sum(product.reshape(CHUNK // 8, 8, -1), axis=0)
            moved = dot(back, d_pre[first : first + CHUNK + PAD, lanes])
            result = taps[3:4, lanes] * grad
            for k in range(3):
                result = result + taps[k : k + 1, lanes] * moved[k * CHUNK : (k + 1) * CHUNK]
            d_rows(here, lanes, result.astype(BF16))
    back = leaving_maps(ids, id_rows, 0, PAD)
    for lanes in groups:
        moved = dot(back, d_pre[0 : 2 * PAD, lanes])
        result = taps[0:1, lanes] * moved[0:PAD]
        for k in range(1, 3):
            result = result + taps[k : k + 1, lanes] * moved[k * PAD : (k + 1) * PAD]
        d_rows(slice(0, PAD), lanes, result.astype(BF16))
    return [
        jnp.concatenate([jnp.sum(part[k], axis=0, keepdims=True) for part in sums], axis=1) for k in range(5)
    ]


def softplus(value):
    return jnp.maximum(value, 0.0) + jnp.log1p(jnp.exp(-jnp.abs(value)))


def arrange_kernel(heads, *refs):
    packs, (small, steps, params) = refs[:-3], refs[-3:]
    blocks, _, width = params.shape
    model = steps.shape[1]
    lane = lax.broadcasted_iota(jnp.int32, (8, LANES), 1)
    values = jnp.zeros((8, LANES), F32)
    rows = []
    for r, pack in enumerate(packs):
        own = jnp.concatenate([pack[6:9, :LANES], jnp.zeros((5, LANES), F32)], axis=0)
        placed = pltpu.roll(own, r * heads, 1) if r else own
        values = jnp.where((lane >= r * heads) & (lane < (r + 1) * heads), placed, values)
        skip = expand(jnp.broadcast_to(pack[8:9, :LANES], (8, LANES)), width, 0)[0:1]
        params[r] = jnp.concatenate([pack[0:6, :], skip, jnp.zeros((1, width), F32)], axis=0)
        rows.append(
            jnp.concatenate([pack[9 + q * heads : 9 + (q + 1) * heads, :] for q in range(model // width)], axis=1)
        )
    rows.append(jnp.zeros((LANES - blocks * heads, model), F32))
    small[...] = values
    steps[...] = jnp.concatenate(rows, axis=0).astype(BF16)


def arrange(packs, heads, model):
    width = packs[0].shape[1]
    return pl.pallas_call(
        functools.partial(arrange_kernel, heads),
        out_shape=[
            jax.ShapeDtypeStruct((8, LANES), F32),
            jax.ShapeDtypeStruct((LANES, model), BF16),
            jax.ShapeDtypeStruct((len(packs), 8, width), F32),
        ],
        name="arrange",
    )(*packs)


def project_rows(values, weights, rows):
    for r, weight in enumerate(weights):
        rows[r, 0] = dot(values, weight[...]).astype(BF16)


def project_first_kernel(blocks, heads, normed, state_w, step_w, small, ids, id_rows, taps, *refs):
    weights, refs = refs[:blocks], refs[blocks:]
    rows, raw, steps, log_decay, cum, state_rows, bc = refs
    length = bc.shape[1]
    values = normed[0]
    state_rows[0] = dot(values, state_w[...]).astype(BF16)
    part = dot_nt(values[PAD:], step_w[...])
    raw[0] = part
    lane = lax.broadcasted_iota(jnp.int32, (length, LANES), 1)
    size = jnp.where(lane < heads, softplus(part + small[0:1, :]), 0.0)
    steps[0] = size
    log_decay[0] = -size * jnp.exp(small[1:2, :])
    ones = triangle(True).astype(F32)
    total = jnp.zeros((1, LANES), F32)
    for c in range(length // CHUNK):
        here = slice(c * CHUNK, (c + 1) * CHUNK)
        value = exact_dot(ones, log_decay[0, here, :]) + total
        cum[0, here, :] = value
        total = value[CHUNK - 1 : CHUNK]

    def store(here, lanes, value):
        bc[0, here, lanes] = value

    conv_forward(state_rows.at[0], ids, id_rows, taps[...], store, length)
    project_rows(values, weights, rows)


def project_more_kernel(blocks, normed, held, *refs):
    project_rows(normed[0], refs[:blocks], refs[blocks])


def project_first(normed, state_w, step_w, small, ids, id_rows, taps, weights, blocks, heads):
    n, padded, model = normed.shape
    width = weights[0].shape[1]
    length = padded - PAD
    whole = lambda a: pl.BlockSpec(a.shape, lambda s: (0,) * a.ndim, pipeline_mode=pl.Buffered(1))
    per_seq = lambda a, b: pl.BlockSpec((1, a, b), lambda s: (s, 0, 0))
    lanes = jax.ShapeDtypeStruct((n, length, LANES), F32)
    return pl.pallas_call(
        functools.partial(project_first_kernel, len(weights), heads),
        grid=(n,),
        in_specs=[
            per_seq(padded, model), whole(state_w), whole(step_w), whole(small), per_seq(*ids.shape[1:]),
            per_seq(*id_rows.shape[1:]), whole(taps),
        ] + [whole(v) for v in weights],
        out_specs=[pl.BlockSpec((len(weights), 1, padded, width), lambda s: (0, s, 0, 0))]
        + [per_seq(length, LANES)] * 4
        + [per_seq(padded, 2 * LANES), per_seq(length, 2 * LANES)],
        out_shape=[
            jax.ShapeDtypeStruct((blocks, n, padded, width), BF16), lanes, lanes, lanes, lanes,
            jax.ShapeDtypeStruct((n, padded, 2 * LANES), BF16),
            jax.ShapeDtypeStruct((n, length, 2 * LANES), BF16),
        ],
        compiler_params=pltpu.CompilerParams(vmem_limit_bytes=VMEM),
        name="project_first",
    )(normed, state_w, step_w, small, ids, id_rows, taps, *weights)


def project_more(normed, rows, weights, first):
    n, padded, model = normed.shape
    width = weights[0].shape[1]
    count = len(weights)
    return pl.pallas_call(
        functools.partial(project_more_kernel, count),
        grid=(n,),
        in_specs=[pl.BlockSpec((1, padded, model), lambda s: (s, 0, 0)), pl.BlockSpec(memory_space=pl.ANY)]
        + [pl.BlockSpec(v.shape, lambda s: (0, 0), pipeline_mode=pl.Buffered(1)) for v in weights],
        out_specs=pl.BlockSpec((count, 1, padded, width), lambda s: (first // count, s, 0, 0)),
        out_shape=jax.ShapeDtypeStruct(rows.shape, BF16),
        input_output_aliases={1: 0},
        compiler_params=pltpu.CompilerParams(vmem_limit_bytes=VMEM),
        name="project_more",
    )(normed, rows, *weights)


def project_gate_kernel(blocks, normed, *refs):
    for r in range(blocks):
        refs[blocks][r, 0] = dot(normed[0, PAD:, :], refs[r][...]).astype(BF16)


def project_gate(normed, weights):
    n, padded, model = normed.shape
    width = weights[0].shape[1]
    count = len(weights)
    return pl.pallas_call(
        functools.partial(project_gate_kernel, count),
        grid=(n,),
        in_specs=[pl.BlockSpec((1, padded, model), lambda s: (s, 0, 0))]
        + [pl.BlockSpec(v.shape, lambda s: (0, 0), pipeline_mode=pl.Buffered(1)) for v in weights],
        out_specs=pl.BlockSpec((count, 1, padded - PAD, width), lambda s: (0, s, 0, 0)),
        out_shape=jax.ShapeDtypeStruct((count, n, padded - PAD, width), BF16),
        compiler_params=pltpu.CompilerParams(vmem_limit_bytes=VMEM),
        name="project_gate",
    )(normed, *weights)


def write_message(message, state, survive):
    cuts, rows, width = message.shape
    own = rows - 16
    survive = jnp.concatenate([survive, survive], axis=0).astype(BF16)
    for i in range(cuts):
        message[i, :own, :] = state[i * own : (i + 1) * own].astype(BF16)
        message[i, own:, :] = survive


def state_kernel(first, per_block, rows, bc, ids, id_rows, steps, cum, taps, *refs):
    acted, message = refs[-2:]
    length, width = acted.shape[2:]
    offset = (pl.program_id(0) + first) * per_block

    def store(here, lanes, value):
        acted[0, 0, here, lanes] = value

    conv_forward(rows.at[0, 0], ids, id_rows, taps[0], store, length)
    total = cum[0, length - 1 : length, :]
    last = ids[0, PAD + length - 1 : PAD + length, :]
    before = ids[0, PAD - 1 : PAD, :]
    state = jnp.zeros((LANES, width), F32)
    for c in range(length // CHUNK):
        here = slice(c * CHUNK, (c + 1) * CHUNK)
        same = (ids[0, PAD + c * CHUNK : PAD + (c + 1) * CHUNK, :] == last).astype(F32)
        tail = jnp.exp(total - cum[0, here, :]) * same * steps[0, here, :]
        scaled = (expand(tail, width, offset) * acted[0, 0, here, :].astype(F32)).astype(BF16)
        state = state + dot_tn(bc[0, here, :LANES], scaled)
    survive = jnp.exp(total) * (last == before).astype(F32)
    write_message(message.at[0, 0], state, expand_row(survive, width, offset))


def state_call(rows, bc, ids, id_rows, steps, cum, taps, held, first, count, per_block, cuts):
    blocks, n, padded, width = rows.shape
    length = padded - PAD
    four = lambda a, b: pl.BlockSpec((1, 1, a, b), lambda g, s: (g + first, s, 0, 0))
    per_seq = lambda a: pl.BlockSpec((1,) + a.shape[1:], lambda g, s: (s, 0, 0))
    piece = LANES // cuts + 16
    return pl.pallas_call(
        functools.partial(state_kernel, first, per_block),
        grid=(count, n),
        in_specs=[
            four(padded, width), per_seq(bc), per_seq(ids), per_seq(id_rows), per_seq(steps), per_seq(cum),
            pl.BlockSpec((1,) + taps.shape[1:], lambda g, s: (g + first, 0, 0)),
        ] + [pl.BlockSpec(memory_space=pl.ANY) for _ in held],
        out_specs=[
            four(length, width),
            pl.BlockSpec((1, 1, cuts, piece, width), lambda g, s: (g + first, s, 0, 0, 0)),
        ],
        out_shape=[
            jax.ShapeDtypeStruct((blocks, n, length, width), BF16),
            jax.ShapeDtypeStruct((blocks, n, cuts, piece, width), BF16),
        ],
        input_output_aliases={7: 0, 8: 1} if held else {},
        compiler_params=pltpu.CompilerParams(vmem_limit_bytes=VMEM),
        name="range_state",
    )(rows, bc, ids, id_rows, steps, cum, taps, *held)


def chunk_marks(ids, c):
    first = PAD + c * CHUNK
    return ids[0, first : first + CHUNK, :], ids[0, first + CHUNK - 1 : first + CHUNK, :], ids[0, first - 1 : first, :]


def chunk_decays(ids, cum, c):
    here, last, before = chunk_marks(ids, c)
    value = cum[0, c * CHUNK : (c + 1) * CHUNK, :]
    base = cum[0, c * CHUNK - 1 : c * CHUNK, :] if c else jnp.zeros((1, LANES), F32)
    end = value[CHUNK - 1 : CHUNK]
    entering = jnp.exp(value - base) * (here == before).astype(F32)
    tail = jnp.exp(end - value) * (here == last).astype(F32)
    survive = jnp.exp(end - base) * (last == before).astype(F32)
    return entering, tail, survive


def lane_halves(pair):
    lane = lax.broadcasted_iota(jnp.int32, pair.shape, 1)
    zero = jnp.zeros_like(pair)
    return jnp.concatenate([jnp.where(lane < HEAD_DIM, pair, zero), jnp.where(lane < HEAD_DIM, zero, pair)], axis=0)


def inside_kernel(per_block, acted, bc, ids, id_rows, steps, cum, mixed, states, carried, turned):
    length, width = acted.shape[2:]
    offset = pl.program_id(1) * per_block
    later = triangle(True)
    for c in range(length // CHUNK):
        here = slice(c * CHUNK, (c + 1) * CHUNK)
        b_part, c_part = bc[0, here, :LANES], bc[0, here, LANES:]
        marks, _, _ = chunk_marks(ids, c)
        same = later & (marks == id_rows[0, 0:1, PAD + c * CHUNK : PAD + (c + 1) * CHUNK])
        scores = jnp.where(same, dot_nt(c_part, b_part), 0.0)
        value = cum[0, here, :]
        turned[...] = jnp.transpose(value)
        entering, tail, survive = chunk_decays(ids, cum, c)
        scaled = (expand(steps[0, here, :], width, offset) * acted[0, 0, here, :].astype(F32)).astype(BF16)
        if c:
            held = carried[...]
            held_low = held.astype(BF16)
            states[0, 0, c - 1] = held_low
            outside = dot(c_part, held_low) * expand(entering, width, offset)
        for pair in range(width // LANES):
            lanes = slice(pair * LANES, (pair + 1) * LANES)
            mixing = []
            for h in (2 * pair, 2 * pair + 1):
                spread = jnp.minimum(column(value, offset + h) - turned[pl.ds(offset + h, 1), :], 0.0)
                mixing.append((scores * jnp.exp(spread)).astype(BF16))
            result = dot(jnp.concatenate(mixing, axis=1), lane_halves(scaled[:, lanes]))
            mixed[0, 0, here, lanes] = result + outside[:, lanes] if c else result
        if c + 1 < length // CHUNK:
            fresh = dot_tn(b_part, (expand(tail, width, offset) * scaled.astype(F32)).astype(BF16))
            if c:
                fresh = fresh + held * expand_row(survive, width, offset)[0:1]
            carried[...] = fresh


def inside_call(acted, bc, ids, id_rows, steps, cum, per_block):
    blocks, n, length, width = acted.shape
    chunks = length // CHUNK
    four = lambda a, b: pl.BlockSpec((1, 1, a, b), lambda s, g: (g, s, 0, 0))
    per_seq = lambda a: pl.BlockSpec((1,) + a.shape[1:], lambda s, g: (s, 0, 0))
    return pl.pallas_call(
        functools.partial(inside_kernel, per_block),
        grid=(n, blocks),
        in_specs=[four(length, width), per_seq(bc), per_seq(ids), per_seq(id_rows), per_seq(steps), per_seq(cum)],
        out_specs=[
            four(length, width),
            pl.BlockSpec((1, 1, chunks - 1, LANES, width), lambda s, g: (g, s, 0, 0, 0)),
        ],
        out_shape=[
            jax.ShapeDtypeStruct((blocks, n, length, width), F32),
            jax.ShapeDtypeStruct((blocks, n, chunks - 1, LANES, width), BF16),
        ],
        scratch_shapes=[pltpu.VMEM((LANES, width), F32), pltpu.VMEM((LANES, LANES), F32)],
        compiler_params=pltpu.CompilerParams(vmem_limit_bytes=VMEM),
        name="inside",
    )(acted, bc, ids, id_rows, steps, cum)


def relay_kernel(backward, message, carried):
    ranges, rows, width = carried.shape
    state = jnp.zeros((rows, width), F32)
    order = range(ranges - 1, -1, -1) if backward else range(ranges)
    for q in order:
        carried[q] = state.astype(BF16)
        decay = message[q, rows : rows + 1, :].astype(F32)
        state = state * decay + message[q, :rows, :].astype(F32)


class Held:
    def __init__(self, value=None):
        self.value = value


def meet(*held):
    for h, value in zip(held, lax.optimization_barrier(tuple(h.value for h in held))):
        h.value = value


def values(held):
    return [h.value for h in held]


def over_ranges(value):
    return lax.all_to_all(value, "seq", 0, 0, tiled=True)


def send_message(message):
    return over_ranges(message.reshape(lax.axis_size("seq"), message.shape[3], message.shape[4]))


def relay(arrived, backward):
    ranges, rows, width = arrived.shape
    return pl.pallas_call(
        functools.partial(relay_kernel, backward),
        out_shape=jax.ShapeDtypeStruct((ranges, rows - 16, width), BF16),
        compiler_params=pltpu.CompilerParams(vmem_limit_bytes=VMEM),
        name="relay",
    )(arrived)


def send_back(carried, blocks, n):
    return over_ranges(carried).reshape(blocks, n, LANES, carried.shape[2])


def middle_kernel(
    blocks, per_block, total_width, mixed, gate, acted, cum, cum_end, bc, ids, ids_before, ids_after, tokens, cotangent,
    params, entered, *refs
):
    weights, refs = refs[:blocks], refs[blocks:]
    output, normed_out, d_gate, d_summed, pulled, gain_grad, skip_grad = refs[:7]
    summed_s, gated_s, grad_s, first_s, second_s, low_s, row_s, pull_s = refs[7:]
    tile, width = mixed.shape[2:]
    t = pl.program_id(0)
    before = ids_before[0, PAD - 1 : PAD, :]
    marks = ids[0]
    c_part = bc[0, :, LANES:]
    slabs = tile // 16
    same = (marks == before).astype(F32)
    decay = jnp.exp(cum[0]) * same
    row_s[...] = jnp.zeros_like(row_s)

    def lanes_sum(value):
        total = value[:, :LANES]
        for i in range(1, width // LANES):
            total = total + value[:, i * LANES : (i + 1) * LANES]
        return total

    @pl.when(t == 0)
    def _():
        gain_grad[...] = jnp.zeros_like(gain_grad)
        skip_grad[...] = jnp.zeros_like(skip_grad)
        pull_s[...] = jnp.zeros_like(pull_s)

    for r in range(blocks):
        first_s[...] = dot(c_part, entered[r, 0])
        second_s[r] = expand(decay, width, r * per_block)
        skip = params[r, 6:7, :]

        def step(i, carry, r=r, skip=skip):
            here = rows_at(i * 16, 16)
            value = mixed[r, 0, here, :] + first_s[here, :] * second_s[r, here, :]
            summed = value + skip * acted[r, 0, here, :].astype(F32)
            g = gate[r, 0, here, :].astype(F32)
            gated = summed * (g * sigmoid(g))
            summed_s[r, here, :] = summed
            gated_s[r, here, :] = gated
            row_s[here, :] = row_s[here, :] + lanes_sum(gated * gated)
            return carry

        lax.fori_loop(0, slabs, step, 0, unroll=4)
    squares = jnp.sum(row_s[...], axis=1, keepdims=True)
    rescale = jnp.broadcast_to(lax.rsqrt(squares / total_width + EPS), (tile, LANES))
    row_s[...] = rescale
    for r in range(blocks):
        gain = params[r, 5:6, :]

        def step(i, carry, r=r, gain=gain):
            here = rows_at(i * 16, 16)
            normed_out[r, 0, here, :] = (gated_s[r, here, :] * widen(row_s[here, :], width) * gain).astype(BF16)
            return carry

        lax.fori_loop(0, slabs, step, 0, unroll=4)
    branch = tokens[0].astype(F32)
    for r in range(blocks):
        branch = branch + dot(normed_out[r, 0], weights[r][...])
    output[0] = branch.astype(BF16)
    first_s[:, :LANES] = jnp.zeros((tile, LANES), F32)
    for r in range(blocks):
        grad_s[r] = dot_nt(cotangent[0], weights[r][...])
        gain = params[r, 5:6, :]

        def step(i, total, r=r, gain=gain):
            here = rows_at(i * 16, 16)
            both = grad_s[r, here, :] * gated_s[r, here, :]
            first_s[here, :LANES] = first_s[here, :LANES] + lanes_sum(both * gain)
            return total + fold8(both * widen(row_s[here, :], width))

        gain_grad[r] = gain_grad[r] + lax.fori_loop(0, slabs, step, jnp.zeros((8, width), F32), unroll=4)
    cross = jnp.sum(first_s[:, :LANES], axis=1, keepdims=True) / total_width
    first_s[:, :LANES] = rescale * rescale * rescale * cross
    for r in range(blocks):
        gain = params[r, 5:6, :]

        def step(i, total, r=r, gain=gain):
            here = rows_at(i * 16, 16)
            g = gate[r, 0, here, :].astype(F32)
            sigma = sigmoid(g)
            d_gated = widen(row_s[here, :], width) * (grad_s[r, here, :] * gain) - gated_s[r, here, :] * widen(
                first_s[here, :LANES], width
            )
            d_sum = d_gated * (g * sigma)
            d_gate[r, 0, here, :] = (d_gated * summed_s[r, here, :] * (sigma * (1.0 + g * (1.0 - sigma)))).astype(BF16)
            low = d_sum.astype(BF16)
            d_summed[r, 0, here, :] = low
            low_s[here, :] = (d_sum * second_s[r, here, :]).astype(BF16)
            return total + fold8(d_sum * acted[r, 0, here, :].astype(F32))

        skip_grad[r] = skip_grad[r] + lax.fori_loop(0, slabs, step, jnp.zeros((8, width), F32), unroll=4)
        pull_s[r] = pull_s[r] + dot_tn(c_part, low_s[...])

    @pl.when(t == pl.num_programs(0) - 1)
    def _():
        survive = jnp.exp(cum_end[0, 7:8, :]) * (ids_after[0, PAD - 1 : PAD, :] == before).astype(F32)
        for r in range(blocks):
            write_message(pulled.at[r, 0], pull_s[r], expand_row(survive, width, r * per_block))


def middle_call(s, mixed, gate, acted, cum, entered, bc, ids, tokens, cotangent, params, weights, per_block, cuts):
    blocks, n, length, width = mixed.shape
    model = tokens.shape[2]
    tile = min(256, length)
    wide = lambda w: pl.BlockSpec((blocks, 1, tile, w), lambda t: (0, s, t, 0))
    wide_out = lambda w: pl.BlockSpec((blocks, 1, tile, w), lambda t: (0, 0, t, 0))
    rows = lambda w: pl.BlockSpec((1, tile, w), lambda t: (s, t, 0))
    one = lambda a: pl.BlockSpec((a.shape[0], 1) + a.shape[2:], lambda t: (0, s, 0, 0), pipeline_mode=pl.Buffered(1))
    whole = lambda a: pl.BlockSpec(a.shape, lambda t: (0,) * a.ndim, pipeline_mode=pl.Buffered(1))
    kept = lambda *shape: pl.BlockSpec(shape, lambda t: (0,) * len(shape))
    piece = LANES // cuts + 16
    edge = lambda a: pl.BlockSpec((1, PAD, LANES), lambda t: (s, a, 0))
    ids_here = ids[:, PAD : PAD + length]
    wide_shape = jax.ShapeDtypeStruct((blocks, 1, length, width), BF16)
    return pl.pallas_call(
        functools.partial(middle_kernel, blocks, per_block, width * blocks),
        grid=(length // tile,),
        in_specs=[
            wide(width), wide(width), wide(width), rows(LANES),
            pl.BlockSpec((1, 8, LANES), lambda t: (s, length // 8 - 1, 0)), rows(2 * LANES), rows(LANES),
            edge(0), edge(length // PAD), rows(model), rows(model), whole(params),
            one(entered),
        ] + [whole(v) for v in weights],
        out_specs=[
            pl.BlockSpec((1, tile, model), lambda t: (0, t, 0)), wide_out(width), wide_out(width), wide_out(width),
            kept(blocks, 1, cuts, piece, width), kept(blocks, 8, width), kept(blocks, 8, width),
        ],
        out_shape=[
            jax.ShapeDtypeStruct((1, length, model), BF16),
            wide_shape, wide_shape, wide_shape,
            jax.ShapeDtypeStruct((blocks, 1, cuts, piece, width), BF16),
            jax.ShapeDtypeStruct((blocks, 8, width), F32),
            jax.ShapeDtypeStruct((blocks, 8, width), F32),
        ],
        scratch_shapes=[
            pltpu.VMEM((blocks, tile, width), F32),
            pltpu.VMEM((blocks, tile, width), F32),
            pltpu.VMEM((blocks, tile, width), F32),
            pltpu.VMEM((tile, width), F32),
            pltpu.VMEM((blocks, tile, width), F32),
            pltpu.VMEM((tile, width), BF16),
            pltpu.VMEM((tile, LANES), F32),
            pltpu.VMEM((blocks, LANES, width), F32),
        ],
        compiler_params=pltpu.CompilerParams(vmem_limit_bytes=VMEM),
        name="middle",
    )(mixed, gate, acted, cum, cum, bc, ids_here, ids, ids, tokens, cotangent, params, entered, *weights)


def inside_back_kernel(
    per_block, acted, d_summed, mixed, bc, ids, id_rows, steps, cum, states, entered, d_scaled, d_b, d_c, d_cum,
    carried, turned,
):
    length, width = acted.shape[2:]
    chunks = length // CHUNK
    g = pl.program_id(0)
    offset = g * per_block
    heads = head_map(width, offset)
    sooner = triangle(False)
    first_before = ids[0, PAD - 1 : PAD, :]
    came = entered[0, 0]

    @pl.when(g == 0)
    def _():
        d_b[...] = jnp.zeros_like(d_b)
        d_c[...] = jnp.zeros_like(d_c)
        d_cum[...] = jnp.zeros_like(d_cum)

    for c in range(chunks - 1, -1, -1):
        here = slice(c * CHUNK, (c + 1) * CHUNK)
        b_part, c_part = bc[0, here, :LANES], bc[0, here, LANES:]
        marks, _, _ = chunk_marks(ids, c)
        same = sooner & (marks == id_rows[0, 0:1, PAD + c * CHUNK : PAD + (c + 1) * CHUNK])
        scores_t = jnp.where(same, dot_nt(b_part, c_part), 0.0)
        value = cum[0, here, :]
        turned[...] = jnp.transpose(value)
        entering, tail, survive = chunk_decays(ids, cum, c)
        scaled = (expand(steps[0, here, :], width, offset) * acted[0, 0, here, :].astype(F32)).astype(BF16)
        grad = d_summed[0, 0, here, :]
        grad_wide = grad.astype(F32)
        from_start = jnp.exp(value) * (marks == first_before).astype(F32)
        start_wide = expand(from_start, width, offset)
        d_c_part = dot_nt((grad_wide * start_wide).astype(BF16), came)
        dots = grad_wide * (mixed[0, 0, here, :] + start_wide * dot(c_part, came))
        if c < chunks - 1:
            held = carried[...]
            held_low = held.astype(BF16)
            tail_wide = expand(tail, width, offset)
            later = dot(b_part, held_low) * tail_wide
            d_b_part = dot_nt((tail_wide * scaled.astype(F32)).astype(BF16), held_low)
        if c:
            entering_grad = (expand(entering, width, offset) * grad_wide).astype(BF16)
            d_c_part = d_c_part + dot_nt(entering_grad, states[0, 0, c - 1])
        d_scores_t = jnp.zeros((CHUNK, CHUNK), F32)
        results = []
        for pair in range(width // LANES):
            lanes = slice(pair * LANES, (pair + 1) * LANES)
            products = dot_nt(lane_halves(scaled[:, lanes]), grad[:, lanes])
            mixing = []
            for half, h in enumerate((2 * pair, 2 * pair + 1)):
                spread = jnp.minimum(turned[pl.ds(offset + h, 1), :] - column(value, offset + h), 0.0)
                decay = jnp.exp(spread)
                mixing.append((scores_t * decay).astype(BF16))
                d_scores_t = d_scores_t + products[half * CHUNK : (half + 1) * CHUNK] * decay
            results.append(dot(jnp.concatenate(mixing, axis=1), lane_halves(grad[:, lanes])))
        result = jnp.concatenate(results, axis=1)
        if c < chunks - 1:
            result = result + later
        d_scaled[0, 0, here, :] = result.astype(BF16)
        d_cum[0, here, :] = d_cum[0, here, :] + by_head(dots - scaled.astype(F32) * result, heads)
        d_scores_t = jnp.where(same, d_scores_t, 0.0).astype(BF16)
        d_b_here = dot(d_scores_t, c_part)
        if c < chunks - 1:
            d_b_here = d_b_here + d_b_part
        d_b[0, here, :] = d_b[0, here, :] + d_b_here
        d_c[0, here, :] = d_c[0, here, :] + d_c_part + dot_tn(d_scores_t, b_part)
        if c:
            pulled = dot_tn(c_part, entering_grad)
            if c < chunks - 1:
                pulled = pulled + held * expand_row(survive, width, offset)[0:1]
            carried[...] = pulled


def inside_back_call(s, acted, d_summed, mixed, bc, ids, id_rows, steps, cum, states, entered, per_block):
    blocks, n, length, width = acted.shape
    four = lambda a, b: pl.BlockSpec((1, 1, a, b), lambda g: (g, s, 0, 0))
    own = lambda a, b: pl.BlockSpec((1, 1, a, b), lambda g: (g, 0, 0, 0))
    per_seq = lambda a: pl.BlockSpec((1,) + a.shape[1:], lambda g: (s, 0, 0))
    summed = pl.BlockSpec((1, length, LANES), lambda g: (0, 0, 0))
    lanes = jax.ShapeDtypeStruct((1, length, LANES), F32)
    return pl.pallas_call(
        functools.partial(inside_back_kernel, per_block),
        grid=(blocks,),
        in_specs=[
            four(length, width), own(length, width), four(length, width), per_seq(bc), per_seq(ids), per_seq(id_rows),
            per_seq(steps), per_seq(cum),
            pl.BlockSpec((1, 1) + states.shape[2:], lambda g: (g, s, 0, 0, 0)),
            four(LANES, width),
        ],
        out_specs=[own(length, width), summed, summed, summed],
        out_shape=[jax.ShapeDtypeStruct((blocks, 1, length, width), BF16), lanes, lanes, lanes],
        scratch_shapes=[pltpu.VMEM((LANES, width), F32), pltpu.VMEM((LANES, LANES), F32)],
        compiler_params=pltpu.CompilerParams(vmem_limit_bytes=VMEM),
        name="inside_back",
    )(acted, d_summed, mixed, bc, ids, id_rows, steps, cum, states, entered)


def close_kernel(
    per_block, rows, acted, d_summed, d_scaled, bc, ids, id_rows, steps, raw, log_decay, cum, d_cum, leaving, entered,
    params, small, state_rows, state_taps, d_b, d_c,
    d_rows, d_raw, d_state, taps_grad, state_taps_grad, small_grad, d_pre, d_acted, d_log, d_step, ends, d_bc, d_pre_bc,
):
    length, width = acted.shape[2:]
    chunks = length // CHUNK
    g = pl.program_id(0)
    offset = g * per_block
    heads = head_map(width, offset)
    last = ids[0, PAD + length - 1 : PAD + length, :]
    before = ids[0, PAD - 1 : PAD, :]
    end = cum[0, length - 1 : length, :]
    skip = params[0, 6:7, :]
    held = leaving[0, 0]
    came = entered[0, 0]

    @pl.when(g == 0)
    def _():
        d_bc[:, :LANES] = d_b[0]
        d_bc[:, LANES:] = d_c[0]
        d_log[...] = d_cum[0]
        d_step[...] = jnp.zeros_like(d_step)
        ends[...] = jnp.zeros_like(ends)

    boundary = jnp.zeros((1, LANES), F32)
    for c in range(chunks):
        here = slice(c * CHUNK, (c + 1) * CHUNK)
        marks, _, _ = chunk_marks(ids, c)
        tail = jnp.exp(end - cum[0, here, :]) * (marks == last).astype(F32)
        tail_wide = expand(tail, width, offset)
        steps_wide = expand(steps[0, here, :], width, offset)
        x = acted[0, 0, here, :].astype(F32)
        scaled = (steps_wide * x).astype(BF16).astype(F32)
        later = dot(bc[0, here, :LANES], held) * tail_wide
        total = d_scaled[0, 0, here, :].astype(F32) + later
        d_acted[here, :] = steps_wide * total + skip * d_summed[0, 0, here, :].astype(F32)
        d_bc[here, :LANES] = d_bc[here, :LANES] + dot_nt((tail_wide * scaled).astype(BF16), held)
        from_later = by_head_low(scaled * later, heads)
        boundary = boundary + jnp.sum(from_later, axis=0, keepdims=True)
        d_log[here, :] = d_log[here, :] - from_later
        d_step[here, :] = d_step[here, :] + by_head_low(x * total, heads)
    product = held.astype(F32) * came.astype(F32)
    product = jnp.sum(product.reshape(LANES // 8, 8, width), axis=0)
    survive = jnp.exp(end) * (last == before).astype(F32)
    boundary = boundary + survive * jnp.sum(by_head(jnp.concatenate([product, product * 0.0], axis=0), heads), axis=0, keepdims=True)
    ends[0:1, :] = ends[0:1, :] + boundary

    def store(here, lanes, value):
        d_rows[0, 0, here, lanes] = value

    sums = conv_backward(
        rows.at[0, 0],
        ids,
        id_rows,
        params[0],
        lambda c, lanes: d_acted[c * CHUNK : (c + 1) * CHUNK, lanes],
        d_pre,
        store,
        length,
    )
    taps_grad[0] = jnp.concatenate(sums + [jnp.zeros((3, width), F32)], axis=0)

    @pl.when(g == pl.num_programs(0) - 1)
    def _():
        rate = jnp.exp(small[1:2, :])
        ones = triangle(False).astype(F32)
        carry = ends[0:1, :]
        decay_sum = jnp.zeros((1, LANES), F32)
        bias_sum = jnp.zeros((1, LANES), F32)
        for c in range(chunks - 1, -1, -1):
            here = slice(c * CHUNK, (c + 1) * CHUNK)
            grads = exact_dot(ones, d_log[here, :]) + carry
            carry = grads[0:1]
            decay_sum = decay_sum + jnp.sum(grads * log_decay[0, here, :], axis=0, keepdims=True)
            value = (d_step[here, :] - grads * rate) * sigmoid(raw[0, here, :] + small[0:1, :])
            bias_sum = bias_sum + jnp.sum(value, axis=0, keepdims=True)
            d_raw[0, here, :] = value.astype(BF16)
        small_grad[...] = jnp.concatenate([bias_sum, decay_sum, jnp.zeros((6, LANES), F32)], axis=0)

        def store_state(here, lanes, value):
            d_state[0, here, lanes] = value

        sums = conv_backward(
            state_rows.at[0],
            ids,
            id_rows,
            state_taps[...],
            lambda c, lanes: d_bc[c * CHUNK : (c + 1) * CHUNK, lanes],
            d_pre_bc,
            store_state,
            length,
        )
        state_taps_grad[...] = jnp.concatenate(sums + [jnp.zeros((3, 2 * LANES), F32)], axis=0)


def close_call(
    s, rows, acted, d_summed, d_scaled, bc, ids, id_rows, steps, raw, log_decay, cum, d_cum, leaving, entered, params,
    small, state_rows, state_taps, d_b, d_c, per_block,
):
    blocks, n, length, width = acted.shape
    four = lambda a, b: pl.BlockSpec((1, 1, a, b), lambda g: (g, s, 0, 0))
    own = lambda a, b: pl.BlockSpec((1, 1, a, b), lambda g: (g, 0, 0, 0))
    per_seq = lambda a: pl.BlockSpec((1,) + a.shape[1:], lambda g: (s, 0, 0))
    kept = lambda *shape: pl.BlockSpec(shape, lambda g: (0,) * len(shape))
    whole = lambda a: kept(*a.shape)
    wide = own(length, width)
    return pl.pallas_call(
        functools.partial(close_kernel, per_block),
        grid=(blocks,),
        in_specs=[
            four(length + PAD, width), four(length, width), wide, wide, per_seq(bc), per_seq(ids), per_seq(id_rows),
            per_seq(steps), per_seq(raw), per_seq(log_decay), per_seq(cum), kept(1, length, LANES), own(LANES, width),
            four(LANES, width),
            pl.BlockSpec((1,) + params.shape[1:], lambda g: (g, 0, 0)), whole(small), per_seq(state_rows),
            whole(state_taps), whole(d_b), whole(d_c),
        ],
        out_specs=[
            own(length + PAD, width), kept(1, length, LANES), kept(1, length + PAD, 2 * LANES),
            pl.BlockSpec((1, 8, width), lambda g: (g, 0, 0)), kept(8, 2 * LANES), kept(8, LANES),
        ],
        out_shape=[
            jax.ShapeDtypeStruct((blocks, 1, length + PAD, width), BF16),
            jax.ShapeDtypeStruct((1, length, LANES), BF16),
            jax.ShapeDtypeStruct((1, length + PAD, 2 * LANES), BF16),
            jax.ShapeDtypeStruct((blocks, 8, width), F32),
            jax.ShapeDtypeStruct((8, 2 * LANES), F32),
            jax.ShapeDtypeStruct((8, LANES), F32),
        ],
        scratch_shapes=[
            pltpu.VMEM((length + 2 * PAD, width), BF16),
            pltpu.VMEM((length, width), F32),
            pltpu.VMEM((length, LANES), F32),
            pltpu.VMEM((length, LANES), F32),
            pltpu.VMEM((8, LANES), F32),
            pltpu.VMEM((length, 2 * LANES), F32),
            pltpu.VMEM((length + 2 * PAD, 2 * LANES), BF16),
        ],
        compiler_params=pltpu.CompilerParams(vmem_limit_bytes=VMEM),
        name="close",
    )(
        rows, acted, d_summed, d_scaled, bc, ids, id_rows, steps, raw, log_decay, cum, d_cum, leaving, entered, params,
        small, state_rows, state_taps, d_b, d_c,
    )


def input_kernel(blocks, d_raw, d_state, tokens, cotangent, gain, state_w, step_w, d_gate, d_rows, *refs):
    row_weights, refs = refs[:blocks], refs[blocks:]
    gate_weights, refs = refs[:blocks], refs[blocks:]
    input_grad, edge, halo, gain_grad, main_s, halo_s, weights_s, gate_s, rows_s, sems = refs
    length = d_gate.shape[2]
    copies = []
    for r in range(blocks):
        moves = [(row_weights[r], weights_s.at[2 * r]), (d_rows.at[r, 0], rows_s.at[r])]
        moves += [(gate_weights[r], weights_s.at[2 * r + 1]), (d_gate.at[r, 0], gate_s.at[r])]
        copies.append([pltpu.make_async_copy(a, b, sems.at[4 * r + i]) for i, (a, b) in enumerate(moves)])
        for copy in copies[r]:
            copy.start()
    total = dot_nt(d_state[0], state_w[...])
    halo_s[...] = total[:PAD]
    main_s[...] = total[PAD:] + dot(d_raw[0], step_w[...])
    for r in range(blocks):
        copies[r][0].wait()
        copies[r][1].wait()
        halo_s[...] = halo_s[...] + dot_nt(rows_s[r, :PAD, :], weights_s[2 * r])
        part = dot_nt(rows_s[r, PAD:, :], weights_s[2 * r])
        copies[r][2].wait()
        copies[r][3].wait()
        main_s[...] = main_s[...] + (part + dot_nt(gate_s[r], weights_s[2 * r + 1]))

    def norm_back(value, token):
        scale = lax.rsqrt(jnp.mean(token * token, axis=1, keepdims=True) + EPS)
        unit = value * gain[...]
        inner = jnp.mean(unit * token, axis=1, keepdims=True)
        return scale * unit - token * (scale * scale * scale * inner), fold8(value * token * scale)

    grad, sums = norm_back(halo_s[...], tokens[0, :PAD, :].astype(F32))
    halo[0] = grad.astype(BF16)

    def step(i, carry):
        here = rows_at(i * 16, 16)
        grad, more = norm_back(main_s[here, :], tokens[0, rows_at(PAD + i * 16, 16), :].astype(F32))
        value = grad + cotangent[0, here, :].astype(F32)
        edge[0] = value
        input_grad[0, here, :] = value.astype(BF16)
        return carry + more

    gain_grad[...] = lax.fori_loop(0, length // 16, step, sums, unroll=4)


def input_call(s, d_gate, d_rows, d_raw, d_state, tokens, cotangent, gain, state_w, step_w, row_weights, gate_weights):
    blocks, _, length, width = d_gate.shape
    padded, model = tokens.shape[1:]
    whole = lambda a: pl.BlockSpec(a.shape, lambda t: (0,) * a.ndim, pipeline_mode=pl.Buffered(1))
    one = lambda a, b: pl.BlockSpec((1, a, b), lambda t: (s, 0, 0), pipeline_mode=pl.Buffered(1))
    kept = lambda *shape: pl.BlockSpec(shape, lambda t: (0,) * len(shape), pipeline_mode=pl.Buffered(1))
    return pl.pallas_call(
        functools.partial(input_kernel, blocks),
        grid=(1,),
        in_specs=[
            whole(d_raw), whole(d_state), one(padded, model), one(length, model), whole(gain), whole(state_w), whole(step_w),
        ] + [pl.BlockSpec(memory_space=pl.ANY)] * (2 + 2 * blocks),
        out_specs=[kept(1, length, model), kept(1, PAD, model), kept(1, PAD, model), kept(8, model)],
        out_shape=[
            jax.ShapeDtypeStruct((1, length, model), BF16),
            jax.ShapeDtypeStruct((1, PAD, model), F32),
            jax.ShapeDtypeStruct((1, PAD, model), BF16),
            jax.ShapeDtypeStruct((8, model), F32),
        ],
        scratch_shapes=[
            pltpu.VMEM((length, model), F32),
            pltpu.VMEM((PAD, model), F32),
            pltpu.VMEM((2 * blocks, model, width), BF16),
            pltpu.VMEM((blocks, length, width), BF16),
            pltpu.VMEM((blocks, padded, width), BF16),
            pltpu.SemaphoreType.DMA((4 * blocks,)),
        ],
        compiler_params=pltpu.CompilerParams(vmem_limit_bytes=VMEM),
        name="input_gradient",
    )(d_raw, d_state, tokens, cotangent, gain, state_w, step_w, d_gate, d_rows, *row_weights, *gate_weights)


def assemble_kernel(count, places, *refs):
    parts, refs = refs[:count], refs[count:]
    edges, refs = (refs[:count], refs[count:]) if len(refs) > 2 * count else ((), refs)
    whole, buffers, (in_sem, out_sem) = refs[0], refs[1:-2], refs[-2:]
    length = parts[0].shape[1]
    reads = [pltpu.make_async_copy(p.at[0], b, in_sem.at[i]) for i, (p, b) in enumerate(zip(parts, buffers))]
    writes = [pltpu.make_async_copy(b, whole.at[places[i]], out_sem.at[i]) for i, b in enumerate(buffers)]
    for read in reads:
        read.start()
    for i, (read, write) in enumerate(zip(reads, writes)):
        read.wait()
        if edges:
            buffers[i][length - PAD :, :] = edges[i][0]
        write.start()
    for write in writes:
        write.wait()


def assemble(parts, edges, places):
    count = len(parts)
    _, length, model = parts[0].shape
    return pl.pallas_call(
        functools.partial(assemble_kernel, count),
        grid_spec=pltpu.PrefetchScalarGridSpec(
            num_scalar_prefetch=1,
            grid=(1,),
            in_specs=[pl.BlockSpec(memory_space=pl.ANY) for _ in parts]
            + [pl.BlockSpec((1, PAD, model), lambda t, i: (0, 0, 0)) for _ in edges],
            out_specs=pl.BlockSpec(memory_space=pl.ANY),
            scratch_shapes=[pltpu.VMEM((length, model), BF16) for _ in parts]
            + [pltpu.SemaphoreType.DMA((count,)), pltpu.SemaphoreType.DMA((count,))],
        ),
        out_shape=jax.ShapeDtypeStruct((count, length, model), BF16),
        compiler_params=pltpu.CompilerParams(vmem_limit_bytes=VMEM),
        name="assemble",
    )(jnp.stack(places).astype(jnp.int32), *parts, *edges)


def weight_grad_kernel(n, halo, rows, *refs):
    grads, (kept, sent) = refs[:n], refs[n:]
    odd = pl.program_id(0) % 2 == 1
    start = PAD if halo else 0
    length = grads[0].shape[2] - start
    skip = rows.shape[1] - length
    total = None
    if halo:
        before = jnp.concatenate([rows[s, :PAD, :] for s in range(n)], axis=0)
        total = dot_tn(before, jnp.concatenate([grad[0, 0, :PAD, :] for grad in grads], axis=0))
    for s in range(n):
        part = dot_tn(rows[s, skip:, :], grads[s][0, 0, start:, :])
        total = part if total is None else total + part
    total = total.astype(BF16)

    @pl.when(odd)
    def _():
        sent[0] = total

    @pl.when(jnp.logical_not(odd))
    def _():
        kept[0] = total


def weight_grad(values, grads):
    n, padded, model = values.shape
    blocks, _, tokens, width = grads[0].shape
    return pl.pallas_call(
        functools.partial(weight_grad_kernel, n, tokens % CHUNK != 0),
        grid=(blocks,),
        in_specs=[pl.BlockSpec(values.shape, lambda g: (0, 0, 0), pipeline_mode=pl.Buffered(1))]
        + [pl.BlockSpec((1, 1, tokens, width), lambda g: (g, 0, 0, 0)) for _ in grads],
        out_specs=[pl.BlockSpec((1, model, width), lambda g: (g // 2, 0, 0))] * 2,
        out_shape=[jax.ShapeDtypeStruct((blocks // 2, model, width), BF16)] * 2,
        compiler_params=pltpu.CompilerParams(vmem_limit_bytes=VMEM),
        name="weight_gradient",
    )(values, *grads)


def state_grad_kernel(n, values, *refs):
    states, (out,) = refs[:n], refs[n:]
    total = dot_tn(values[0], states[0][0])
    for s in range(1, n):
        total = total + dot_tn(values[s], states[s][0])
    out[...] = total.astype(BF16)


def state_grad(values, states):
    return pl.pallas_call(
        functools.partial(state_grad_kernel, len(states)),
        out_shape=jax.ShapeDtypeStruct((values.shape[2], states[0].shape[2]), BF16),
        compiler_params=pltpu.CompilerParams(vmem_limit_bytes=VMEM),
        name="state_weight_gradient",
    )(values, *states)


def pack_kernel(n, per_block, values, *refs):
    groups, outs = [refs[i * n : (i + 1) * n] for i in range(7)], refs[7 * n :]
    steps, taps, state_taps, rest, gains, skips, norms = groups
    add = lambda refs, *at: functools.reduce(lambda a, b: a + b, [ref[at] for ref in refs])
    column_sum = lambda value: jnp.sum(value, axis=0, keepdims=True)
    step = dot_tn(steps[0][0], values[0, PAD:, :])
    for s in range(1, n):
        step = step + dot_tn(steps[s][0], values[s, PAD:, :])
    model = step.shape[1]
    width = outs[0].shape[1]
    norm = column_sum(add(norms, Ellipsis))
    rest = add(rest, Ellipsis)
    state = add(state_taps, Ellipsis)
    for r, out in enumerate(outs):
        out[...] = jnp.zeros_like(out)
        out[0:5, :] = add(taps, r)[0:5]
        out[5:6, :] = column_sum(add(gains, r))
        out[6:7, :] = column_sum(add(skips, r))
        mine = pltpu.roll(rest, (LANES - r * per_block) % LANES, 1) if r else rest
        out[7:8, :LANES] = mine[0:1]
        out[7:8, LANES : 2 * LANES] = mine[1:2]
        row = 8
        for q in range(0, model, width):
            out[row : row + per_block, :] = step[r * per_block : (r + 1) * per_block, q : q + width]
            row += per_block
        for q in range(0, model, width):
            out[row : row + 1, :] = norm[:, q : q + width]
            row += 1
        out[row : row + 5, : 2 * LANES] = state[0:5]


def pack_sums(values, width, per_block, blocks, *groups):
    n, _, model = values.shape
    rows = 8 + per_block * (model // width) + model // width + 5
    return pl.pallas_call(
        functools.partial(pack_kernel, n, per_block),
        out_shape=[jax.ShapeDtypeStruct((-(-rows // 8) * 8, width), F32)] * blocks,
        compiler_params=pltpu.CompilerParams(vmem_limit_bytes=VMEM),
        name="pack",
    )(values, *[v for group in groups for v in group])


def unpack_kernel(packed, norm, steps, taps, state_taps, params, gains):
    heads, width = params.shape[1], packed.shape[1]
    model = steps.shape[1]
    taps[...] = packed[0:5, :]
    for k in range(width // LANES):
        gains[k : k + 1, :] = packed[5:6, k * LANES : (k + 1) * LANES]
    params[0:1, :] = packed[7:8, :heads]
    params[1:2, :] = packed[7:8, LANES : LANES + heads]
    skips = packed[6:7, :]
    lane = lax.broadcasted_iota(jnp.int32, (heads, width), 1)
    head = lax.broadcasted_iota(jnp.int32, (heads, width), 0)
    mine = lax.shift_right_logical(lane, 6) == head
    column = jnp.sum(jnp.where(mine, skips, 0.0), axis=1, keepdims=True)
    params[2:3, :] = jnp.transpose(jnp.broadcast_to(column, (heads, LANES)))[0:1, :]
    row = 8
    for q in range(0, model, width):
        steps[:, q : q + width] = packed[row : row + heads, :]
        row += heads
    for k in range(model // LANES):
        at = k * LANES
        norm[k : k + 1, :] = packed[row + at // width : row + at // width + 1, at % width : at % width + LANES]
    row += model // width
    state_taps[...] = packed[row : row + 5, : 2 * LANES]


def unpack_sums(packed, heads, model):
    width = packed.shape[1]
    shapes = [(model // LANES, LANES), (heads, model), (5, width), (5, 2 * LANES), (3, heads), (width // LANES, LANES)]
    return pl.pallas_call(
        unpack_kernel, out_shape=[jax.ShapeDtypeStruct(shape, F32) for shape in shapes], name="unpack"
    )(packed)


def swapped(value, axis, step):
    return lax.ppermute(value, axis, [(i, i ^ step) for i in range(lax.axis_size(axis))])


def reached(value):
    return {r: swapped(value, "head", r) if r else value for r in [0, 1] + list(range(2, lax.axis_size("head"), 2))}


def forwarded(parts):
    rest = {r + 1: swapped(parts[r], "head", 1) for r in parts if r and r % 2 == 0}
    return [{**parts, **rest}[r] for r in range(lax.axis_size("head"))]


def gathered(value):
    return forwarded(reached(value))


def crossed(value):
    return {r: swapped(value, "head", r) if r else value for r in range(0, lax.axis_size("head"), 2)}


def completed(parts):
    rest = {r + 1: swapped(part, "head", 1) for r, part in parts.items()}
    return [{**parts, **rest}[r] for r in range(lax.axis_size("head"))]


def bits_of(axis):
    return [1 << i for i in range((lax.axis_size(axis) - 1).bit_length())]


def added(a, b, dtype=None):
    return (a.astype(F32) + b.astype(F32)).astype(dtype or a.dtype)


def tree_sum(values):
    while len(values) > 1:
        values = [a + b for a, b in zip(values[::2], values[1::2])]
    return values[0]


def head_sum(value, bits):
    for bit in reversed(bits):
        half = value.shape[0] // 2
        arrived = yield value[half:], "head", bit
        value = added(value[:half], arrived)
    return value[0]


def ranges_sum(value):
    ranges = lax.axis_size("seq")
    me = lax.axis_index("seq")
    lead, rest = value.shape[0], value.shape[2:]
    piece = (value.shape[1] // ranges,) + rest
    for bit in bits_of("seq"):
        mine = (me // bit) % 2
        halves = value.reshape((lead, ranges // bit // 2, 2) + piece)
        arrived = yield lax.dynamic_index_in_dim(halves, 1 - mine, 2, keepdims=False), "seq", bit
        kept = lax.dynamic_index_in_dim(halves, mine, 2, keepdims=False)
        value = added(kept, arrived, F32 if 2 * bit == ranges else value.dtype)
    return value.reshape((lead,) + piece)


def weight_sum(kept, sent, ranges_first):
    arrived = yield sent, "head", 1
    value = added(kept, arrived)
    bits = bits_of("head")[1:]
    if ranges_first:
        value = yield from ranges_sum(value)
        return (yield from head_sum(value, bits))
    value = yield from head_sum(value, bits)
    return (yield from ranges_sum(value[None]))[0]


def sum_of_state(value):
    for bit in bits_of("head"):
        arrived = yield value, "head", bit
        value = added(value, arrived)
    return (yield from ranges_sum(value[None]))[0]


class Chain(Held):
    def __init__(self, steps):
        super().__init__()
        self.steps, self.done = steps, False
        self.advance()

    def advance(self):
        if self.done:
            return
        try:
            self.value = swapped(*self.steps.send(self.value))
        except StopIteration as end:
            self.value, self.done = end.value, True

    def finish(self):
        while not self.done:
            self.advance()
        return self.value


def assembled(parts, edges=None):
    n = len(parts)
    me = lax.axis_index("head")
    pieces, places, last_rows = [], [], []
    for s in range(n):
        for r, part in enumerate(parts[s]):
            pieces.append(part)
            places.append((me ^ r) * n + s)
            if edges is not None:
                last_rows.append(edges[r][s : s + 1])
    return assemble(pieces, last_rows, places)


def padded_lanes(value, size):
    return jnp.pad(value, ((0, 0), (0, size - value.shape[1])))


def shards(
    tokens,
    doc_ids,
    norm_gain,
    head_input_weight,
    state_input_weight,
    timestep_input_weight,
    conv_x,
    conv_state,
    head_params,
    gated_gain,
    output_weight,
    cotangent,
):
    seqs, length, model = tokens.shape
    blocks = lax.axis_size("head")
    ranges = lax.axis_size("seq")
    n = seqs // blocks
    width = gated_gain.shape[0]
    heads = head_params.shape[1]
    me = lax.axis_index("head")
    tokens = lax.dynamic_slice_in_dim(tokens, me * n, n, 0)
    cotangent = lax.dynamic_slice_in_dim(cotangent, me * n, n, 0)
    before = lax.ppermute(tokens[:, length - PAD :], "seq", [(i, i + 1) for i in range(ranges - 1)])
    padded = jnp.concatenate([before, tokens], axis=1)

    start = lax.axis_index("seq") * length
    lead = jnp.concatenate(
        [jnp.full((seqs, PAD), -1, jnp.int32), doc_ids, jnp.full((seqs, PAD), -2, jnp.int32)], axis=1
    )
    ids = lax.dynamic_slice(lead, (me * n, start), (n, length + 2 * PAD)).astype(F32)
    id_rows = jnp.broadcast_to(ids[:, None], (n, 8, length + 2 * PAD))
    ids = jnp.broadcast_to(ids[:, :, None], (n, length + 2 * PAD, LANES))

    pack = jnp.concatenate(
        [
            conv_x,
            gated_gain[None],
            padded_lanes(head_params, width),
            *[jnp.transpose(timestep_input_weight[q : q + width]).astype(F32) for q in range(0, model, width)],
        ],
        axis=0,
    )
    half = blocks // 2
    packs, side = lax.optimization_barrier((reached(pack), head_input_weight.reshape(model, 2 * width)))
    packs = forwarded(packs)
    row_parts = reached(side[:, width:])
    small, step_weights, params = arrange(packs, heads, model)
    state_taps = jnp.pad(conv_state, ((0, 3), (0, 0)))

    tok_float = padded.astype(F32)
    scale = lax.rsqrt(jnp.mean(tok_float * tok_float, axis=-1, keepdims=True) + EPS)
    normed = (tok_float * scale * norm_gain).astype(BF16)
    rows, raw, steps, log_decay, cum, state_rows, bc = project_first(
        normed, state_input_weight, step_weights, small, ids, id_rows, state_taps, [row_parts[0], row_parts[1]], blocks,
        heads * blocks,
    )
    row_parts, rows, gate_own, out_own = lax.optimization_barrier(
        (row_parts, rows, side[:, :width], output_weight)
    )
    row_weights = forwarded(row_parts)
    cuts = ranges // (blocks * n)
    held = state_call(rows, bc, ids, id_rows, steps, cum, params, (), 0, 2, heads, cuts)
    held, rows = lax.optimization_barrier((held, rows))
    acted, message = held
    for r in range(2, blocks, 2):
        rows = project_more(normed, rows, row_weights[r : r + 2], r)
        acted, message = state_call(rows, bc, ids, id_rows, steps, cum, params, (acted, message), r, 2, heads, cuts)
    mixed, states = inside_call(acted, bc, ids, id_rows, steps, cum, heads)
    mixed, arrived = Held(mixed), Held(send_message(message))
    meet(arrived, mixed)
    entered = Held(send_back(relay(arrived.value, False), blocks, n))
    gate_weights = gathered(gate_own)
    out_weights = gathered(out_own)
    gate = Held(project_gate(normed, gate_weights))
    meet(entered, gate)

    cuts = ranges // blocks
    every = range(n)
    outs, normed_outs, d_gates, d_sums, messages, gain_parts, skip_parts = [[] for _ in range(7)]
    for s in every:
        parts = middle_call(
            s, mixed.value, gate.value, acted, cum, entered.value, bc, ids, tokens, cotangent, params, out_weights, heads,
            cuts,
        )
        for held, part in zip((outs, normed_outs, d_gates, d_sums, messages), parts):
            held.append(Held(part))
        gain_parts.append(parts[5])
        skip_parts.append(parts[6])
        meet(entered, messages[s])
    for out in outs:
        out.value = crossed(out.value)
    d_scaled, insides, leaving, d_rows, d_raws, d_states, closes = [[] for _ in range(7)]

    def inside_back():
        s = len(d_scaled)
        part, *rest = inside_back_call(
            s, acted, d_sums[s].value, mixed.value, bc, ids, id_rows, steps, cum, states, entered.value, heads
        )
        d_scaled.append(Held(part))
        insides.append(rest)

    def close():
        s = len(d_rows)
        d_b, d_c, d_cum = insides[s]
        parts = close_call(
            s, rows, acted, d_sums[s].value, d_scaled[s].value, bc, ids, id_rows, steps, raw, log_decay, cum, d_cum,
            leaving[s].value, entered.value, params, small, state_rows, state_taps, d_b, d_c, heads,
        )
        for held, part in zip((d_rows, d_raws, d_states), parts):
            held.append(Held(part))
        closes.append(parts[3:])

    for s in every:
        arrived = Held(send_message(messages[s].value))
        if s:
            inside_back()
            meet(arrived, d_scaled[s], out_sum, gate_sum)
        else:
            meet(arrived, *messages[1:])
        carried = Held(relay(arrived.value, True))
        if s:
            out_sum.advance()
            meet(carried, leaving[s - 1])
        else:
            meet(carried, d_sums[0], *normed_outs, *d_gates)
        leaving.append(Held(send_back(carried.value, blocks, 1)))
        if s:
            close()
            meet(leaving[s], d_rows[s - 1], out_sum)
            out_sum.advance()
            gate_sum.advance()
        else:
            inside_back()
            out_grads = Held(weight_grad(cotangent, values(normed_outs)))
            gate_grads = Held(weight_grad(normed, values(d_gates)))
            meet(leaving[0], d_scaled[0], out_grads, gate_grads, *outs, *messages[1:], *d_sums[1:])
            out_sum = Chain(weight_sum(*out_grads.value, False))
            gate_sum = Chain(weight_sum(*gate_grads.value, False))
    close()
    meet(d_rows[-1], out_sum)
    out_sum.advance()

    state_part = Held(state_grad(normed, values(d_states)))
    meet(state_part, *d_rows)
    state_sum = Chain(sum_of_state(state_part.value))
    rows_grads = Held(weight_grad(normed, values(d_rows)))
    gain = Held(norm_gain[None])
    meet(rows_grads, out_sum, gate_sum, gain, state_sum)
    for chain in (out_sum, gate_sum, state_sum):
        chain.advance()
    rows_sum = Chain(weight_sum(*rows_grads.value, True))
    meet(rows_sum, gain)
    rows_sum.advance()
    inputs, edges, halos, norm_parts = [], [], [], []
    for s in every:
        *parts, norm_part = input_call(
            s, d_gates[s].value, d_rows[s].value, d_raws[s].value, d_states[s].value, padded, cotangent, gain.value,
            state_input_weight, step_weights, row_weights, gate_weights,
        )
        for held, part in zip((inputs, edges, halos), parts):
            held.append(Held(part))
        norm_parts.append(norm_part)
        if s < n - 1:
            meet(gain, inputs[s], gate_sum, out_sum, state_sum)
            gate_sum.advance()
            out_sum.advance()
            state_sum.advance()
            inputs[s].value = crossed(inputs[s].value)
    meet(inputs[-1], rows_sum, state_sum, gate_sum, *halos, *edges, *outs)
    for chain in (rows_sum, state_sum, gate_sum):
        chain.advance()
    inputs[-1].value = crossed(inputs[-1].value)
    smalls = pack_sums(
        normed, width, heads, blocks, values(d_raws), *[[c[i] for c in closes] for i in range(3)], gain_parts, skip_parts,
        norm_parts,
    )
    halo = Held(lax.ppermute(jnp.concatenate(values(halos), axis=0), "seq", [(i + 1, i) for i in range(ranges - 1)]))
    own = Held(list(smalls))
    meet(own, *inputs[:-1])
    own.value = [swapped(part, "head", r) if r else part for r, part in enumerate(own.value)]
    output = Held(assembled([completed(part) for part in values(outs)]))
    meet(own, output)
    own.value = tree_sum(own.value)
    steps = bits_of("seq")
    for i, bit in enumerate(steps):
        came = Held(swapped(own.value, "seq", bit))
        also = [gate_sum, halo] if i == 0 else inputs if i == 1 else [whole_input] if i == 2 else []
        meet(came, own, rows_sum, state_sum, *also)
        for chain in (rows_sum, state_sum):
            chain.advance()
        own.value = own.value + came.value
        if i == 0:
            gate_sum.advance()
            edge = crossed(added(jnp.concatenate(values(edges), axis=0), halo.value, BF16))
        if i == 1:
            whole_input = Held(assembled([completed(part) for part in values(inputs)], completed(edge)))
    out_grad = jnp.transpose(out_sum.finish())
    both = own.value
    norm_grad, steps_grad, taps_grad, state_taps_grad, params_grad, gains_grad = unpack_sums(both, heads, model)
    return (
        output.value,
        whole_input.value,
        norm_grad.reshape(model),
        jnp.stack([gate_sum.finish(), rows_sum.finish()], axis=1),
        state_sum.finish(),
        jnp.transpose(steps_grad),
        taps_grad,
        state_taps_grad,
        params_grad,
        gains_grad.reshape(width),
        out_grad,
    )


def solution(mesh):
    return jax.shard_map(
        shards,
        mesh=mesh,
        in_specs=(
            P(None, "seq", None),
            P(),
            P(),
            P(None, None, "head"),
            P(),
            P(None, "head"),
            P(None, "head"),
            P(),
            P(None, "head"),
            P("head"),
            P("head", None),
            P(None, "seq", None),
        ),
        out_specs=(
            P(None, "seq", None),
            P(None, "seq", None),
            P(),
            P("seq", None, "head"),
            P("seq", None),
            P(None, "head"),
            P(None, "head"),
            P(),
            P(None, "head"),
            P("head"),
            P("head", "seq"),
        ),
        check_vma=False,
    )
```

```python
import functools

import jax
import jax.numpy as jnp
from jax import lax
from jax.experimental import pallas as pl
from jax.experimental.pallas import tpu as pltpu
from jax.sharding import PartitionSpec as P

F32 = jnp.float32
BF16 = jnp.bfloat16
EPS = 1e-5
CHUNK = 128
PAD = 16
LANES = 128
HEAD_DIM = 64
VMEM = 60 * 1024 * 1024


def dot(a, b):
    return lax.dot_general(a, b, (((1,), (0,)), ((), ())), preferred_element_type=F32)


def dot_nt(a, b):
    return lax.dot_general(a, b, (((1,), (1,)), ((), ())), preferred_element_type=F32)


def dot_tn(a, b):
    return lax.dot_general(a, b, (((0,), (0,)), ((), ())), preferred_element_type=F32)


def split(value):
    high = value.astype(BF16)
    return high, (value - high.astype(F32)).astype(BF16)


def head_map(width, offset):
    lane = lax.broadcasted_iota(jnp.int32, (LANES, width), 1)
    row = lax.broadcasted_iota(jnp.int32, (LANES, width), 0)
    return (lax.shift_right_logical(lane, 6) + offset == row).astype(F32).astype(BF16)


def expand(value, width, offset):
    lane = lax.shift_right_logical(lax.broadcasted_iota(jnp.int32, value.shape, 1), 6) + offset
    return jnp.concatenate(
        [jnp.take_along_axis(value, lane + 2 * p, axis=1) for p in range(width // LANES)], axis=1
    )


def expand_row(value, width, offset):
    return expand(jnp.broadcast_to(value, (8, LANES)), width, offset)


def column(value, index):
    return jnp.take_along_axis(value, jnp.zeros(value.shape, jnp.int32) + index, axis=1)


def by_head(value, heads):
    high, low = split(value)
    return dot_nt(high, heads) + dot_nt(low, heads)


def by_head_low(value, heads):
    return dot_nt(value.astype(BF16), heads)


def widen(value, width):
    return jnp.concatenate([value] * (width // LANES), axis=1)


def fold8(value):
    return value[0:8] + value[8:16]


def sigmoid(value):
    return 0.5 * jnp.tanh(0.5 * value) + 0.5


def triangle(lower):
    row = lax.broadcasted_iota(jnp.int32, (CHUNK, CHUNK), 0)
    column = lax.broadcasted_iota(jnp.int32, (CHUNK, CHUNK), 1)
    return (row >= column if lower else row <= column)


def exact_dot(ones, value):
    return jnp.dot(ones, value, precision=lax.Precision.HIGHEST, preferred_element_type=F32)


def rows_at(start, count):
    return pl.ds(pl.multiple_of(start, 16), count)


def entering_maps(columns, rows, first, count):
    window = count + PAD
    token = lax.broadcasted_iota(jnp.int32, (count, window), 0)
    entry = lax.broadcasted_iota(jnp.int32, (count, window), 1)
    same = wide_marks(columns[0, first : first + count, :], window) == rows[0, 0:1, first - PAD : first + count]
    distance = entry - token
    return jnp.concatenate(
        [jnp.where(same & (distance == PAD - 3 + k), 1.0, 0.0).astype(BF16) for k in range(3)], axis=0
    )


def leaving_maps(columns, rows, first, count):
    window = count + PAD
    row = lax.broadcasted_iota(jnp.int32, (count, window), 0)
    token = lax.broadcasted_iota(jnp.int32, (count, window), 1)
    same = wide_marks(columns[0, first : first + count, :], window) == rows[0, 0:1, first : first + window]
    distance = token - row
    return jnp.concatenate(
        [jnp.where(same & (distance == 3 - k), 1.0, 0.0).astype(BF16) for k in range(3)], axis=0
    )


def wide_marks(columns, window):
    whole = jnp.concatenate([columns] * -(-window // LANES), axis=1)
    return whole[:, :window]


def conv_sum(rows, maps, taps, first, lanes):
    moved = dot(maps, rows[first - PAD : first + CHUNK, lanes])
    entering = [moved[k * CHUNK : (k + 1) * CHUNK] for k in range(3)]
    entering.append(rows[first : first + CHUNK, lanes].astype(F32))
    total = taps[4:5, lanes]
    for k in range(4):
        total = total + taps[k : k + 1, lanes] * entering[k]
    return total, entering


def lane_groups(width):
    step = min(width, 2 * LANES)
    return [slice(i, i + step) for i in range(0, width, step)]


def conv_forward(rows, ids, id_rows, taps, store, length):
    for c in range(length // CHUNK):
        first = PAD + c * CHUNK
        maps = entering_maps(ids, id_rows, first, CHUNK)
        for lanes in lane_groups(rows.shape[1]):
            total, _ = conv_sum(rows, maps, taps, first, lanes)
            store(slice(c * CHUNK, (c + 1) * CHUNK), lanes, (total * sigmoid(total)).astype(BF16))


def conv_backward(rows, ids, id_rows, taps, d_acted, d_pre, d_rows, length):
    width = d_pre.shape[1]
    zero = jnp.zeros((16, width), BF16)
    d_pre[0:16, :] = zero
    d_pre[length + PAD : length + PAD + 16, :] = zero
    groups = lane_groups(width)
    sums = [[jnp.zeros((8, g.stop - g.start), F32) for _ in range(5)] for g in groups]
    for c in range(length // CHUNK - 1, -1, -1):
        first = PAD + c * CHUNK
        here = slice(first, first + CHUNK)
        maps = entering_maps(ids, id_rows, first, CHUNK)
        back = leaving_maps(ids, id_rows, first, CHUNK)
        for i, lanes in enumerate(groups):
            total, entering = conv_sum(rows, maps, taps, first, lanes)
            sigma = sigmoid(total)
            grad = d_acted(c, lanes) * (sigma * (1.0 + total * (1.0 - sigma)))
            d_pre[here, lanes] = grad.astype(BF16)
            for k in range(5):
                product = grad * entering[k] if k < 4 else grad
                sums[i][k] = sums[i][k] + jnp.sum(product.reshape(CHUNK // 8, 8, -1), axis=0)
            moved = dot(back, d_pre[first : first + CHUNK + PAD, lanes])
            result = taps[3:4, lanes] * grad
            for k in range(3):
                result = result + taps[k : k + 1, lanes] * moved[k * CHUNK : (k + 1) * CHUNK]
            d_rows(here, lanes, result.astype(BF16))
    back = leaving_maps(ids, id_rows, 0, PAD)
    for lanes in groups:
        moved = dot(back, d_pre[0 : 2 * PAD, lanes])
        result = taps[0:1, lanes] * moved[0:PAD]
        for k in range(1, 3):
            result = result + taps[k : k + 1, lanes] * moved[k * PAD : (k + 1) * PAD]
        d_rows(slice(0, PAD), lanes, result.astype(BF16))
    return [
        jnp.concatenate([jnp.sum(part[k], axis=0, keepdims=True) for part in sums], axis=1) for k in range(5)
    ]


def softplus(value):
    return jnp.maximum(value, 0.0) + jnp.log1p(jnp.exp(-jnp.abs(value)))


def arrange_kernel(heads, *refs):
    packs, (small, steps, params) = refs[:-3], refs[-3:]
    blocks, _, width = params.shape
    model = steps.shape[1]
    lane = lax.broadcasted_iota(jnp.int32, (8, LANES), 1)
    values = jnp.zeros((8, LANES), F32)
    rows = []
    for r, pack in enumerate(packs):
        own = jnp.concatenate([pack[6:9, :LANES], jnp.zeros((5, LANES), F32)], axis=0)
        placed = pltpu.roll(own, r * heads, 1) if r else own
        values = jnp.where((lane >= r * heads) & (lane < (r + 1) * heads), placed, values)
        skip = expand(jnp.broadcast_to(pack[8:9, :LANES], (8, LANES)), width, 0)[0:1]
        params[r] = jnp.concatenate([pack[0:6, :], skip, jnp.zeros((1, width), F32)], axis=0)
        rows.append(
            jnp.concatenate([pack[9 + q * heads : 9 + (q + 1) * heads, :] for q in range(model // width)], axis=1)
        )
    rows.append(jnp.zeros((LANES - blocks * heads, model), F32))
    small[...] = values
    steps[...] = jnp.concatenate(rows, axis=0).astype(BF16)


def arrange(packs, heads, model):
    width = packs[0].shape[1]
    return pl.pallas_call(
        functools.partial(arrange_kernel, heads),
        out_shape=[
            jax.ShapeDtypeStruct((8, LANES), F32),
            jax.ShapeDtypeStruct((LANES, model), BF16),
            jax.ShapeDtypeStruct((len(packs), 8, width), F32),
        ],
        name="arrange",
    )(*packs)


def project_rows(values, weights, rows):
    for r, weight in enumerate(weights):
        rows[r, 0] = dot(values, weight[...]).astype(BF16)


def project_first_kernel(blocks, heads, normed, state_w, step_w, small, ids, id_rows, taps, *refs):
    weights, refs = refs[:blocks], refs[blocks:]
    rows, raw, steps, log_decay, cum, state_rows, bc = refs
    length = bc.shape[1]
    values = normed[0]
    state_rows[0] = dot(values, state_w[...]).astype(BF16)
    part = dot_nt(values[PAD:], step_w[...])
    raw[0] = part
    lane = lax.broadcasted_iota(jnp.int32, (length, LANES), 1)
    size = jnp.where(lane < heads, softplus(part + small[0:1, :]), 0.0)
    steps[0] = size
    log_decay[0] = -size * jnp.exp(small[1:2, :])
    ones = triangle(True).astype(F32)
    total = jnp.zeros((1, LANES), F32)
    for c in range(length // CHUNK):
        here = slice(c * CHUNK, (c + 1) * CHUNK)
        value = exact_dot(ones, log_decay[0, here, :]) + total
        cum[0, here, :] = value
        total = value[CHUNK - 1 : CHUNK]

    def store(here, lanes, value):
        bc[0, here, lanes] = value

    conv_forward(state_rows.at[0], ids, id_rows, taps[...], store, length)
    project_rows(values, weights, rows)


def project_more_kernel(blocks, normed, held, *refs):
    project_rows(normed[0], refs[:blocks], refs[blocks])


def project_first(normed, state_w, step_w, small, ids, id_rows, taps, weights, blocks, heads):
    n, padded, model = normed.shape
    width = weights[0].shape[1]
    length = padded - PAD
    whole = lambda a: pl.BlockSpec(a.shape, lambda s: (0,) * a.ndim, pipeline_mode=pl.Buffered(1))
    per_seq = lambda a, b: pl.BlockSpec((1, a, b), lambda s: (s, 0, 0))
    lanes = jax.ShapeDtypeStruct((n, length, LANES), F32)
    return pl.pallas_call(
        functools.partial(project_first_kernel, len(weights), heads),
        grid=(n,),
        in_specs=[
            per_seq(padded, model), whole(state_w), whole(step_w), whole(small), per_seq(*ids.shape[1:]),
            per_seq(*id_rows.shape[1:]), whole(taps),
        ] + [whole(v) for v in weights],
        out_specs=[pl.BlockSpec((len(weights), 1, padded, width), lambda s: (0, s, 0, 0))]
        + [per_seq(length, LANES)] * 4
        + [per_seq(padded, 2 * LANES), per_seq(length, 2 * LANES)],
        out_shape=[
            jax.ShapeDtypeStruct((blocks, n, padded, width), BF16), lanes, lanes, lanes, lanes,
            jax.ShapeDtypeStruct((n, padded, 2 * LANES), BF16),
            jax.ShapeDtypeStruct((n, length, 2 * LANES), BF16),
        ],
        compiler_params=pltpu.CompilerParams(vmem_limit_bytes=VMEM),
        name="project_first",
    )(normed, state_w, step_w, small, ids, id_rows, taps, *weights)


def project_more(normed, rows, weights, first):
    n, padded, model = normed.shape
    width = weights[0].shape[1]
    count = len(weights)
    return pl.pallas_call(
        functools.partial(project_more_kernel, count),
        grid=(n,),
        in_specs=[pl.BlockSpec((1, padded, model), lambda s: (s, 0, 0)), pl.BlockSpec(memory_space=pl.ANY)]
        + [pl.BlockSpec(v.shape, lambda s: (0, 0), pipeline_mode=pl.Buffered(1)) for v in weights],
        out_specs=pl.BlockSpec((count, 1, padded, width), lambda s: (first // count, s, 0, 0)),
        out_shape=jax.ShapeDtypeStruct(rows.shape, BF16),
        input_output_aliases={1: 0},
        compiler_params=pltpu.CompilerParams(vmem_limit_bytes=VMEM),
        name="project_more",
    )(normed, rows, *weights)


def project_gate_kernel(blocks, normed, *refs):
    for r in range(blocks):
        refs[blocks][r, 0] = dot(normed[0, PAD:, :], refs[r][...]).astype(BF16)


def project_gate(normed, weights):
    n, padded, model = normed.shape
    width = weights[0].shape[1]
    count = len(weights)
    return pl.pallas_call(
        functools.partial(project_gate_kernel, count),
        grid=(n,),
        in_specs=[pl.BlockSpec((1, padded, model), lambda s: (s, 0, 0))]
        + [pl.BlockSpec(v.shape, lambda s: (0, 0), pipeline_mode=pl.Buffered(1)) for v in weights],
        out_specs=pl.BlockSpec((count, 1, padded - PAD, width), lambda s: (0, s, 0, 0)),
        out_shape=jax.ShapeDtypeStruct((count, n, padded - PAD, width), BF16),
        compiler_params=pltpu.CompilerParams(vmem_limit_bytes=VMEM),
        name="project_gate",
    )(normed, *weights)


def write_message(message, state, survive):
    cuts, rows, width = message.shape
    own = rows - 16
    survive = jnp.concatenate([survive, survive], axis=0).astype(BF16)
    for i in range(cuts):
        message[i, :own, :] = state[i * own : (i + 1) * own].astype(BF16)
        message[i, own:, :] = survive


def state_kernel(first, per_block, rows, bc, ids, id_rows, steps, cum, taps, *refs):
    acted, message = refs[-2:]
    length, width = acted.shape[2:]
    offset = (pl.program_id(0) + first) * per_block

    def store(here, lanes, value):
        acted[0, 0, here, lanes] = value

    conv_forward(rows.at[0, 0], ids, id_rows, taps[0], store, length)
    total = cum[0, length - 1 : length, :]
    last = ids[0, PAD + length - 1 : PAD + length, :]
    before = ids[0, PAD - 1 : PAD, :]
    state = jnp.zeros((LANES, width), F32)
    for c in range(length // CHUNK):
        here = slice(c * CHUNK, (c + 1) * CHUNK)
        same = (ids[0, PAD + c * CHUNK : PAD + (c + 1) * CHUNK, :] == last).astype(F32)
        tail = jnp.exp(total - cum[0, here, :]) * same * steps[0, here, :]
        scaled = (expand(tail, width, offset) * acted[0, 0, here, :].astype(F32)).astype(BF16)
        state = state + dot_tn(bc[0, here, :LANES], scaled)
    survive = jnp.exp(total) * (last == before).astype(F32)
    write_message(message.at[0, 0], state, expand_row(survive, width, offset))


def state_call(rows, bc, ids, id_rows, steps, cum, taps, held, first, count, per_block, cuts):
    blocks, n, padded, width = rows.shape
    length = padded - PAD
    four = lambda a, b: pl.BlockSpec((1, 1, a, b), lambda g, s: (g + first, s, 0, 0))
    per_seq = lambda a: pl.BlockSpec((1,) + a.shape[1:], lambda g, s: (s, 0, 0))
    piece = LANES // cuts + 16
    return pl.pallas_call(
        functools.partial(state_kernel, first, per_block),
        grid=(count, n),
        in_specs=[
            four(padded, width), per_seq(bc), per_seq(ids), per_seq(id_rows), per_seq(steps), per_seq(cum),
            pl.BlockSpec((1,) + taps.shape[1:], lambda g, s: (g + first, 0, 0)),
        ] + [pl.BlockSpec(memory_space=pl.ANY) for _ in held],
        out_specs=[
            four(length, width),
            pl.BlockSpec((1, 1, cuts, piece, width), lambda g, s: (g + first, s, 0, 0, 0)),
        ],
        out_shape=[
            jax.ShapeDtypeStruct((blocks, n, length, width), BF16),
            jax.ShapeDtypeStruct((blocks, n, cuts, piece, width), BF16),
        ],
        input_output_aliases={7: 0, 8: 1} if held else {},
        compiler_params=pltpu.CompilerParams(vmem_limit_bytes=VMEM),
        name="range_state",
    )(rows, bc, ids, id_rows, steps, cum, taps, *held)


def chunk_marks(ids, c):
    first = PAD + c * CHUNK
    return ids[0, first : first + CHUNK, :], ids[0, first + CHUNK - 1 : first + CHUNK, :], ids[0, first - 1 : first, :]


def chunk_decays(ids, cum, c):
    here, last, before = chunk_marks(ids, c)
    value = cum[0, c * CHUNK : (c + 1) * CHUNK, :]
    base = cum[0, c * CHUNK - 1 : c * CHUNK, :] if c else jnp.zeros((1, LANES), F32)
    end = value[CHUNK - 1 : CHUNK]
    entering = jnp.exp(value - base) * (here == before).astype(F32)
    tail = jnp.exp(end - value) * (here == last).astype(F32)
    survive = jnp.exp(end - base) * (last == before).astype(F32)
    return entering, tail, survive


def lane_halves(pair):
    lane = lax.broadcasted_iota(jnp.int32, pair.shape, 1)
    zero = jnp.zeros_like(pair)
    return jnp.concatenate([jnp.where(lane < HEAD_DIM, pair, zero), jnp.where(lane < HEAD_DIM, zero, pair)], axis=0)


def inside_kernel(per_block, acted, bc, ids, id_rows, steps, cum, mixed, states, carried, turned):
    length, width = acted.shape[2:]
    offset = pl.program_id(1) * per_block
    later = triangle(True)
    for c in range(length // CHUNK):
        here = slice(c * CHUNK, (c + 1) * CHUNK)
        b_part, c_part = bc[0, here, :LANES], bc[0, here, LANES:]
        marks, _, _ = chunk_marks(ids, c)
        same = later & (marks == id_rows[0, 0:1, PAD + c * CHUNK : PAD + (c + 1) * CHUNK])
        scores = jnp.where(same, dot_nt(c_part, b_part), 0.0)
        value = cum[0, here, :]
        turned[...] = jnp.transpose(value)
        entering, tail, survive = chunk_decays(ids, cum, c)
        scaled = (expand(steps[0, here, :], width, offset) * acted[0, 0, here, :].astype(F32)).astype(BF16)
        if c:
            held = carried[...]
            held_low = held.astype(BF16)
            states[0, 0, c - 1] = held_low
            outside = dot(c_part, held_low) * expand(entering, width, offset)
        for pair in range(width // LANES):
            lanes = slice(pair * LANES, (pair + 1) * LANES)
            mixing = []
            for h in (2 * pair, 2 * pair + 1):
                spread = jnp.minimum(column(value, offset + h) - turned[pl.ds(offset + h, 1), :], 0.0)
                mixing.append((scores * jnp.exp(spread)).astype(BF16))
            result = dot(jnp.concatenate(mixing, axis=1), lane_halves(scaled[:, lanes]))
            mixed[0, 0, here, lanes] = result + outside[:, lanes] if c else result
        if c + 1 < length // CHUNK:
            fresh = dot_tn(b_part, (expand(tail, width, offset) * scaled.astype(F32)).astype(BF16))
            if c:
                fresh = fresh + held * expand_row(survive, width, offset)[0:1]
            carried[...] = fresh


def inside_call(acted, bc, ids, id_rows, steps, cum, per_block):
    blocks, n, length, width = acted.shape
    chunks = length // CHUNK
    four = lambda a, b: pl.BlockSpec((1, 1, a, b), lambda s, g: (g, s, 0, 0))
    per_seq = lambda a: pl.BlockSpec((1,) + a.shape[1:], lambda s, g: (s, 0, 0))
    return pl.pallas_call(
        functools.partial(inside_kernel, per_block),
        grid=(n, blocks),
        in_specs=[four(length, width), per_seq(bc), per_seq(ids), per_seq(id_rows), per_seq(steps), per_seq(cum)],
        out_specs=[
            four(length, width),
            pl.BlockSpec((1, 1, chunks - 1, LANES, width), lambda s, g: (g, s, 0, 0, 0)),
        ],
        out_shape=[
            jax.ShapeDtypeStruct((blocks, n, length, width), F32),
            jax.ShapeDtypeStruct((blocks, n, chunks - 1, LANES, width), BF16),
        ],
        scratch_shapes=[pltpu.VMEM((LANES, width), F32), pltpu.VMEM((LANES, LANES), F32)],
        compiler_params=pltpu.CompilerParams(vmem_limit_bytes=VMEM),
        name="inside",
    )(acted, bc, ids, id_rows, steps, cum)


def relay_kernel(backward, message, carried):
    ranges, rows, width = carried.shape
    state = jnp.zeros((rows, width), F32)
    order = range(ranges - 1, -1, -1) if backward else range(ranges)
    for q in order:
        carried[q] = state.astype(BF16)
        decay = message[q, rows : rows + 1, :].astype(F32)
        state = state * decay + message[q, :rows, :].astype(F32)


class Held:
    def __init__(self, value=None):
        self.value = value


def meet(*held):
    for h, value in zip(held, lax.optimization_barrier(tuple(h.value for h in held))):
        h.value = value


def values(held):
    return [h.value for h in held]


def over_ranges(value):
    return lax.all_to_all(value, "seq", 0, 0, tiled=True)


def send_message(message):
    return over_ranges(message.reshape(lax.axis_size("seq"), message.shape[3], message.shape[4]))


def relay(arrived, backward):
    ranges, rows, width = arrived.shape
    return pl.pallas_call(
        functools.partial(relay_kernel, backward),
        out_shape=jax.ShapeDtypeStruct((ranges, rows - 16, width), BF16),
        compiler_params=pltpu.CompilerParams(vmem_limit_bytes=VMEM),
        name="relay",
    )(arrived)


def send_back(carried, blocks, n):
    return over_ranges(carried).reshape(blocks, n, LANES, carried.shape[2])


def middle_kernel(
    blocks, per_block, total_width, mixed, gate, acted, cum, cum_end, bc, ids, ids_before, ids_after, tokens, cotangent,
    params, entered, *refs
):
    weights, refs = refs[:blocks], refs[blocks:]
    output, normed_out, d_gate, d_summed, pulled, gain_grad, skip_grad = refs[:7]
    summed_s, gated_s, grad_s, first_s, second_s, low_s, row_s, pull_s, sigma_s = refs[7:]
    tile, width = mixed.shape[2:]
    t = pl.program_id(0)
    before = ids_before[0, PAD - 1 : PAD, :]
    marks = ids[0]
    c_part = bc[0, :, LANES:]
    slabs = tile // 16
    same = (marks == before).astype(F32)
    decay = jnp.exp(cum[0]) * same
    row_s[...] = jnp.zeros_like(row_s)

    def lanes_sum(value):
        total = value[:, :LANES]
        for i in range(1, width // LANES):
            total = total + value[:, i * LANES : (i + 1) * LANES]
        return total

    @pl.when(t == 0)
    def _():
        gain_grad[...] = jnp.zeros_like(gain_grad)
        skip_grad[...] = jnp.zeros_like(skip_grad)
        pull_s[...] = jnp.zeros_like(pull_s)

    for r in range(blocks):
        first_s[...] = dot(c_part, entered[r, 0])
        second_s[r] = expand(decay, width, r * per_block)
        skip = params[r, 6:7, :]

        def step(i, carry, r=r, skip=skip):
            here = rows_at(i * 16, 16)
            value = mixed[r, 0, here, :] + first_s[here, :] * second_s[r, here, :]
            summed = value + skip * acted[r, 0, here, :].astype(F32)
            g = gate[r, 0, here, :].astype(F32)
            sigma = sigmoid(g)
            gated = summed * (g * sigma)
            sigma_s[r, here, :] = sigma
            summed_s[r, here, :] = summed
            gated_s[r, here, :] = gated
            row_s[here, :] = row_s[here, :] + lanes_sum(gated * gated)
            return carry

        lax.fori_loop(0, slabs, step, 0, unroll=8)
    squares = jnp.sum(row_s[...], axis=1, keepdims=True)
    rescale = jnp.broadcast_to(lax.rsqrt(squares / total_width + EPS), (tile, LANES))
    row_s[...] = rescale
    for r in range(blocks):
        gain = params[r, 5:6, :]

        def step(i, carry, r=r, gain=gain):
            here = rows_at(i * 16, 16)
            normed_out[r, 0, here, :] = (gated_s[r, here, :] * widen(row_s[here, :], width) * gain).astype(BF16)
            return carry

        lax.fori_loop(0, slabs, step, 0, unroll=8)
    branch = tokens[0].astype(F32)
    for r in range(blocks):
        branch = branch + dot(normed_out[r, 0], weights[r][...])
    output[0] = branch.astype(BF16)
    first_s[:, :LANES] = jnp.zeros((tile, LANES), F32)
    for r in range(blocks):
        grad_s[r] = dot_nt(cotangent[0], weights[r][...])
        gain = params[r, 5:6, :]

        def step(i, total, r=r, gain=gain):
            here = rows_at(i * 16, 16)
            both = grad_s[r, here, :] * gated_s[r, here, :]
            first_s[here, :LANES] = first_s[here, :LANES] + lanes_sum(both * gain)
            return total + fold8(both * widen(row_s[here, :], width))

        gain_grad[r] = gain_grad[r] + lax.fori_loop(0, slabs, step, jnp.zeros((8, width), F32), unroll=8)
    cross = jnp.sum(first_s[:, :LANES], axis=1, keepdims=True) / total_width
    first_s[:, :LANES] = rescale * rescale * rescale * cross
    for r in range(blocks):
        gain = params[r, 5:6, :]

        def step(i, total, r=r, gain=gain):
            here = rows_at(i * 16, 16)
            sigma = sigma_s[r, here, :]
            silu = gate[r, 0, here, :].astype(F32) * sigma
            d_gated = widen(row_s[here, :], width) * (grad_s[r, here, :] * gain) - gated_s[r, here, :] * widen(
                first_s[here, :LANES], width
            )
            d_sum = d_gated * silu
            slope = sigma + silu * (1.0 - sigma)
            d_gate[r, 0, here, :] = (d_gated * summed_s[r, here, :] * slope).astype(BF16)
            low = d_sum.astype(BF16)
            d_summed[r, 0, here, :] = low
            low_s[here, :] = (d_sum * second_s[r, here, :]).astype(BF16)
            return total + fold8(d_sum * acted[r, 0, here, :].astype(F32))

        skip_grad[r] = skip_grad[r] + lax.fori_loop(0, slabs, step, jnp.zeros((8, width), F32), unroll=8)
        pull_s[r] = pull_s[r] + dot_tn(c_part, low_s[...])

    @pl.when(t == pl.num_programs(0) - 1)
    def _():
        survive = jnp.exp(cum_end[0, 7:8, :]) * (ids_after[0, PAD - 1 : PAD, :] == before).astype(F32)
        for r in range(blocks):
            write_message(pulled.at[r, 0], pull_s[r], expand_row(survive, width, r * per_block))


def middle_call(s, mixed, gate, acted, cum, entered, bc, ids, tokens, cotangent, params, weights, per_block, cuts):
    blocks, n, length, width = mixed.shape
    model = tokens.shape[2]
    tile = min(256, length)
    wide = lambda w: pl.BlockSpec((blocks, 1, tile, w), lambda t: (0, s, t, 0))
    wide_out = lambda w: pl.BlockSpec((blocks, 1, tile, w), lambda t: (0, 0, t, 0))
    rows = lambda w: pl.BlockSpec((1, tile, w), lambda t: (s, t, 0))
    one = lambda a: pl.BlockSpec((a.shape[0], 1) + a.shape[2:], lambda t: (0, s, 0, 0), pipeline_mode=pl.Buffered(1))
    whole = lambda a: pl.BlockSpec(a.shape, lambda t: (0,) * a.ndim, pipeline_mode=pl.Buffered(1))
    kept = lambda *shape: pl.BlockSpec(shape, lambda t: (0,) * len(shape))
    piece = LANES // cuts + 16
    edge = lambda a: pl.BlockSpec((1, PAD, LANES), lambda t: (s, a, 0))
    ids_here = ids[:, PAD : PAD + length]
    wide_shape = jax.ShapeDtypeStruct((blocks, 1, length, width), BF16)
    return pl.pallas_call(
        functools.partial(middle_kernel, blocks, per_block, width * blocks),
        grid=(length // tile,),
        in_specs=[
            wide(width), wide(width), wide(width), rows(LANES),
            pl.BlockSpec((1, 8, LANES), lambda t: (s, length // 8 - 1, 0)), rows(2 * LANES), rows(LANES),
            edge(0), edge(length // PAD), rows(model), rows(model), whole(params),
            one(entered),
        ] + [whole(v) for v in weights],
        out_specs=[
            pl.BlockSpec((1, tile, model), lambda t: (0, t, 0)), wide_out(width), wide_out(width), wide_out(width),
            kept(blocks, 1, cuts, piece, width), kept(blocks, 8, width), kept(blocks, 8, width),
        ],
        out_shape=[
            jax.ShapeDtypeStruct((1, length, model), BF16),
            wide_shape, wide_shape, wide_shape,
            jax.ShapeDtypeStruct((blocks, 1, cuts, piece, width), BF16),
            jax.ShapeDtypeStruct((blocks, 8, width), F32),
            jax.ShapeDtypeStruct((blocks, 8, width), F32),
        ],
        scratch_shapes=[
            pltpu.VMEM((blocks, tile, width), F32),
            pltpu.VMEM((blocks, tile, width), F32),
            pltpu.VMEM((blocks, tile, width), F32),
            pltpu.VMEM((tile, width), F32),
            pltpu.VMEM((blocks, tile, width), F32),
            pltpu.VMEM((tile, width), BF16),
            pltpu.VMEM((tile, LANES), F32),
            pltpu.VMEM((blocks, LANES, width), F32),
            pltpu.VMEM((blocks, tile, width), F32),
        ],
        compiler_params=pltpu.CompilerParams(vmem_limit_bytes=VMEM),
        name="middle",
    )(mixed, gate, acted, cum, cum, bc, ids_here, ids, ids, tokens, cotangent, params, entered, *weights)


def inside_back_kernel(
    per_block, acted, d_summed, mixed, bc, ids, id_rows, steps, cum, states, entered, d_scaled, d_b, d_c, d_cum,
    carried, turned,
):
    length, width = acted.shape[2:]
    chunks = length // CHUNK
    g = pl.program_id(0)
    offset = g * per_block
    heads = head_map(width, offset)
    sooner = triangle(False)
    first_before = ids[0, PAD - 1 : PAD, :]
    came = entered[0, 0]

    @pl.when(g == 0)
    def _():
        d_b[...] = jnp.zeros_like(d_b)
        d_c[...] = jnp.zeros_like(d_c)
        d_cum[...] = jnp.zeros_like(d_cum)

    for c in range(chunks - 1, -1, -1):
        here = slice(c * CHUNK, (c + 1) * CHUNK)
        b_part, c_part = bc[0, here, :LANES], bc[0, here, LANES:]
        marks, _, _ = chunk_marks(ids, c)
        same = sooner & (marks == id_rows[0, 0:1, PAD + c * CHUNK : PAD + (c + 1) * CHUNK])
        scores_t = jnp.where(same, dot_nt(b_part, c_part), 0.0)
        value = cum[0, here, :]
        turned[...] = jnp.transpose(value)
        entering, tail, survive = chunk_decays(ids, cum, c)
        scaled = (expand(steps[0, here, :], width, offset) * acted[0, 0, here, :].astype(F32)).astype(BF16)
        grad = d_summed[0, 0, here, :]
        grad_wide = grad.astype(F32)
        from_start = jnp.exp(value) * (marks == first_before).astype(F32)
        start_wide = expand(from_start, width, offset)
        d_c_part = dot_nt((grad_wide * start_wide).astype(BF16), came)
        dots = grad_wide * (mixed[0, 0, here, :] + start_wide * dot(c_part, came))
        if c < chunks - 1:
            held = carried[...]
            held_low = held.astype(BF16)
            tail_wide = expand(tail, width, offset)
            later = dot(b_part, held_low) * tail_wide
            d_b_part = dot_nt((tail_wide * scaled.astype(F32)).astype(BF16), held_low)
        if c:
            entering_grad = (expand(entering, width, offset) * grad_wide).astype(BF16)
            d_c_part = d_c_part + dot_nt(entering_grad, states[0, 0, c - 1])
        d_scores_t = jnp.zeros((CHUNK, CHUNK), F32)
        results = []
        for pair in range(width // LANES):
            lanes = slice(pair * LANES, (pair + 1) * LANES)
            products = dot_nt(lane_halves(scaled[:, lanes]), grad[:, lanes])
            mixing = []
            for half, h in enumerate((2 * pair, 2 * pair + 1)):
                spread = jnp.minimum(turned[pl.ds(offset + h, 1), :] - column(value, offset + h), 0.0)
                decay = jnp.exp(spread)
                mixing.append((scores_t * decay).astype(BF16))
                d_scores_t = d_scores_t + products[half * CHUNK : (half + 1) * CHUNK] * decay
            results.append(dot(jnp.concatenate(mixing, axis=1), lane_halves(grad[:, lanes])))
        result = jnp.concatenate(results, axis=1)
        if c < chunks - 1:
            result = result + later
        d_scaled[0, 0, here, :] = result.astype(BF16)
        d_cum[0, here, :] = d_cum[0, here, :] + by_head(dots - scaled.astype(F32) * result, heads)
        d_scores_t = jnp.where(same, d_scores_t, 0.0).astype(BF16)
        d_b_here = dot(d_scores_t, c_part)
        if c < chunks - 1:
            d_b_here = d_b_here + d_b_part
        d_b[0, here, :] = d_b[0, here, :] + d_b_here
        d_c[0, here, :] = d_c[0, here, :] + d_c_part + dot_tn(d_scores_t, b_part)
        if c:
            pulled = dot_tn(c_part, entering_grad)
            if c < chunks - 1:
                pulled = pulled + held * expand_row(survive, width, offset)[0:1]
            carried[...] = pulled


def inside_back_call(s, acted, d_summed, mixed, bc, ids, id_rows, steps, cum, states, entered, per_block):
    blocks, n, length, width = acted.shape
    four = lambda a, b: pl.BlockSpec((1, 1, a, b), lambda g: (g, s, 0, 0))
    own = lambda a, b: pl.BlockSpec((1, 1, a, b), lambda g: (g, 0, 0, 0))
    per_seq = lambda a: pl.BlockSpec((1,) + a.shape[1:], lambda g: (s, 0, 0))
    summed = pl.BlockSpec((1, length, LANES), lambda g: (0, 0, 0))
    lanes = jax.ShapeDtypeStruct((1, length, LANES), F32)
    return pl.pallas_call(
        functools.partial(inside_back_kernel, per_block),
        grid=(blocks,),
        in_specs=[
            four(length, width), own(length, width), four(length, width), per_seq(bc), per_seq(ids), per_seq(id_rows),
            per_seq(steps), per_seq(cum),
            pl.BlockSpec((1, 1) + states.shape[2:], lambda g: (g, s, 0, 0, 0)),
            four(LANES, width),
        ],
        out_specs=[own(length, width), summed, summed, summed],
        out_shape=[jax.ShapeDtypeStruct((blocks, 1, length, width), BF16), lanes, lanes, lanes],
        scratch_shapes=[pltpu.VMEM((LANES, width), F32), pltpu.VMEM((LANES, LANES), F32)],
        compiler_params=pltpu.CompilerParams(vmem_limit_bytes=VMEM),
        name="inside_back",
    )(acted, d_summed, mixed, bc, ids, id_rows, steps, cum, states, entered)


def close_kernel(
    per_block, rows, acted, d_summed, d_scaled, bc, ids, id_rows, steps, raw, log_decay, cum, d_cum, leaving, entered,
    params, small, state_rows, state_taps, d_b, d_c,
    d_rows, d_raw, d_state, taps_grad, state_taps_grad, small_grad, d_pre, d_acted, d_log, d_step, ends, d_bc, d_pre_bc,
):
    length, width = acted.shape[2:]
    chunks = length // CHUNK
    g = pl.program_id(0)
    offset = g * per_block
    heads = head_map(width, offset)
    last = ids[0, PAD + length - 1 : PAD + length, :]
    before = ids[0, PAD - 1 : PAD, :]
    end = cum[0, length - 1 : length, :]
    skip = params[0, 6:7, :]
    held = leaving[0, 0]
    came = entered[0, 0]

    @pl.when(g == 0)
    def _():
        d_bc[:, :LANES] = d_b[0]
        d_bc[:, LANES:] = d_c[0]
        d_log[...] = d_cum[0]
        d_step[...] = jnp.zeros_like(d_step)
        ends[...] = jnp.zeros_like(ends)

    boundary = jnp.zeros((1, LANES), F32)
    for c in range(chunks):
        here = slice(c * CHUNK, (c + 1) * CHUNK)
        marks, _, _ = chunk_marks(ids, c)
        tail = jnp.exp(end - cum[0, here, :]) * (marks == last).astype(F32)
        tail_wide = expand(tail, width, offset)
        steps_wide = expand(steps[0, here, :], width, offset)
        x = acted[0, 0, here, :].astype(F32)
        scaled = (steps_wide * x).astype(BF16).astype(F32)
        later = dot(bc[0, here, :LANES], held) * tail_wide
        total = d_scaled[0, 0, here, :].astype(F32) + later
        d_acted[here, :] = steps_wide * total + skip * d_summed[0, 0, here, :].astype(F32)
        d_bc[here, :LANES] = d_bc[here, :LANES] + dot_nt((tail_wide * scaled).astype(BF16), held)
        from_later = by_head_low(scaled * later, heads)
        boundary = boundary + jnp.sum(from_later, axis=0, keepdims=True)
        d_log[here, :] = d_log[here, :] - from_later
        d_step[here, :] = d_step[here, :] + by_head_low(x * total, heads)
    product = held.astype(F32) * came.astype(F32)
    product = jnp.sum(product.reshape(LANES // 8, 8, width), axis=0)
    survive = jnp.exp(end) * (last == before).astype(F32)
    boundary = boundary + survive * jnp.sum(by_head(jnp.concatenate([product, product * 0.0], axis=0), heads), axis=0, keepdims=True)
    ends[0:1, :] = ends[0:1, :] + boundary

    def store(here, lanes, value):
        d_rows[0, 0, here, lanes] = value

    sums = conv_backward(
        rows.at[0, 0],
        ids,
        id_rows,
        params[0],
        lambda c, lanes: d_acted[c * CHUNK : (c + 1) * CHUNK, lanes],
        d_pre,
        store,
        length,
    )
    taps_grad[0] = jnp.concatenate(sums + [jnp.zeros((3, width), F32)], axis=0)

    @pl.when(g == pl.num_programs(0) - 1)
    def _():
        rate = jnp.exp(small[1:2, :])
        ones = triangle(False).astype(F32)
        carry = ends[0:1, :]
        decay_sum = jnp.zeros((1, LANES), F32)
        bias_sum = jnp.zeros((1, LANES), F32)
        for c in range(chunks - 1, -1, -1):
            here = slice(c * CHUNK, (c + 1) * CHUNK)
            grads = exact_dot(ones, d_log[here, :]) + carry
            carry = grads[0:1]
            decay_sum = decay_sum + jnp.sum(grads * log_decay[0, here, :], axis=0, keepdims=True)
            value = (d_step[here, :] - grads * rate) * sigmoid(raw[0, here, :] + small[0:1, :])
            bias_sum = bias_sum + jnp.sum(value, axis=0, keepdims=True)
            d_raw[0, here, :] = value.astype(BF16)
        small_grad[...] = jnp.concatenate([bias_sum, decay_sum, jnp.zeros((6, LANES), F32)], axis=0)

        def store_state(here, lanes, value):
            d_state[0, here, lanes] = value

        sums = conv_backward(
            state_rows.at[0],
            ids,
            id_rows,
            state_taps[...],
            lambda c, lanes: d_bc[c * CHUNK : (c + 1) * CHUNK, lanes],
            d_pre_bc,
            store_state,
            length,
        )
        state_taps_grad[...] = jnp.concatenate(sums + [jnp.zeros((3, 2 * LANES), F32)], axis=0)


def close_call(
    s, rows, acted, d_summed, d_scaled, bc, ids, id_rows, steps, raw, log_decay, cum, d_cum, leaving, entered, params,
    small, state_rows, state_taps, d_b, d_c, per_block,
):
    blocks, n, length, width = acted.shape
    four = lambda a, b: pl.BlockSpec((1, 1, a, b), lambda g: (g, s, 0, 0))
    own = lambda a, b: pl.BlockSpec((1, 1, a, b), lambda g: (g, 0, 0, 0))
    per_seq = lambda a: pl.BlockSpec((1,) + a.shape[1:], lambda g: (s, 0, 0))
    kept = lambda *shape: pl.BlockSpec(shape, lambda g: (0,) * len(shape))
    whole = lambda a: kept(*a.shape)
    wide = own(length, width)
    return pl.pallas_call(
        functools.partial(close_kernel, per_block),
        grid=(blocks,),
        in_specs=[
            four(length + PAD, width), four(length, width), wide, wide, per_seq(bc), per_seq(ids), per_seq(id_rows),
            per_seq(steps), per_seq(raw), per_seq(log_decay), per_seq(cum), kept(1, length, LANES), own(LANES, width),
            four(LANES, width),
            pl.BlockSpec((1,) + params.shape[1:], lambda g: (g, 0, 0)), whole(small), per_seq(state_rows),
            whole(state_taps), whole(d_b), whole(d_c),
        ],
        out_specs=[
            own(length + PAD, width), kept(1, length, LANES), kept(1, length + PAD, 2 * LANES),
            pl.BlockSpec((1, 8, width), lambda g: (g, 0, 0)), kept(8, 2 * LANES), kept(8, LANES),
        ],
        out_shape=[
            jax.ShapeDtypeStruct((blocks, 1, length + PAD, width), BF16),
            jax.ShapeDtypeStruct((1, length, LANES), BF16),
            jax.ShapeDtypeStruct((1, length + PAD, 2 * LANES), BF16),
            jax.ShapeDtypeStruct((blocks, 8, width), F32),
            jax.ShapeDtypeStruct((8, 2 * LANES), F32),
            jax.ShapeDtypeStruct((8, LANES), F32),
        ],
        scratch_shapes=[
            pltpu.VMEM((length + 2 * PAD, width), BF16),
            pltpu.VMEM((length, width), F32),
            pltpu.VMEM((length, LANES), F32),
            pltpu.VMEM((length, LANES), F32),
            pltpu.VMEM((8, LANES), F32),
            pltpu.VMEM((length, 2 * LANES), F32),
            pltpu.VMEM((length + 2 * PAD, 2 * LANES), BF16),
        ],
        compiler_params=pltpu.CompilerParams(vmem_limit_bytes=VMEM),
        name="close",
    )(
        rows, acted, d_summed, d_scaled, bc, ids, id_rows, steps, raw, log_decay, cum, d_cum, leaving, entered, params,
        small, state_rows, state_taps, d_b, d_c,
    )


def input_kernel(blocks, d_raw, d_state, tokens, cotangent, gain, state_w, step_w, d_gate, d_rows, *refs):
    row_weights, refs = refs[:blocks], refs[blocks:]
    gate_weights, refs = refs[:blocks], refs[blocks:]
    input_grad, edge, halo, gain_grad, main_s, halo_s, weights_s, gate_s, rows_s, sems = refs
    length = d_gate.shape[2]
    copies = []
    for r in range(blocks):
        moves = [(row_weights[r], weights_s.at[2 * r]), (d_rows.at[r, 0], rows_s.at[r])]
        moves += [(gate_weights[r], weights_s.at[2 * r + 1]), (d_gate.at[r, 0], gate_s.at[r])]
        copies.append([pltpu.make_async_copy(a, b, sems.at[4 * r + i]) for i, (a, b) in enumerate(moves)])
        for copy in copies[r]:
            copy.start()
    total = dot_nt(d_state[0], state_w[...])
    halo_s[...] = total[:PAD]
    main_s[...] = total[PAD:] + dot(d_raw[0], step_w[...])
    for r in range(blocks):
        copies[r][0].wait()
        copies[r][1].wait()
        halo_s[...] = halo_s[...] + dot_nt(rows_s[r, :PAD, :], weights_s[2 * r])
        part = dot_nt(rows_s[r, PAD:, :], weights_s[2 * r])
        copies[r][2].wait()
        copies[r][3].wait()
        main_s[...] = main_s[...] + (part + dot_nt(gate_s[r], weights_s[2 * r + 1]))

    def norm_back(value, token):
        scale = lax.rsqrt(jnp.mean(token * token, axis=1, keepdims=True) + EPS)
        unit = value * gain[...]
        inner = jnp.mean(unit * token, axis=1, keepdims=True)
        return scale * unit - token * (scale * scale * scale * inner), fold8(value * token * scale)

    grad, sums = norm_back(halo_s[...], tokens[0, :PAD, :].astype(F32))
    halo[0] = grad.astype(BF16)

    def step(i, carry):
        here = rows_at(i * 16, 16)
        grad, more = norm_back(main_s[here, :], tokens[0, rows_at(PAD + i * 16, 16), :].astype(F32))
        value = grad + cotangent[0, here, :].astype(F32)
        edge[0] = value
        input_grad[0, here, :] = value.astype(BF16)
        return carry + more

    gain_grad[...] = lax.fori_loop(0, length // 16, step, sums, unroll=4)


def input_call(s, d_gate, d_rows, d_raw, d_state, tokens, cotangent, gain, state_w, step_w, row_weights, gate_weights):
    blocks, _, length, width = d_gate.shape
    padded, model = tokens.shape[1:]
    whole = lambda a: pl.BlockSpec(a.shape, lambda t: (0,) * a.ndim, pipeline_mode=pl.Buffered(1))
    one = lambda a, b: pl.BlockSpec((1, a, b), lambda t: (s, 0, 0), pipeline_mode=pl.Buffered(1))
    kept = lambda *shape: pl.BlockSpec(shape, lambda t: (0,) * len(shape), pipeline_mode=pl.Buffered(1))
    return pl.pallas_call(
        functools.partial(input_kernel, blocks),
        grid=(1,),
        in_specs=[
            whole(d_raw), whole(d_state), one(padded, model), one(length, model), whole(gain), whole(state_w), whole(step_w),
        ] + [pl.BlockSpec(memory_space=pl.ANY)] * (2 + 2 * blocks),
        out_specs=[kept(1, length, model), kept(1, PAD, model), kept(1, PAD, model), kept(8, model)],
        out_shape=[
            jax.ShapeDtypeStruct((1, length, model), BF16),
            jax.ShapeDtypeStruct((1, PAD, model), F32),
            jax.ShapeDtypeStruct((1, PAD, model), BF16),
            jax.ShapeDtypeStruct((8, model), F32),
        ],
        scratch_shapes=[
            pltpu.VMEM((length, model), F32),
            pltpu.VMEM((PAD, model), F32),
            pltpu.VMEM((2 * blocks, model, width), BF16),
            pltpu.VMEM((blocks, length, width), BF16),
            pltpu.VMEM((blocks, padded, width), BF16),
            pltpu.SemaphoreType.DMA((4 * blocks,)),
        ],
        compiler_params=pltpu.CompilerParams(vmem_limit_bytes=VMEM),
        name="input_gradient",
    )(d_raw, d_state, tokens, cotangent, gain, state_w, step_w, d_gate, d_rows, *row_weights, *gate_weights)


def assemble_kernel(count, places, *refs):
    parts, refs = refs[:count], refs[count:]
    edges, refs = (refs[:count], refs[count:]) if len(refs) > 2 * count else ((), refs)
    whole, buffers, (in_sem, out_sem) = refs[0], refs[1:-2], refs[-2:]
    length = parts[0].shape[1]
    reads = [pltpu.make_async_copy(p.at[0], b, in_sem.at[i]) for i, (p, b) in enumerate(zip(parts, buffers))]
    writes = [pltpu.make_async_copy(b, whole.at[places[i]], out_sem.at[i]) for i, b in enumerate(buffers)]
    for read in reads:
        read.start()
    for i, (read, write) in enumerate(zip(reads, writes)):
        read.wait()
        if edges:
            buffers[i][length - PAD :, :] = edges[i][0]
        write.start()
    for write in writes:
        write.wait()


def assemble(parts, edges, places):
    count = len(parts)
    _, length, model = parts[0].shape
    return pl.pallas_call(
        functools.partial(assemble_kernel, count),
        grid_spec=pltpu.PrefetchScalarGridSpec(
            num_scalar_prefetch=1,
            grid=(1,),
            in_specs=[pl.BlockSpec(memory_space=pl.ANY) for _ in parts]
            + [pl.BlockSpec((1, PAD, model), lambda t, i: (0, 0, 0)) for _ in edges],
            out_specs=pl.BlockSpec(memory_space=pl.ANY),
            scratch_shapes=[pltpu.VMEM((length, model), BF16) for _ in parts]
            + [pltpu.SemaphoreType.DMA((count,)), pltpu.SemaphoreType.DMA((count,))],
        ),
        out_shape=jax.ShapeDtypeStruct((count, length, model), BF16),
        compiler_params=pltpu.CompilerParams(vmem_limit_bytes=VMEM),
        name="assemble",
    )(jnp.stack(places).astype(jnp.int32), *parts, *edges)


def weight_grad_kernel(n, halo, rows, *refs):
    grads, (kept, sent) = refs[:n], refs[n:]
    odd = pl.program_id(0) % 2 == 1
    start = PAD if halo else 0
    length = grads[0].shape[2] - start
    skip = rows.shape[1] - length
    total = None
    if halo:
        before = jnp.concatenate([rows[s, :PAD, :] for s in range(n)], axis=0)
        total = dot_tn(before, jnp.concatenate([grad[0, 0, :PAD, :] for grad in grads], axis=0))
    for s in range(n):
        part = dot_tn(rows[s, skip:, :], grads[s][0, 0, start:, :])
        total = part if total is None else total + part
    total = total.astype(BF16)

    @pl.when(odd)
    def _():
        sent[0] = total

    @pl.when(jnp.logical_not(odd))
    def _():
        kept[0] = total


def weight_grad(values, grads):
    n, padded, model = values.shape
    blocks, _, tokens, width = grads[0].shape
    return pl.pallas_call(
        functools.partial(weight_grad_kernel, n, tokens % CHUNK != 0),
        grid=(blocks,),
        in_specs=[pl.BlockSpec(values.shape, lambda g: (0, 0, 0), pipeline_mode=pl.Buffered(1))]
        + [pl.BlockSpec((1, 1, tokens, width), lambda g: (g, 0, 0, 0)) for _ in grads],
        out_specs=[pl.BlockSpec((1, model, width), lambda g: (g // 2, 0, 0))] * 2,
        out_shape=[jax.ShapeDtypeStruct((blocks // 2, model, width), BF16)] * 2,
        compiler_params=pltpu.CompilerParams(vmem_limit_bytes=VMEM),
        name="weight_gradient",
    )(values, *grads)


def state_grad_kernel(n, values, *refs):
    states, (out,) = refs[:n], refs[n:]
    total = dot_tn(values[0], states[0][0])
    for s in range(1, n):
        total = total + dot_tn(values[s], states[s][0])
    out[...] = total.astype(BF16)


def state_grad(values, states):
    return pl.pallas_call(
        functools.partial(state_grad_kernel, len(states)),
        out_shape=jax.ShapeDtypeStruct((values.shape[2], states[0].shape[2]), BF16),
        compiler_params=pltpu.CompilerParams(vmem_limit_bytes=VMEM),
        name="state_weight_gradient",
    )(values, *states)


def pack_kernel(n, per_block, values, *refs):
    groups, outs = [refs[i * n : (i + 1) * n] for i in range(7)], refs[7 * n :]
    steps, taps, state_taps, rest, gains, skips, norms = groups
    add = lambda refs, *at: functools.reduce(lambda a, b: a + b, [ref[at] for ref in refs])
    column_sum = lambda value: jnp.sum(value, axis=0, keepdims=True)
    step = dot_tn(steps[0][0], values[0, PAD:, :])
    for s in range(1, n):
        step = step + dot_tn(steps[s][0], values[s, PAD:, :])
    model = step.shape[1]
    width = outs[0].shape[1]
    norm = column_sum(add(norms, Ellipsis))
    rest = add(rest, Ellipsis)
    state = add(state_taps, Ellipsis)
    for r, out in enumerate(outs):
        out[...] = jnp.zeros_like(out)
        out[0:5, :] = add(taps, r)[0:5]
        out[5:6, :] = column_sum(add(gains, r))
        out[6:7, :] = column_sum(add(skips, r))
        mine = pltpu.roll(rest, (LANES - r * per_block) % LANES, 1) if r else rest
        out[7:8, :LANES] = mine[0:1]
        out[7:8, LANES : 2 * LANES] = mine[1:2]
        row = 8
        for q in range(0, model, width):
            out[row : row + per_block, :] = step[r * per_block : (r + 1) * per_block, q : q + width]
            row += per_block
        for q in range(0, model, width):
            out[row : row + 1, :] = norm[:, q : q + width]
            row += 1
        out[row : row + 5, : 2 * LANES] = state[0:5]


def pack_sums(values, width, per_block, blocks, *groups):
    n, _, model = values.shape
    rows = 8 + per_block * (model // width) + model // width + 5
    return pl.pallas_call(
        functools.partial(pack_kernel, n, per_block),
        out_shape=[jax.ShapeDtypeStruct((-(-rows // 8) * 8, width), F32)] * blocks,
        compiler_params=pltpu.CompilerParams(vmem_limit_bytes=VMEM),
        name="pack",
    )(values, *[v for group in groups for v in group])


def unpack_kernel(packed, norm, steps, taps, state_taps, params, gains):
    heads, width = params.shape[1], packed.shape[1]
    model = steps.shape[1]
    taps[...] = packed[0:5, :]
    for k in range(width // LANES):
        gains[k : k + 1, :] = packed[5:6, k * LANES : (k + 1) * LANES]
    params[0:1, :] = packed[7:8, :heads]
    params[1:2, :] = packed[7:8, LANES : LANES + heads]
    skips = packed[6:7, :]
    lane = lax.broadcasted_iota(jnp.int32, (heads, width), 1)
    head = lax.broadcasted_iota(jnp.int32, (heads, width), 0)
    mine = lax.shift_right_logical(lane, 6) == head
    column = jnp.sum(jnp.where(mine, skips, 0.0), axis=1, keepdims=True)
    params[2:3, :] = jnp.transpose(jnp.broadcast_to(column, (heads, LANES)))[0:1, :]
    row = 8
    for q in range(0, model, width):
        steps[:, q : q + width] = packed[row : row + heads, :]
        row += heads
    for k in range(model // LANES):
        at = k * LANES
        norm[k : k + 1, :] = packed[row + at // width : row + at // width + 1, at % width : at % width + LANES]
    row += model // width
    state_taps[...] = packed[row : row + 5, : 2 * LANES]


def unpack_sums(packed, heads, model):
    width = packed.shape[1]
    shapes = [(model // LANES, LANES), (heads, model), (5, width), (5, 2 * LANES), (3, heads), (width // LANES, LANES)]
    return pl.pallas_call(
        unpack_kernel, out_shape=[jax.ShapeDtypeStruct(shape, F32) for shape in shapes], name="unpack"
    )(packed)


def swapped(value, axis, step):
    return lax.ppermute(value, axis, [(i, i ^ step) for i in range(lax.axis_size(axis))])


def reached(value):
    return {r: swapped(value, "head", r) if r else value for r in [0, 1] + list(range(2, lax.axis_size("head"), 2))}


def forwarded(parts):
    rest = {r + 1: swapped(parts[r], "head", 1) for r in parts if r and r % 2 == 0}
    return [{**parts, **rest}[r] for r in range(lax.axis_size("head"))]


def gathered(value):
    return forwarded(reached(value))


def crossed(value):
    return {r: swapped(value, "head", r) if r else value for r in range(0, lax.axis_size("head"), 2)}


def completed(parts):
    rest = {r + 1: swapped(part, "head", 1) for r, part in parts.items()}
    return [{**parts, **rest}[r] for r in range(lax.axis_size("head"))]


def bits_of(axis):
    return [1 << i for i in range((lax.axis_size(axis) - 1).bit_length())]


def added(a, b, dtype=None):
    return (a.astype(F32) + b.astype(F32)).astype(dtype or a.dtype)


def tree_sum(values):
    while len(values) > 1:
        values = [a + b for a, b in zip(values[::2], values[1::2])]
    return values[0]


def head_sum(value, bits):
    for bit in reversed(bits):
        half = value.shape[0] // 2
        arrived = yield value[half:], "head", bit
        value = added(value[:half], arrived)
    return value[0]


def ranges_sum(value):
    ranges = lax.axis_size("seq")
    me = lax.axis_index("seq")
    lead, rest = value.shape[0], value.shape[2:]
    piece = (value.shape[1] // ranges,) + rest
    for bit in bits_of("seq"):
        mine = (me // bit) % 2
        halves = value.reshape((lead, ranges // bit // 2, 2) + piece)
        arrived = yield lax.dynamic_index_in_dim(halves, 1 - mine, 2, keepdims=False), "seq", bit
        kept = lax.dynamic_index_in_dim(halves, mine, 2, keepdims=False)
        value = added(kept, arrived, F32 if 2 * bit == ranges else value.dtype)
    return value.reshape((lead,) + piece)


def weight_sum(kept, sent, ranges_first):
    arrived = yield sent, "head", 1
    value = added(kept, arrived)
    bits = bits_of("head")[1:]
    if ranges_first:
        value = yield from ranges_sum(value)
        return (yield from head_sum(value, bits))
    value = yield from head_sum(value, bits)
    return (yield from ranges_sum(value[None]))[0]


def sum_of_state(value):
    for bit in bits_of("head"):
        arrived = yield value, "head", bit
        value = added(value, arrived)
    return (yield from ranges_sum(value[None]))[0]


class Chain(Held):
    def __init__(self, steps):
        super().__init__()
        self.steps, self.done = steps, False
        self.advance()

    def advance(self):
        if self.done:
            return
        try:
            self.value = swapped(*self.steps.send(self.value))
        except StopIteration as end:
            self.value, self.done = end.value, True

    def finish(self):
        while not self.done:
            self.advance()
        return self.value


def assembled(parts, edges=None):
    n = len(parts)
    me = lax.axis_index("head")
    pieces, places, last_rows = [], [], []
    for s in range(n):
        for r, part in enumerate(parts[s]):
            pieces.append(part)
            places.append((me ^ r) * n + s)
            if edges is not None:
                last_rows.append(edges[r][s : s + 1])
    return assemble(pieces, last_rows, places)


def padded_lanes(value, size):
    return jnp.pad(value, ((0, 0), (0, size - value.shape[1])))


def shards(
    tokens,
    doc_ids,
    norm_gain,
    head_input_weight,
    state_input_weight,
    timestep_input_weight,
    conv_x,
    conv_state,
    head_params,
    gated_gain,
    output_weight,
    cotangent,
):
    seqs, length, model = tokens.shape
    blocks = lax.axis_size("head")
    ranges = lax.axis_size("seq")
    n = seqs // blocks
    width = gated_gain.shape[0]
    heads = head_params.shape[1]
    me = lax.axis_index("head")
    tokens = lax.dynamic_slice_in_dim(tokens, me * n, n, 0)
    cotangent = lax.dynamic_slice_in_dim(cotangent, me * n, n, 0)
    before = lax.ppermute(tokens[:, length - PAD :], "seq", [(i, i + 1) for i in range(ranges - 1)])
    padded = jnp.concatenate([before, tokens], axis=1)

    start = lax.axis_index("seq") * length
    lead = jnp.concatenate(
        [jnp.full((seqs, PAD), -1, jnp.int32), doc_ids, jnp.full((seqs, PAD), -2, jnp.int32)], axis=1
    )
    ids = lax.dynamic_slice(lead, (me * n, start), (n, length + 2 * PAD)).astype(F32)
    id_rows = jnp.broadcast_to(ids[:, None], (n, 8, length + 2 * PAD))
    ids = jnp.broadcast_to(ids[:, :, None], (n, length + 2 * PAD, LANES))

    pack = jnp.concatenate(
        [
            conv_x,
            gated_gain[None],
            padded_lanes(head_params, width),
            *[jnp.transpose(timestep_input_weight[q : q + width]).astype(F32) for q in range(0, model, width)],
        ],
        axis=0,
    )
    half = blocks // 2
    packs, side = lax.optimization_barrier((reached(pack), head_input_weight.reshape(model, 2 * width)))
    packs = forwarded(packs)
    row_parts = reached(side[:, width:])
    small, step_weights, params = arrange(packs, heads, model)
    state_taps = jnp.pad(conv_state, ((0, 3), (0, 0)))

    tok_float = padded.astype(F32)
    scale = lax.rsqrt(jnp.mean(tok_float * tok_float, axis=-1, keepdims=True) + EPS)
    normed = (tok_float * scale * norm_gain).astype(BF16)
    rows, raw, steps, log_decay, cum, state_rows, bc = project_first(
        normed, state_input_weight, step_weights, small, ids, id_rows, state_taps, [row_parts[0], row_parts[1]], blocks,
        heads * blocks,
    )
    row_parts, rows, gate_own, out_own = lax.optimization_barrier(
        (row_parts, rows, side[:, :width], output_weight)
    )
    row_weights = forwarded(row_parts)
    cuts = ranges // (blocks * n)
    held = state_call(rows, bc, ids, id_rows, steps, cum, params, (), 0, 2, heads, cuts)
    held, rows = lax.optimization_barrier((held, rows))
    acted, message = held
    for r in range(2, blocks, 2):
        rows = project_more(normed, rows, row_weights[r : r + 2], r)
        acted, message = state_call(rows, bc, ids, id_rows, steps, cum, params, (acted, message), r, 2, heads, cuts)
    mixed, states = inside_call(acted, bc, ids, id_rows, steps, cum, heads)
    mixed, arrived = Held(mixed), Held(send_message(message))
    meet(arrived, mixed)
    entered = Held(send_back(relay(arrived.value, False), blocks, n))
    gate_weights = gathered(gate_own)
    out_weights = gathered(out_own)
    gate = Held(project_gate(normed, gate_weights))
    meet(entered, gate)

    cuts = ranges // blocks
    every = range(n)
    outs, normed_outs, d_gates, d_sums, messages, gain_parts, skip_parts = [[] for _ in range(7)]
    for s in every:
        parts = middle_call(
            s, mixed.value, gate.value, acted, cum, entered.value, bc, ids, tokens, cotangent, params, out_weights, heads,
            cuts,
        )
        for held, part in zip((outs, normed_outs, d_gates, d_sums, messages), parts):
            held.append(Held(part))
        gain_parts.append(parts[5])
        skip_parts.append(parts[6])
        meet(entered, messages[s])
    for out in outs:
        out.value = crossed(out.value)
    d_scaled, insides, leaving, d_rows, d_raws, d_states, closes = [[] for _ in range(7)]

    def inside_back():
        s = len(d_scaled)
        part, *rest = inside_back_call(
            s, acted, d_sums[s].value, mixed.value, bc, ids, id_rows, steps, cum, states, entered.value, heads
        )
        d_scaled.append(Held(part))
        insides.append(rest)

    def close():
        s = len(d_rows)
        d_b, d_c, d_cum = insides[s]
        parts = close_call(
            s, rows, acted, d_sums[s].value, d_scaled[s].value, bc, ids, id_rows, steps, raw, log_decay, cum, d_cum,
            leaving[s].value, entered.value, params, small, state_rows, state_taps, d_b, d_c, heads,
        )
        for held, part in zip((d_rows, d_raws, d_states), parts):
            held.append(Held(part))
        closes.append(parts[3:])

    for s in every:
        arrived = Held(send_message(messages[s].value))
        if s:
            inside_back()
            meet(arrived, d_scaled[s], out_sum, gate_sum)
        else:
            meet(arrived, *messages[1:])
        carried = Held(relay(arrived.value, True))
        if s:
            out_sum.advance()
            meet(carried, leaving[s - 1])
        else:
            meet(carried, d_sums[0], *normed_outs, *d_gates)
        leaving.append(Held(send_back(carried.value, blocks, 1)))
        if s:
            close()
            meet(leaving[s], d_rows[s - 1], out_sum)
            out_sum.advance()
            gate_sum.advance()
        else:
            inside_back()
            out_grads = Held(weight_grad(cotangent, values(normed_outs)))
            gate_grads = Held(weight_grad(normed, values(d_gates)))
            meet(leaving[0], d_scaled[0], out_grads, gate_grads, *outs, *messages[1:], *d_sums[1:])
            out_sum = Chain(weight_sum(*out_grads.value, False))
            gate_sum = Chain(weight_sum(*gate_grads.value, False))
    close()
    meet(d_rows[-1], out_sum)
    out_sum.advance()

    state_part = Held(state_grad(normed, values(d_states)))
    meet(state_part, *d_rows)
    state_sum = Chain(sum_of_state(state_part.value))
    rows_grads = Held(weight_grad(normed, values(d_rows)))
    gain = Held(norm_gain[None])
    meet(rows_grads, out_sum, gate_sum, gain, state_sum)
    for chain in (out_sum, gate_sum, state_sum):
        chain.advance()
    rows_sum = Chain(weight_sum(*rows_grads.value, True))
    meet(rows_sum, gain)
    rows_sum.advance()
    inputs, edges, halos, norm_parts = [], [], [], []
    for s in every:
        *parts, norm_part = input_call(
            s, d_gates[s].value, d_rows[s].value, d_raws[s].value, d_states[s].value, padded, cotangent, gain.value,
            state_input_weight, step_weights, row_weights, gate_weights,
        )
        for held, part in zip((inputs, edges, halos), parts):
            held.append(Held(part))
        norm_parts.append(norm_part)
        if s < n - 1:
            meet(gain, inputs[s], gate_sum, out_sum, state_sum)
            gate_sum.advance()
            out_sum.advance()
            state_sum.advance()
            inputs[s].value = crossed(inputs[s].value)
    meet(inputs[-1], rows_sum, state_sum, gate_sum, *halos, *edges, *outs)
    for chain in (rows_sum, state_sum, gate_sum):
        chain.advance()
    inputs[-1].value = crossed(inputs[-1].value)
    smalls = pack_sums(
        normed, width, heads, blocks, values(d_raws), *[[c[i] for c in closes] for i in range(3)], gain_parts, skip_parts,
        norm_parts,
    )
    halo = Held(lax.ppermute(jnp.concatenate(values(halos), axis=0), "seq", [(i + 1, i) for i in range(ranges - 1)]))
    own = Held(list(smalls))
    meet(own, *inputs[:-1])
    own.value = [swapped(part, "head", r) if r else part for r, part in enumerate(own.value)]
    output = Held(assembled([completed(part) for part in values(outs)]))
    meet(own, output)
    own.value = tree_sum(own.value)
    steps = bits_of("seq")
    for i, bit in enumerate(steps):
        came = Held(swapped(own.value, "seq", bit))
        also = [gate_sum, halo] if i == 0 else inputs if i == 1 else [whole_input] if i == 2 else []
        meet(came, own, rows_sum, state_sum, *also)
        for chain in (rows_sum, state_sum):
            chain.advance()
        own.value = own.value + came.value
        if i == 0:
            gate_sum.advance()
            edge = crossed(added(jnp.concatenate(values(edges), axis=0), halo.value, BF16))
        if i == 1:
            whole_input = Held(assembled([completed(part) for part in values(inputs)], completed(edge)))
    out_grad = jnp.transpose(out_sum.finish())
    both = own.value
    norm_grad, steps_grad, taps_grad, state_taps_grad, params_grad, gains_grad = unpack_sums(both, heads, model)
    return (
        output.value,
        whole_input.value,
        norm_grad.reshape(model),
        jnp.stack([gate_sum.finish(), rows_sum.finish()], axis=1),
        state_sum.finish(),
        jnp.transpose(steps_grad),
        taps_grad,
        state_taps_grad,
        params_grad,
        gains_grad.reshape(width),
        out_grad,
    )


def solution(mesh):
    return jax.shard_map(
        shards,
        mesh=mesh,
        in_specs=(
            P(None, "seq", None),
            P(),
            P(),
            P(None, None, "head"),
            P(),
            P(None, "head"),
            P(None, "head"),
            P(),
            P(None, "head"),
            P("head"),
            P("head", None),
            P(None, "seq", None),
        ),
        out_specs=(
            P(None, "seq", None),
            P(None, "seq", None),
            P(),
            P("seq", None, "head"),
            P("seq", None),
            P(None, "head"),
            P(None, "head"),
            P(),
            P(None, "head"),
            P("head"),
            P("head", "seq"),
        ),
        check_vma=False,
    )
```
